32 devices in a mesh: dp: 2 (over x), lat: 4 (over z), lon: 4 (over y, core).
Axes of the slice: x: 2, y: 2, z: 4, core: 2. Of those that a mesh axis runs over, the one named last changes fastest.
Arguments:
- hidden_in: bfloat16 [2, 120, 240, 384], P('dp', 'lat', 'lon'), may hold values from -6 to 6
- grad_out: bfloat16 [2, 120, 240, 384], P('dp', 'lat', 'lon'), may hold values from -6 to 6
- norm_gain: float32 [384], replicated, may hold values from 0.5 to 1.5
- w_qkv: bfloat16 [384, 1152], replicated, may hold values from -0.3125 to 0.3125
- w_proj: bfloat16 [384, 384], replicated, may hold values from -0.3125 to 0.3125
Outputs:
- grad_in: bfloat16 [2, 120, 240, 384], P('dp', 'lat', 'lon')
- grad_qkv: float32 [384, 1152], P('dp', ('lat', 'lon'))
- grad_proj: float32 [384, 384], P('dp', ('lat', 'lon'))
The draws below stay inside these ranges and needn't reach their ends.
All inputs are finite; a program needn't handle non-finite values.
Results may differ from the reference program's by a relative error of at most 0.0083.
Values may be sent and summed in bfloat16 or wider, within the bound.
No kernel may reach another device: no remote copies, remote signals or barrier semaphores. Data moves between devices by JAX's collectives and lax.ppermute only.
A program may use at most 64 MiB of HBM per device.

```python
import jax
import jax.numpy as jnp
from jax import lax

D = 384
HEADS = 6
WIN = 30
SHIFT = 15
BATCH = 2
NLAT = 120
NLON = 240
CELLS = 57600


def steps_of(key, shape, cuts, low, top_value):
    loudness = 1.0
    for axis_at, shards_of in cuts:
        heights = jax.random.uniform(jax.random.fold_in(jax.random.fold_in(key, 6), axis_at), (shards_of,), jnp.float32, low / len(cuts), top_value / len(cuts))
        loudness = loudness * jnp.repeat(jnp.exp(heights), shape[axis_at] // shards_of).reshape((-1,) + (1,) * (len(shape) - 1 - axis_at))
    return loudness


def noise(own_key, shape, spread, most, shards=(), kind=jnp.bfloat16):
    array = jax.random.normal(own_key, shape, jnp.float32) * spread
    if len(shards) > 0:
        array = steps_of(own_key, shape, shards, -0.22, 0.18) * array
    return jnp.clip(array, min=-most, max=most).astype(kind)


def setup_inputs(seed: int = 0) -> dict:
    splits = jax.random.split(jax.random.key(seed), 6)
    hidden_in = noise(splits[0], (BATCH, NLAT, NLON, D), 1.0, 6.0, ((0, 2), (1, 4), (2, 4)))
    grad_out = noise(splits[1], (BATCH, NLAT, NLON, D), 1.0, 6.0, ((0, 2), (1, 4), (2, 4)))
    norm_gain = jnp.clip(1.0 + 0.1 * jax.random.normal(splits[2], (D,), jnp.float32), 0.5, 1.5)
    w_qkv = noise(splits[3], (D, 3 * D), D ** -0.5, 0.3125)
    w_proj = noise(splits[4], (D, D), D ** -0.5, 0.3125)
    return {"hidden_in": hidden_in, "grad_out": grad_out, "norm_gain": norm_gain, "w_qkv": w_qkv, "w_proj": w_proj}


EPSILON = 1e-05

def attend_head(query_rows, key_rows, value_rows, grad_rows, key_valid, scaling):
    scores = jnp.dot(query_rows, key_rows.T, preferred_element_type=jnp.float32) * scaling
    weights_raw = jnp.exp(scores) * key_valid[None, :]
    attention = weights_raw / lax.optimization_barrier(jnp.sum(weights_raw, axis=-1, keepdims=True))
    attention_low = attention.astype(jnp.bfloat16)
    outputs = jnp.dot(attention_low, value_rows, preferred_element_type=jnp.float32).astype(jnp.bfloat16)
    dprobs = jnp.dot(grad_rows, value_rows.T, preferred_element_type=jnp.float32)
    row_total = lax.optimization_barrier(jnp.sum(attention * dprobs, axis=-1, keepdims=True))
    dscores = (attention * (dprobs - row_total) * scaling).astype(jnp.bfloat16)
    dquery = jnp.dot(dscores, key_rows, preferred_element_type=jnp.float32).astype(jnp.bfloat16)
    dkey_rows = jnp.dot(dscores.T, query_rows, preferred_element_type=jnp.float32).astype(jnp.bfloat16)
    dvalue = jnp.dot(attention_low.T, grad_rows, preferred_element_type=jnp.float32).astype(jnp.bfloat16)
    return (outputs, dquery, dkey_rows, dvalue)

def window_grads(window_cells, cotangent, key_valid, norm_gain, w_qkv, w_proj):
    model_width = window_cells.shape[1]
    head_size = model_width // HEADS
    scaling = head_size ** (-0.5)
    values_f = window_cells.astype(jnp.float32)
    average = lax.optimization_barrier(jnp.mean(values_f, axis=1, keepdims=True))
    centred = values_f - average
    inverse_std = lax.rsqrt(lax.optimization_barrier(jnp.mean(centred * centred, axis=1, keepdims=True)) + EPSILON)
    normed = centred * inverse_std
    normal_low = (normed * norm_gain).astype(jnp.bfloat16)
    qkv = jnp.dot(normal_low, w_qkv, preferred_element_type=jnp.float32).astype(jnp.bfloat16)
    back_rows = jnp.dot(cotangent, w_proj.T, preferred_element_type=jnp.float32).astype(jnp.bfloat16)

    def split_heads(matrix):
        return matrix.reshape(matrix.shape[0], HEADS, head_size).transpose(1, 0, 2)

    def merge_heads(stacked):
        return stacked.transpose(1, 0, 2).reshape(stacked.shape[1], model_width)

    def one_head(inputs):
        return attend_head(inputs[0], inputs[1], inputs[2], inputs[3], key_valid, scaling)
    heads_in = (split_heads(qkv[:, :model_width]), split_heads(qkv[:, model_width:2 * model_width]), split_heads(qkv[:, 2 * model_width:]), split_heads(back_rows))
    outputs, dquery, dkey_rows, dvalue = lax.map(one_head, heads_in)
    attended = merge_heads(outputs)
    dqkv = jnp.concatenate([merge_heads(dquery), merge_heads(dkey_rows), merge_heads(dvalue)], axis=1)
    proj_part = jnp.dot(attended.T, cotangent, preferred_element_type=jnp.float32)
    qkv_part = jnp.dot(normal_low.T, dqkv, preferred_element_type=jnp.float32)
    dnormed = jnp.dot(dqkv, w_qkv.T, preferred_element_type=jnp.float32) * norm_gain
    dcells = inverse_std * (dnormed - lax.optimization_barrier(jnp.mean(dnormed, axis=1, keepdims=True)) - normed * lax.optimization_barrier(jnp.mean(dnormed * normed, axis=1, keepdims=True)))
    return (dcells.astype(jnp.bfloat16), qkv_part, proj_part)

def to_windows(grid_field):
    shape = grid_field.shape
    split = grid_field.reshape(shape[0], shape[1] // WIN, WIN, shape[2] // WIN, WIN, shape[3])
    return split.transpose(0, 1, 3, 2, 4, 5).reshape(-1, WIN * WIN, shape[3])

def from_windows(windows, samples, lat_rows, lon_cols):
    split = windows.reshape(samples, lat_rows // WIN, lon_cols // WIN, WIN, WIN, windows.shape[-1])
    return split.transpose(0, 1, 3, 2, 4, 5).reshape(samples, lat_rows, lon_cols, windows.shape[-1])

def shift_ahead(grid_field):
    rolled = jnp.roll(grid_field, -SHIFT, axis=2)
    padding = jnp.zeros_like(rolled[:, :SHIFT])
    return jnp.concatenate([rolled[:, SHIFT:], padding], axis=1)

def shift_behind(grid_field):
    rolled = jnp.roll(grid_field, SHIFT, axis=2)
    padding = jnp.zeros_like(rolled[:, :SHIFT])
    return jnp.concatenate([padding, rolled[:, :-SHIFT]], axis=1)

def reference(hidden_in, grad_out, norm_gain, w_qkv, w_proj):
    shifted = shift_ahead(hidden_in)
    cotangent = shift_ahead(grad_out)
    row_index = jnp.arange(NLAT, dtype=jnp.int32)
    valid_rows = (row_index < NLAT - SHIFT).astype(jnp.float32)
    valid_field = jnp.broadcast_to(valid_rows[None, :, None, None], (BATCH, NLAT, NLON, 1))
    valid_windows = to_windows(valid_field)[..., 0]

    def step_window(totals, inputs):
        dcells, qkv_part, proj_part = window_grads(inputs[0], inputs[1], inputs[2], norm_gain, w_qkv, w_proj)
        return ((totals[0] + qkv_part, totals[1] + proj_part), dcells)
    starting = (jnp.zeros((D, 3 * D), jnp.float32), jnp.zeros((D, D), jnp.float32))
    sums, dwindows = lax.scan(step_window, starting, (to_windows(shifted), to_windows(cotangent), valid_windows))
    dshift = from_windows(dwindows, BATCH, NLAT, NLON)
    returned = shift_behind(dshift)
    grad_in = (grad_out.astype(jnp.float32) + returned.astype(jnp.float32)).astype(jnp.bfloat16)
    factor = float(CELLS) ** (-0.5)
    return (grad_in, sums[0] * factor, sums[1] * factor)
```

```python
import functools, math
import jax, jax.numpy as jnp
from jax import lax
from jax.experimental import pallas as pl
from jax.experimental.pallas import tpu as pltpu

from jax.sharding import PartitionSpec as P

HEADS = 6
WIN = 30
SHIFT = 15
EPSILON = 1e-05
BF = jnp.bfloat16
F32 = jnp.float32
LN2 = math.log(2.0)

def mm(a, b):
    return lax.dot_general(a, b, (((1,), (0,)), ((), ())), preferred_element_type=F32)

def mm_t(a, b):
    return lax.dot_general(a, b, (((1,), (1,)), ((), ())), preferred_element_type=F32)

def blocks_of(n, step):
    return [(at, min(step, n - at)) for at in range(0, n, step)]

def window_kernel(head, x_ref, c_ref, valid_ref, gain_ref, wqkv_ref, wproj_ref,
                  d_ref, gq_ref, gp_ref,
                  nl, q_s, k_s, v_s, b_s, kT, vT, bT, e_s, p_s, ds_s, dqkv, attT):
    cells, width = x_ref.shape
    pair = 2 * head
    pairs = width // pair
    qscale = head ** -0.5 / LN2
    x = x_ref[...].astype(F32)
    mean = jnp.mean(x, axis=1, keepdims=True)
    cen = x - mean
    rstd = lax.rsqrt(jnp.mean(cen * cen, axis=1, keepdims=True) + EPSILON)
    gain = gain_ref[...]
    nl[...] = (cen * rstd * gain).astype(BF)
    qb = blocks_of(cells, 256)

    def one_pair(j, _):
        cols = pl.ds(pl.multiple_of(j * pair, pair), pair)
        colk = pl.ds(pl.multiple_of(width + j * pair, pair), pair)
        colv = pl.ds(pl.multiple_of(2 * width + j * pair, pair), pair)
        q_s[...] = (mm(nl[...], wqkv_ref[:, cols]) * qscale).astype(BF)
        k_s[...] = mm(nl[...], wqkv_ref[:, colk]).astype(BF)
        v_s[...] = mm(nl[...], wqkv_ref[:, colv]).astype(BF)
        b_s[...] = mm_t(c_ref[...], wproj_ref[cols, :]).astype(BF)
        kT[...] = k_s[...].T
        vT[...] = v_s[...].T
        bT[...] = b_s[...].T
        lane = lax.broadcasted_iota(jnp.int32, (cells, pair), 1)
        row = lax.broadcasted_iota(jnp.int32, (pair, cells), 0)
        valid_col = valid_ref[0]
        outs = []
        for h in range(2):
            own = (lane >= head) if h else (lane < head)
            own_r = (row >= head) if h else (row < head)
            aug = 0 if h else head
            bias = jnp.where(lane == aug, (valid_col - 1.0) * 30000.0, 0.0).astype(BF)
            kk = jnp.where(own, k_s[...], bias)
            qq = jnp.where(own, q_s[...], jnp.where(lane == aug, 1.0, 0.0).astype(BF))
            two = (lane == aug) | (lane == aug + 1)
            vv = jnp.where(own, v_s[...], jnp.where(two, 1.0, 0.0).astype(BF))
            vvT = jnp.where(own_r, vT[...], jnp.where(row == aug, 1.0, 0.0).astype(BF))
            for at, n in qb:
                s = mm_t(kk, qq[at:at + n])
                e = jnp.exp2(s).astype(BF)
                oT = mm(vvT, e)
                total = oT[aug:aug + 1]
                inv = 1.0 / total
                aT = oT * inv
                attT[pl.ds(pl.multiple_of(j * pair + h * head, head), head), at:at + n] = aT[h * head:(h + 1) * head].astype(BF)
                bTn = bT[:, at:at + n].astype(F32)
                ownn = own_r[:, :n]
                rown = row[:, :n]
                rt = jnp.sum(jnp.where(ownn, bTn * aT, 0.0), axis=0, keepdims=True)
                hi = rt.astype(BF).astype(F32)
                lo = rt - hi
                baug = jnp.where(ownn, bTn, jnp.where(rown == aug, -hi, jnp.where(rown == aug + 1, -lo, 0.0))).astype(BF)
                p = e * inv.astype(BF)
                p_s[h, :, at:at + n] = p
                dp = mm(vv, baug).astype(BF)
                ds_s[h, :, at:at + n] = p * dp
            dv = mm(p_s[h], b_s[...])
            dk = mm(ds_s[h], q_s[...]) * LN2
            dqT = mm(kT[...], ds_s[h]) * (head ** -0.5)
            outs.append((dqT, dk, dv))
        dqT = jnp.where(row < head, outs[0][0], outs[1][0]).astype(BF)
        dqkv[:, cols] = dqT.T
        dqkv[:, colk] = jnp.where(lane < head, outs[0][1], outs[1][1]).astype(BF)
        dqkv[:, colv] = jnp.where(lane < head, outs[0][2], outs[1][2]).astype(BF)
        return 0

    lax.fori_loop(0, pairs, one_pair, 0)
    gp_ref[...] = mm(attT[...], c_ref[...])
    gq_ref[...] = mm(nl[...].T, dqkv[...])
    dn = mm_t(dqkv[...], wqkv_ref[...]) * gain
    normed = cen * rstd
    d = rstd * (dn - jnp.mean(dn, axis=1, keepdims=True) - normed * jnp.mean(dn * normed, axis=1, keepdims=True))
    d_ref[...] = d.astype(BF)

def window_call(x, c, valid, gain, wqkv, wproj):
    cells, width = x.shape
    head = width // HEADS
    pair = 2 * head
    return pl.pallas_call(
        functools.partial(window_kernel, head),
        out_shape=(jax.ShapeDtypeStruct((cells, width), BF),
                   jax.ShapeDtypeStruct((width, 3 * width), F32),
                   jax.ShapeDtypeStruct((width, width), F32)),
        in_specs=[pl.BlockSpec(memory_space=pltpu.VMEM)] * 6,
        out_specs=[pl.BlockSpec(memory_space=pltpu.VMEM)] * 3,
        scratch_shapes=[pltpu.VMEM((cells, width), BF)]
        + [pltpu.VMEM((cells, pair), BF)] * 4
        + [pltpu.VMEM((pair, cells), BF)] * 3
        + [pltpu.VMEM((1, 128), BF)]
        + [pltpu.VMEM((2, cells, cells), BF)] * 2
        + [pltpu.VMEM((cells, 3 * width), BF), pltpu.VMEM((width, cells), BF)],
        cost_estimate=pl.CostEstimate(flops=24 * cells * width * width + 12 * cells * cells * width, bytes_accessed=8 * 2**20, transcendentals=HEADS * cells * cells),
        compiler_params=pltpu.CompilerParams(vmem_limit_bytes=56 * 2**20),
    )(x, c, valid, gain, wqkv, wproj)


def permuted(value, axes, target):
    sizes = [lax.axis_size(a) for a in axes]
    pairs = []
    for source in range(math.prod(sizes)):
        at, rest = [], source
        for size in reversed(sizes):
            at.append(rest % size)
            rest //= size
        goal = target(*reversed(at))
        if goal is None:
            continue
        flat = 0
        for size, place in zip(sizes, goal):
            flat = flat * size + place
        pairs.append((source, flat))
    return lax.ppermute(value, tuple(axes), pairs)


def from_next(value, lat=False, lon=False):
    rows, cols = lax.axis_size("lat"), lax.axis_size("lon")

    def target(i, j):
        a, b = i - int(lat), (j - int(lon)) % cols
        return (a, b) if a >= 0 else None

    return permuted(value, ("lat", "lon"), target)


def to_next(value, lat=False, lon=False):
    rows, cols = lax.axis_size("lat"), lax.axis_size("lon")

    def target(i, j):
        a, b = i + int(lat), (j + int(lon)) % cols
        return (a, b) if a < rows else None

    return permuted(value, ("lat", "lon"), target)


def scatter_direct(value, axis, dim):
    count = lax.axis_size(axis)
    me = lax.axis_index(axis)
    share = value.shape[dim] // count
    total = lax.dynamic_slice_in_dim(value, me * share, share, dim).astype(F32)
    for step in range(1, count):
        goal = (me + step) % count
        part = lax.dynamic_slice_in_dim(value, goal * share, share, dim).astype(BF)
        got = permuted(part, (axis,), lambda i, s=step: ((i + s) % count,))
        total = total + got.astype(F32)
    return total


def scatter_bit(value, axis, bit, dim):
    me = (lax.axis_index(axis) // bit) % 2
    mine = lax.dynamic_index_in_dim(value, me, dim, keepdims=False).astype(F32)
    other = lax.dynamic_index_in_dim(value, 1 - me, dim, keepdims=False).astype(BF)
    got = permuted(other, (axis,), lambda i: (i ^ bit,))
    return mine + got.astype(F32)


def reduce_weights(gq, gp):
    lats, lons, dps = lax.axis_size("lat"), lax.axis_size("lon"), lax.axis_size("dp")
    width = gq.shape[1]
    parts = lats * lons
    joined = jnp.concatenate(
        [gq.reshape(parts, -1, width), gp.reshape(parts, -1, width)], axis=1
    )
    deep = joined.shape[1]
    total = joined.reshape(lats, lons, deep, width)
    bit = 1
    left = lons
    while left % 2 == 0:
        shape = total.shape
        total = scatter_bit(
            total.reshape(lats, left // 2, 2, deep, total.shape[-1]), "lon", bit, 2
        )
        left //= 2
        bit *= 2
        if bit == 2:
            total = scatter_direct(total, "dp", 3)
    if left > 1:
        raise ValueError("lon size")
    total = total.reshape(lats, deep, total.shape[-1])
    total = scatter_direct(total, "lat", 0)[0]
    cut = gq.shape[0] // parts
    return total[:cut].T, total[cut:].T


def per_device(hidden_in, grad_out, norm_gain, w_qkv, w_proj):
    samples, lat_rows, lon_cols, width = hidden_in.shape
    half = WIN // 2
    nr, nc = lat_rows // WIN, lon_cols // WIN
    short = half + (-half) % 16
    wide = WIN + (-WIN) % 16
    both = jnp.stack([hidden_in, grad_out])
    gain = norm_gain.reshape(1, width)

    def piece(rows_at, cols_at, n, pad_to):
        cut = lax.slice_in_dim(both, rows_at, rows_at + half, axis=2)
        cut = lax.slice_in_dim(cut, cols_at, cols_at + n, axis=3)
        return jnp.pad(cut, ((0, 0), (0, 0), (0, 0), (0, pad_to - n), (0, 0)))

    last = lax.axis_index("lat") == lax.axis_size("lat") - 1
    inner = [wc * WIN + SHIFT for wc in range(nc - 1)]
    edge = (nc - 1) * WIN + SHIFT
    lat_in = [from_next(piece(0, at, WIN, wide), lat=True) for at in inner]
    held = (piece(0, edge, half, short), piece(0, 0, half, short))
    lon_send = [piece(r * half, 0, half, short) for r in range(1, 2 * nr)]
    if lat_in:
        held, lat_in, lon_send = lax.optimization_barrier((held, lat_in, lon_send))
    lat_edge = from_next(held[0], lat=True)
    corner = from_next(held[1], lat=True, lon=True)
    lon_in = [from_next(p, lon=True) for p in lon_send]

    def valid_of(n, pad_to, pieces):
        ok = jnp.broadcast_to((jnp.arange(pad_to) < n)[None], (half, pad_to)).reshape(-1)
        count = len(pieces)
        oks = jnp.stack([ok & jnp.logical_not(p) for p in pieces]).reshape(-1)
        return jnp.broadcast_to(oks.astype(F32)[None, :, None], (1, oks.shape[0], 128))

    sums = None
    out_inner, out_edge = {}, {}
    for b in range(samples):
        for wc in range(nc):
            for wr in range(nr):
                end = wr == nr - 1
                gone = last if end else jnp.bool_(False)
                top = (2 * wr + 1) * half
                if wc < nc - 1:
                    low = lat_in[wc] if end else piece(top + half, inner[wc], WIN, wide)
                    parts = [piece(top, inner[wc], WIN, wide), low]
                    valid = valid_of(WIN, wide, [jnp.bool_(False), gone])
                else:
                    a = lat_edge if end else piece(top + half, edge, half, short)
                    d = corner if end else lon_in[2 * wr + 1]
                    parts = [piece(top, edge, half, short), lon_in[2 * wr], a, d]
                    valid = valid_of(half, short, [jnp.bool_(False)] * 2 + [gone] * 2)
                cells = jnp.concatenate(
                    [p[:, b].reshape(2, -1, width) for p in parts], axis=1
                )
                dcells, gq, gp = window_call(cells[0], cells[1], valid, gain, w_qkv, w_proj)
                sums = (gq, gp) if sums is None else (sums[0] + gq, sums[1] + gp)
                if wc < nc - 1:
                    out_inner[b, wr, wc] = dcells.reshape(2, half, wide, width)[:, :, :WIN]
                else:
                    out_edge[b, wr] = dcells.reshape(2, 2, half, short, width)[:, :, :, :half]

    def over_lat(f):
        halves = [f(wr) for wr in range(nr)]
        carried = halves[nr - 1][1]
        own = [h for pair in halves for h in pair][:-1]
        return carried, own

    samples_out = []
    for b in range(samples):
        columns = []
        for wc in range(nc - 1):
            carried, own = over_lat(lambda wr: (out_inner[b, wr, wc][0], out_inner[b, wr, wc][1]))
            columns.append(jnp.concatenate([to_next(carried, lat=True)] + own, axis=0))
        carried, own = over_lat(lambda wr: (out_edge[b, wr][0, 0], out_edge[b, wr][1, 0]))
        columns.append(jnp.concatenate([to_next(carried, lat=True)] + own, axis=0))
        carried, own = over_lat(lambda wr: (out_edge[b, wr][0, 1], out_edge[b, wr][1, 1]))
        first = jnp.concatenate(
            [to_next(carried, lat=True, lon=True)] + [to_next(o, lon=True) for o in own], axis=0
        )
        samples_out.append(jnp.concatenate([first] + columns, axis=1))
    returned = jnp.stack(samples_out)
    grad_in = (grad_out.astype(F32) + returned.astype(F32)).astype(BF)
    total_cells = (
        lax.axis_size("dp") * samples * lat_rows * lax.axis_size("lat") * lon_cols * lax.axis_size("lon")
    )
    factor = float(total_cells) ** (-0.5)
    gq, gp = reduce_weights(sums[0].T, sums[1].T)
    return (grad_in, gq * factor, gp * factor)


def solution(mesh):
    in_specs = (P("dp", "lat", "lon", None), P("dp", "lat", "lon", None), P(), P(), P())
    out_specs = (P("dp", "lat", "lon", None), P("dp", ("lat", "lon")), P("dp", ("lat", "lon")))
    return jax.shard_map(
        per_device, mesh=mesh, in_specs=in_specs, out_specs=out_specs, check_vma=False
    )
```

```python
import functools, math
import jax, jax.numpy as jnp
from jax import lax
from jax.experimental import pallas as pl
from jax.experimental.pallas import tpu as pltpu

from jax.sharding import PartitionSpec as P

HEADS = 6
WIN = 30
SHIFT = 15
EPSILON = 1e-05
BF = jnp.bfloat16
F32 = jnp.float32
LN2 = math.log(2.0)

def mm(a, b):
    return lax.dot_general(a, b, (((1,), (0,)), ((), ())), preferred_element_type=F32)

def mm_t(a, b):
    return lax.dot_general(a, b, (((1,), (1,)), ((), ())), preferred_element_type=F32)

def blocks_of(n, step):
    return [(at, min(step, n - at)) for at in range(0, n, step)]

def window_kernel(head, metas, split, flag_ref, *refs):
    count = len(metas)
    pieces, refs = refs[:count], refs[count:]
    gain_ref, wqkv_ref, wproj_ref = refs[:3]
    refs = refs[3:]
    if split[0]:
        prev, refs = refs[:2], refs[2:]
    d_refs, refs = refs[:count], refs[count:]
    (gq_ref, gp_ref), refs = refs[:2], refs[2:]
    c_ref, nl, q_s, k_s, v_s, b_s, kT, vT, bT, p_s, ds_s, dqkv, attT = refs[:13]
    cells, width = c_ref.shape
    pair = 2 * head
    pairs = width // pair
    qscale = head ** -0.5 / LN2
    at = 0
    starts = []
    for p in pieces:
        starts.append(at)
        c_ref[at:at + p.shape[1]] = p[1]
        at += p.shape[1]
    lastf = flag_ref[0].astype(F32)
    oks = []
    for p, (n, pad, gone) in zip(pieces, metas):
        place = lax.broadcasted_iota(jnp.int32, (p.shape[1], pair), 0)
        ok = jnp.where(lax.rem(place, pad) < n, 1.0, 0.0)
        oks.append(ok * (1.0 - lastf) if gone else ok)
    valid_col = jnp.concatenate(oks, axis=0)
    x = jnp.concatenate([p[0] for p in pieces], axis=0).astype(F32)
    mean = jnp.mean(x, axis=1, keepdims=True)
    cen = x - mean
    rstd = lax.rsqrt(jnp.mean(cen * cen, axis=1, keepdims=True) + EPSILON)
    gain = gain_ref[...]
    nl[...] = (cen * rstd * gain).astype(BF)
    qb = blocks_of(cells, cells)

    def one_pair(j, _):
        cols = pl.ds(pl.multiple_of(j * pair, pair), pair)
        colk = pl.ds(pl.multiple_of(width + j * pair, pair), pair)
        colv = pl.ds(pl.multiple_of(2 * width + j * pair, pair), pair)
        q_s[...] = (mm(nl[...], wqkv_ref[:, cols]) * qscale).astype(BF)
        k_s[...] = mm(nl[...], wqkv_ref[:, colk]).astype(BF)
        v_s[...] = mm(nl[...], wqkv_ref[:, colv]).astype(BF)
        b_s[...] = mm_t(c_ref[...], wproj_ref[cols, :]).astype(BF)
        kT[...] = k_s[...].T
        vT[...] = v_s[...].T
        bT[...] = b_s[...].T
        lane = lax.broadcasted_iota(jnp.int32, (cells, pair), 1)
        row = lax.broadcasted_iota(jnp.int32, (pair, cells), 0)
        outs = []
        for h in range(2):
            own = (lane >= head) if h else (lane < head)
            own_r = (row >= head) if h else (row < head)
            aug = 0 if h else head
            bias = jnp.where(lane == aug, (valid_col - 1.0) * 30000.0, 0.0).astype(BF)
            kk = jnp.where(own, k_s[...], bias)
            qq = jnp.where(own, q_s[...], jnp.where(lane == aug, 1.0, 0.0).astype(BF))
            two = (lane == aug) | (lane == aug + 1)
            vv = jnp.where(own, v_s[...], jnp.where(two, 1.0, 0.0).astype(BF))
            vvT = jnp.where(own_r, vT[...], jnp.where(row == aug, 1.0, 0.0).astype(BF))
            for at, n in qb:
                s = mm_t(kk, qq[at:at + n])
                e = jnp.exp2(s).astype(BF)
                oT = mm(vvT, e)
                total = oT[aug:aug + 1]
                inv = 1.0 / total
                aT = oT * inv
                attT[pl.ds(pl.multiple_of(j * pair + h * head, head), head), at:at + n] = aT[h * head:(h + 1) * head].astype(BF)
                bTn = bT[:, at:at + n].astype(F32)
                ownn = own_r[:, :n]
                rown = row[:, :n]
                rt = jnp.sum(jnp.where(ownn, bTn * aT, 0.0), axis=0, keepdims=True)
                hi = rt.astype(BF).astype(F32)
                lo = rt - hi
                baug = jnp.where(ownn, bTn, jnp.where(rown == aug, -hi, jnp.where(rown == aug + 1, -lo, 0.0))).astype(BF)
                p = e * inv.astype(BF)
                p_s[h, :, at:at + n] = p
                dp = mm(vv, baug).astype(BF)
                ds_s[h, :, at:at + n] = p * dp
            dv = mm(p_s[h], b_s[...])
            dk = mm(ds_s[h], q_s[...]) * LN2
            dqT = mm(kT[...], ds_s[h]) * (head ** -0.5)
            outs.append((dqT, dk, dv))
        dqT = jnp.where(row < head, outs[0][0], outs[1][0]).astype(BF)
        dqkv[:, cols] = dqT.T
        dqkv[:, colk] = jnp.where(lane < head, outs[0][1], outs[1][1]).astype(BF)
        dqkv[:, colv] = jnp.where(lane < head, outs[0][2], outs[1][2]).astype(BF)
        return 0

    lax.fori_loop(0, pairs, one_pair, 0)
    gp = mm(attT[...], c_ref[...])
    gq = mm(nl[...].T, dqkv[...])
    if split[0]:
        gq = gq + prev[0][...]
        gp = gp + prev[1][...]
    if split[1] is None:
        gq_ref[...] = gq
        gp_ref[...] = gp
    else:
        joined = refs[13]
        parts = split[1]
        gqT, gpT = gq.T, gp.T
        dq_rows, dp_rows = gqT.shape[0] // parts, gpT.shape[0] // parts
        for i in range(parts):
            joined[i, :dq_rows] = gqT[i * dq_rows:(i + 1) * dq_rows]
            joined[i, dq_rows:] = gpT[i * dp_rows:(i + 1) * dp_rows]
        me = flag_ref[1]
        for i in range(parts // 2):
            gq_ref[i] = joined[2 * i + me]
            gp_ref[i] = joined[2 * i + 1 - me].astype(BF)
    dn = mm_t(dqkv[...], wqkv_ref[...]) * gain
    normed = cen * rstd
    d = rstd * (dn - jnp.mean(dn, axis=1, keepdims=True) - normed * jnp.mean(dn * normed, axis=1, keepdims=True))
    d = d.astype(BF)
    for ref, at in zip(d_refs, starts):
        ref[...] = d[at:at + ref.shape[0]]


def window_call(pieces, metas, flags, gain, wqkv, wproj, prev, parts):
    width = wproj.shape[0]
    head = width // HEADS
    pair = 2 * head
    sizes = [p.shape[1] for p in pieces]
    cells = sum(sizes)
    deep = 4 * width // parts if parts else 0
    if parts is None:
        sums = (jax.ShapeDtypeStruct((width, 3 * width), F32), jax.ShapeDtypeStruct((width, width), F32))
    else:
        sums = (jax.ShapeDtypeStruct((parts // 2, deep, width), F32),
                jax.ShapeDtypeStruct((parts // 2, deep, width), BF))
    scratch = ([pltpu.VMEM((cells, width), BF)] * 2
               + [pltpu.VMEM((cells, pair), BF)] * 4
               + [pltpu.VMEM((pair, cells), BF)] * 3
               + [pltpu.VMEM((2, cells, cells), BF)] * 2
               + [pltpu.VMEM((cells, 3 * width), BF), pltpu.VMEM((width, cells), BF)])
    if parts is not None:
        scratch.append(pltpu.VMEM((parts, deep, width), F32))
    vmem = pl.BlockSpec(memory_space=pltpu.VMEM)
    args = list(pieces) + [gain, wqkv, wproj] + (list(prev) if prev else [])
    outs = pl.pallas_call(
        functools.partial(window_kernel, head, metas, (prev is not None, parts)),
        out_shape=tuple(jax.ShapeDtypeStruct((n, width), BF) for n in sizes) + sums,
        in_specs=[pl.BlockSpec(memory_space=pltpu.SMEM)] + [vmem] * len(args),
        out_specs=[vmem] * (len(sizes) + 2),
        scratch_shapes=scratch,
        cost_estimate=pl.CostEstimate(
            flops=24 * cells * width * width + 12 * cells * cells * width,
            bytes_accessed=8 * 2**20,
            transcendentals=HEADS * cells * cells,
        ),
        compiler_params=pltpu.CompilerParams(vmem_limit_bytes=60 * 2**20),
    )(flags, *args)
    return outs[:len(sizes)], outs[-2:]


def permuted(value, axes, target):
    sizes = [lax.axis_size(a) for a in axes]
    pairs = []
    for source in range(math.prod(sizes)):
        at, rest = [], source
        for size in reversed(sizes):
            at.append(rest % size)
            rest //= size
        goal = target(*reversed(at))
        if goal is None:
            continue
        flat = 0
        for size, place in zip(sizes, goal):
            flat = flat * size + place
        pairs.append((source, flat))
    return lax.ppermute(value, tuple(axes), pairs)


def from_next(value, lat=False, lon=False):
    rows, cols = lax.axis_size("lat"), lax.axis_size("lon")

    def target(i, j):
        a, b = i - int(lat), (j - int(lon)) % cols
        return (a, b) if a >= 0 else None

    return permuted(value, ("lat", "lon"), target)


def to_next(value, lat=False, lon=False):
    rows, cols = lax.axis_size("lat"), lax.axis_size("lon")

    def target(i, j):
        a, b = i + int(lat), (j + int(lon)) % cols
        return (a, b) if a < rows else None

    return permuted(value, ("lat", "lon"), target)


def scatter_direct(value, axis, dim):
    count = lax.axis_size(axis)
    me = lax.axis_index(axis)
    share = value.shape[dim] // count
    total = lax.dynamic_slice_in_dim(value, me * share, share, dim).astype(F32)
    for step in range(1, count):
        goal = (me + step) % count
        part = lax.dynamic_slice_in_dim(value, goal * share, share, dim).astype(BF)
        got = permuted(part, (axis,), lambda i, s=step: ((i + s) % count,))
        total = total + got.astype(F32)
    return total


def scatter_bit(value, axis, bit, dim):
    me = (lax.axis_index(axis) // bit) % 2
    mine = lax.dynamic_index_in_dim(value, me, dim, keepdims=False).astype(F32)
    other = lax.dynamic_index_in_dim(value, 1 - me, dim, keepdims=False).astype(BF)
    got = permuted(other, (axis,), lambda i: (i ^ bit,))
    return mine + got.astype(F32)


def reduce_weights(keep, send, lons):
    half, deep, width = keep.shape
    got = permuted(send, ("lon",), lambda i: (i ^ 1,))
    lats = lax.axis_size("lat")
    total = (keep + got.astype(F32)).reshape(lats, lons // 2, deep, width)
    bit, left = 2, lons // 2
    while left > 1:
        total = scatter_bit(total.reshape(lats, left // 2, 2, deep, width), "lon", bit, 2)
        left //= 2
        bit *= 2
    total = scatter_direct(total.reshape(lats, deep, width), "dp", 2)
    return scatter_direct(total, "lat", 0)[0]


def per_device(hidden_in, grad_out, norm_gain, w_qkv, w_proj):
    samples, lat_rows, lon_cols, width = hidden_in.shape
    half = WIN // 2
    nr, nc = lat_rows // WIN, lon_cols // WIN
    short = half + (-half) % 16
    wide = WIN + (-WIN) % 16
    gain = norm_gain.reshape(1, width)
    lons = lax.axis_size("lon")
    parts = lax.axis_size("lat") * lons
    if lons & (lons - 1) or lons < 2:
        raise ValueError("lon size")

    def pieces_of(x, c):
        def piece(rows_at, cols_at, n, pad_to, rows=half):
            cuts = [v[:, rows_at:rows_at + rows, cols_at:cols_at + n] for v in (x, c)]
            return jnp.pad(jnp.stack(cuts), ((0, 0), (0, 0), (0, 0), (0, pad_to - n), (0, 0)))
        return piece

    at_last = lax.axis_index("lat") == lax.axis_size("lat") - 1
    flags = jnp.stack([at_last.astype(jnp.int32), lax.axis_index("lon") % 2])
    inner = [wc * WIN + SHIFT for wc in range(nc - 1)]
    edge = (nc - 1) * WIN + SHIFT
    first = pieces_of(hidden_in, grad_out)
    lat_send = [first(0, at, WIN, wide) for at in inner]
    hid, got, lat_send = lax.optimization_barrier((hidden_in, grad_out, lat_send))
    lat_in = [from_next(p, lat=True) for p in lat_send]
    piece = pieces_of(hid, got)
    lon_in = from_next(piece(0, 0, half, short, lat_rows), lon=True)
    edge_send = jnp.stack([piece(0, edge, half, short), lon_in[:, :, :half]], axis=2)
    if lat_in:
        edge_send, lat_in = lax.optimization_barrier((edge_send, lat_in))
    edge_in = from_next(edge_send, lat=True)

    order = [(b, wr, wc) for b in range(samples) for wc in range(nc) for wr in range(nr)]
    sums = None
    out = {}
    for step, (b, wr, wc) in enumerate(order):
        end = wr == nr - 1
        top = (2 * wr + 1) * half
        if wc < nc - 1:
            low = lat_in[wc] if end else piece(top + half, inner[wc], WIN, wide)
            cells = [piece(top, inner[wc], WIN, wide), low]
            metas = ((WIN, wide, False), (WIN, wide, end))
        else:
            side = lon_in[:, :, top:top + half]
            if end:
                low = [edge_in[:, :, 0], edge_in[:, :, 1]]
            else:
                low = [piece(top + half, edge, half, short), lon_in[:, :, top + half:top + WIN]]
            cells = [piece(top, edge, half, short), side] + low
            metas = ((half, short, False),) * 2 + ((half, short, end),) * 2
        cells = [p[:, b].reshape(2, -1, width) for p in cells]
        done, sums = window_call(
            cells, metas, flags, gain, w_qkv, w_proj, sums, parts if step == len(order) - 1 else None
        )
        out[b, wr, wc] = [
            d.reshape(half, pad, width)[:, :n] for d, (n, pad, _) in zip(done, metas)
        ]

    rows_out = []
    for b in range(samples):
        columns = []
        for wc in range(nc - 1):
            carried = to_next(out[b, nr - 1, wc][1], lat=True)
            own = [out[b, wr, wc][i] for wr in range(nr) for i in range(2)][:-1]
            columns.append(jnp.concatenate([carried] + own, axis=0))
        carried = to_next(out[b, nr - 1, nc - 1][2], lat=True)
        own = [out[b, wr, nc - 1][i] for wr in range(nr) for i in (0, 2)][:-1]
        columns.append(jnp.concatenate([carried] + own, axis=0))
        carried = to_next(out[b, nr - 1, nc - 1][3], lat=True, lon=True)
        own = [to_next(out[b, wr, nc - 1][i], lon=True) for wr in range(nr) for i in (1, 3)][:-1]
        columns.insert(0, jnp.concatenate([carried] + own, axis=0))
        rows_out.append(jnp.concatenate(columns, axis=1))
    returned = jnp.stack(rows_out)
    grad_in = (grad_out.astype(F32) + returned.astype(F32)).astype(BF)
    total_cells = (
        lax.axis_size("dp") * samples * lat_rows * lax.axis_size("lat") * lon_cols * lons
    )
    factor = float(total_cells) ** (-0.5)
    total = reduce_weights(sums[0], sums[1], lons).T * factor
    cut = 3 * width // parts
    return (grad_in, total[:, :cut], total[:, cut:])


def solution(mesh):
    in_specs = (P("dp", "lat", "lon", None), P("dp", "lat", "lon", None), P(), P(), P())
    out_specs = (P("dp", "lat", "lon", None), P("dp", ("lat", "lon")), P("dp", ("lat", "lon")))
    return jax.shard_map(
        per_device, mesh=mesh, in_specs=in_specs, out_specs=out_specs, check_vma=False
    )
```

```python
import functools, math
import jax, jax.numpy as jnp
from jax import lax
from jax.experimental import pallas as pl
from jax.experimental.pallas import tpu as pltpu

from jax.sharding import PartitionSpec as P

HEADS = 6
WIN = 30
SHIFT = 15
EPSILON = 1e-05
BF = jnp.bfloat16
F32 = jnp.float32
LN2 = math.log(2.0)

def mm(a, b):
    return lax.dot_general(a, b, (((1,), (0,)), ((), ())), preferred_element_type=F32)

def mm_t(a, b):
    return lax.dot_general(a, b, (((1,), (1,)), ((), ())), preferred_element_type=F32)

def blocks_of(n, step):
    return [(at, min(step, n - at)) for at in range(0, n, step)]

def window_kernel(head, metas, split, *refs):
    count = len(metas)
    pieces, refs = refs[:count], refs[count:]
    gain_ref, wqkv_ref, wproj_ref = refs[:3]
    refs = refs[3:]
    if split[0]:
        prev, refs = refs[:2], refs[2:]
    d_refs, refs = refs[:count], refs[count:]
    (gq_ref, gp_ref), refs = refs[:2], refs[2:]
    c_ref, nl, q_s, k_s, v_s, b_s, kT, vT, bT, p_s, ds_s, dqkv, attT = refs[:13]
    cells, width = c_ref.shape
    pair = 2 * head
    pairs = width // pair
    qscale = head ** -0.5 / LN2
    at = 0
    starts = []
    for p in pieces:
        starts.append(at)
        c_ref[at:at + p.shape[1]] = p[1]
        at += p.shape[1]
    odd = lax.rem(lax.axis_index("lon"), 2)
    packed = jnp.where((lax.axis_index("lat") == lax.axis_size("lat") - 1) & (odd == 0), 1.0, 0.0)
    oks, seconds = [], []
    for p, (n, pad, other) in zip(pieces, metas):
        place = lax.broadcasted_iota(jnp.int32, (p.shape[1], pair), 0)
        oks.append(jnp.where(lax.rem(place, pad) < n, 1.0, 0.0))
        seconds.append(jnp.full((p.shape[1], pair), packed if other else 0.0, F32))
    valid_col = jnp.concatenate(oks, axis=0)
    second = jnp.concatenate(seconds, axis=0)
    x = jnp.concatenate([p[0] for p in pieces], axis=0).astype(F32)
    mean = jnp.mean(x, axis=1, keepdims=True)
    cen = x - mean
    rstd = lax.rsqrt(jnp.mean(cen * cen, axis=1, keepdims=True) + EPSILON)
    gain = gain_ref[...][None]
    nl[...] = (cen * rstd * gain).astype(BF)
    qb = blocks_of(cells, cells)

    def one_pair(j, _):
        cols = pl.ds(pl.multiple_of(j * pair, pair), pair)
        colk = pl.ds(pl.multiple_of(width + j * pair, pair), pair)
        colv = pl.ds(pl.multiple_of(2 * width + j * pair, pair), pair)
        q_s[...] = (mm(nl[...], wqkv_ref[:, cols]) * qscale).astype(BF)
        k_s[...] = mm(nl[...], wqkv_ref[:, colk]).astype(BF)
        v_s[...] = mm(nl[...], wqkv_ref[:, colv]).astype(BF)
        b_s[...] = mm_t(c_ref[...], wproj_ref[cols, :]).astype(BF)
        kT[...] = k_s[...].T
        vT[...] = v_s[...].T
        bT[...] = b_s[...].T
        lane = lax.broadcasted_iota(jnp.int32, (cells, pair), 1)
        row = lax.broadcasted_iota(jnp.int32, (pair, cells), 0)
        outs = []
        for h in range(2):
            own = (lane >= head) if h else (lane < head)
            own_r = (row >= head) if h else (row < head)
            aug = 0 if h else head
            seen = jnp.where(lane == aug, valid_col * (1.0 - second), valid_col * second)
            two = (lane == aug) | (lane == aug + 1)
            bias = jnp.where(two, (seen - 1.0) * 30000.0, 0.0).astype(BF)
            group = jnp.where(lane == aug, 1.0 - second, second)
            kk = jnp.where(own, k_s[...], bias)
            qq = jnp.where(own, q_s[...], jnp.where(two, group, 0.0).astype(BF))
            vv = jnp.where(own, v_s[...], jnp.where(two, 1.0, 0.0).astype(BF))
            vvT = jnp.where(own_r, vT[...], jnp.where(row == aug, 1.0, 0.0).astype(BF))
            for at, n in qb:
                s = mm_t(kk, qq[at:at + n])
                e = jnp.exp2(s).astype(BF)
                oT = mm(vvT, e)
                total = oT[aug:aug + 1]
                inv = 1.0 / total
                aT = oT * inv
                attT[pl.ds(pl.multiple_of(j * pair + h * head, head), head), at:at + n] = aT[h * head:(h + 1) * head].astype(BF)
                bTn = bT[:, at:at + n].astype(F32)
                ownn = own_r[:, :n]
                rown = row[:, :n]
                rt = jnp.sum(jnp.where(ownn, bTn * aT, 0.0), axis=0, keepdims=True)
                hi = rt.astype(BF).astype(F32)
                lo = rt - hi
                baug = jnp.where(ownn, bTn, jnp.where(rown == aug, -hi, jnp.where(rown == aug + 1, -lo, 0.0))).astype(BF)
                p = e * inv.astype(BF)
                p_s[h, :, at:at + n] = p
                dp = mm(vv, baug).astype(BF)
                ds_s[h, :, at:at + n] = p * dp
            dv = mm(p_s[h], b_s[...])
            dk = mm(ds_s[h], q_s[...]) * LN2
            dqT = mm(kT[...], ds_s[h]) * (head ** -0.5)
            outs.append((dqT, dk, dv))
        dqT = jnp.where(row < head, outs[0][0], outs[1][0]).astype(BF)
        dqkv[:, cols] = dqT.T
        dqkv[:, colk] = jnp.where(lane < head, outs[0][1], outs[1][1]).astype(BF)
        dqkv[:, colv] = jnp.where(lane < head, outs[0][2], outs[1][2]).astype(BF)
        return 0

    lax.fori_loop(0, pairs, one_pair, 0)
    gp = mm(attT[...], c_ref[...])
    gq = mm(nl[...].T, dqkv[...])
    if split[0]:
        gq = gq + prev[0][...]
        gp = gp + prev[1][...]
    if split[1] is None:
        gq_ref[...] = gq
        gp_ref[...] = gp
    else:
        joined = refs[13]
        parts = split[1]
        gqT, gpT = gq.T, gp.T
        dq_rows, dp_rows = gqT.shape[0] // parts, gpT.shape[0] // parts
        for i in range(parts):
            joined[i, :dq_rows] = gqT[i * dq_rows:(i + 1) * dq_rows]
            joined[i, dq_rows:] = gpT[i * dp_rows:(i + 1) * dp_rows]
        me = odd
        for i in range(parts // 2):
            gq_ref[i] = joined[2 * i + me]
            gp_ref[i] = joined[2 * i + 1 - me].astype(BF)
    dn = mm_t(dqkv[...], wqkv_ref[...]) * gain
    normed = cen * rstd
    d = rstd * (dn - jnp.mean(dn, axis=1, keepdims=True) - normed * jnp.mean(dn * normed, axis=1, keepdims=True))
    d = d.astype(BF)
    for ref, at in zip(d_refs, starts):
        ref[...] = d[at:at + ref.shape[0]]


def window_call(pieces, metas, gain, wqkv, wproj, prev, parts):
    width = wproj.shape[0]
    head = width // HEADS
    pair = 2 * head
    sizes = [p.shape[1] for p in pieces]
    cells = sum(sizes)
    deep = 4 * width // parts if parts else 0
    if parts is None:
        sums = (jax.ShapeDtypeStruct((width, 3 * width), F32), jax.ShapeDtypeStruct((width, width), F32))
    else:
        sums = (jax.ShapeDtypeStruct((parts // 2, deep, width), F32),
                jax.ShapeDtypeStruct((parts // 2, deep, width), BF))
    scratch = ([pltpu.VMEM((cells, width), BF)] * 2
               + [pltpu.VMEM((cells, pair), BF)] * 4
               + [pltpu.VMEM((pair, cells), BF)] * 3
               + [pltpu.VMEM((2, cells, cells), BF)] * 2
               + [pltpu.VMEM((cells, 3 * width), BF), pltpu.VMEM((width, cells), BF)])
    if parts is not None:
        scratch.append(pltpu.VMEM((parts, deep, width), F32))
    vmem = pl.BlockSpec(memory_space=pltpu.VMEM)
    args = list(pieces) + [gain, wqkv, wproj] + (list(prev) if prev else [])
    outs = pl.pallas_call(
        functools.partial(window_kernel, head, metas, (prev is not None, parts)),
        out_shape=tuple(jax.ShapeDtypeStruct((n, width), BF) for n in sizes) + sums,
        in_specs=[vmem] * len(args),
        out_specs=[vmem] * (len(sizes) + 2),
        scratch_shapes=scratch,
        cost_estimate=pl.CostEstimate(
            flops=24 * cells * width * width + 12 * cells * cells * width,
            bytes_accessed=8 * 2**20,
            transcendentals=HEADS * cells * cells,
        ),
        compiler_params=pltpu.CompilerParams(vmem_limit_bytes=60 * 2**20),
    )(*args)
    return outs[:len(sizes)], outs[-2:]


def permuted(value, axes, target):
    sizes = [lax.axis_size(a) for a in axes]
    pairs = []
    for source in range(math.prod(sizes)):
        at, rest = [], source
        for size in reversed(sizes):
            at.append(rest % size)
            rest //= size
        goal = target(*reversed(at))
        if goal is None:
            continue
        flat = 0
        for size, place in zip(sizes, goal):
            flat = flat * size + place
        pairs.append((source, flat))
    return lax.ppermute(value, tuple(axes), pairs)


def shared(value, back=False):
    lats, lons = lax.axis_size("lat"), lax.axis_size("lon")
    pairs = []
    for i in range(lats):
        for j in range(lons):
            if j % 2 == 0:
                goal = (i - 1, j) if i > 0 else None
            else:
                goal = (i + 1, j) if i < lats - 1 else (i, j - 1)
            if goal is not None:
                pair = (i * lons + j, goal[0] * lons + goal[1])
                pairs.append(pair[::-1] if back else pair)
    return lax.ppermute(value, ("lat", "lon"), pairs)


def along_lon(value, step):
    count = lax.axis_size("lon")
    return lax.ppermute(value, "lon", [(j, (j + step) % count) for j in range(count)])


def scatter_direct(value, axis, dim):
    count = lax.axis_size(axis)
    me = lax.axis_index(axis)
    share = value.shape[dim] // count
    total = lax.dynamic_slice_in_dim(value, me * share, share, dim).astype(F32)
    for step in range(1, count):
        goal = (me + step) % count
        part = lax.dynamic_slice_in_dim(value, goal * share, share, dim).astype(BF)
        got = permuted(part, (axis,), lambda i, s=step: ((i + s) % count,))
        total = total + got.astype(F32)
    return total


def scatter_bit(value, axis, bit, dim):
    me = (lax.axis_index(axis) // bit) % 2
    mine = lax.dynamic_index_in_dim(value, me, dim, keepdims=False).astype(F32)
    other = lax.dynamic_index_in_dim(value, 1 - me, dim, keepdims=False).astype(BF)
    got = permuted(other, (axis,), lambda i: (i ^ bit,))
    return mine + got.astype(F32)


def reduce_weights(keep, send, lons):
    half, deep, width = keep.shape
    got = permuted(send, ("lon",), lambda i: (i ^ 1,))
    lats = lax.axis_size("lat")
    total = (keep + got.astype(F32)).reshape(lats, lons // 2, deep, width)
    bit, left = 2, lons // 2
    while left > 1:
        total = scatter_bit(total.reshape(lats, left // 2, 2, deep, width), "lon", bit, 2)
        left //= 2
        bit *= 2
    total = scatter_direct(total.reshape(lats, deep, width), "dp", 2)
    return scatter_direct(total, "lat", 0)[0]


def per_device(hidden_in, grad_out, norm_gain, w_qkv, w_proj):
    samples, lat_rows, lon_cols, width = hidden_in.shape
    half = WIN // 2
    nr, nc = lat_rows // WIN, lon_cols // WIN
    short = half + (-half) % 16
    wide = WIN + (-WIN) % 16
    lons = lax.axis_size("lon")
    parts = lax.axis_size("lat") * lons
    if lons & (lons - 1) or lons < 2:
        raise ValueError("lon size")

    odd = lax.axis_index("lon") % 2
    idle = (lax.axis_index("lat") == 0) & (odd == 1)
    end = lat_rows - half
    own_at, sent_at = jnp.where(odd == 1, 0, end), jnp.where(odd == 1, end, 0)

    def pieces_of(x, c):
        def piece(rows_at, cols_at, n, pad_to, rows=half):
            cuts = [
                lax.dynamic_slice_in_dim(v[:, :, cols_at:cols_at + n], rows_at, rows, 1) for v in (x, c)
            ]
            return jnp.pad(jnp.stack(cuts), ((0, 0), (0, 0), (0, 0), (0, pad_to - n), (0, 0)))
        return piece

    def cleared(value):
        return jnp.where(idle, jnp.zeros_like(value), value)

    inner = [wc * WIN + SHIFT for wc in range(nc - 1)]
    edge = (nc - 1) * WIN + SHIFT
    first = pieces_of(hidden_in, grad_out)
    sent = [first(sent_at, at, WIN, wide) for at in inner]
    hid, cot, sent = lax.optimization_barrier((hidden_in, grad_out, sent))
    inner_in = [shared(p) for p in sent]
    piece = pieces_of(hid, cot)
    lon_in = along_lon(piece(0, 0, half, short, lat_rows), -1)
    own_inner = [cleared(piece(own_at, at, WIN, wide)) for at in inner]
    own_edge = cleared(piece(own_at, edge, half, short))

    def side(at):
        return lax.dynamic_slice_in_dim(lon_in, at, half, 2)

    own_side = cleared(side(own_at))
    edge_sent = jnp.stack([piece(sent_at, edge, half, short), side(sent_at)], axis=2)
    if inner_in:
        edge_sent, inner_in = lax.optimization_barrier((edge_sent, inner_in))
    edge_in = shared(edge_sent)

    order = [(b, wr, wc) for b in range(samples) for wc in range(nc) for wr in range(nr)]
    sums = None
    out = {}
    for step, (b, wr, wc) in enumerate(order):
        top = (2 * wr + 1) * half
        if wr < nr - 1 and wc < nc - 1:
            cells = [piece(top + i * half, inner[wc], WIN, wide) for i in range(2)]
            metas = ((WIN, wide, False),) * 2
        elif wr < nr - 1:
            cells = [
                f(top + i * half)
                for i in range(2)
                for f in (lambda at: piece(at, edge, half, short), side)
            ]
            metas = ((half, short, False),) * 4
        elif wc < nc - 1:
            cells = [own_inner[wc], inner_in[wc]]
            metas = ((WIN, wide, False), (WIN, wide, True))
        else:
            cells = [own_edge, own_side, edge_in[:, :, 0], edge_in[:, :, 1]]
            metas = ((half, short, False),) * 2 + ((half, short, True),) * 2
        cells = [p[:, b].reshape(2, -1, width) for p in cells]
        done, sums = window_call(
            cells, metas, norm_gain, w_qkv, w_proj, sums, parts if step == len(order) - 1 else None
        )
        out[b, wr, wc] = [d.reshape(half, pad, width) for d, (n, pad, _) in zip(done, metas)]

    rows_out = []
    for b in range(samples):
        def stacked(own, back, between):
            upper = jnp.where(odd == 1, own, back)
            lower = jnp.where(odd == 1, back, own)
            return jnp.concatenate([upper] + between + [lower], axis=0)

        columns = []
        for wc in range(nc - 1):
            own, other = out[b, nr - 1, wc]
            between = [out[b, wr, wc][i][:, :WIN] for wr in range(nr - 1) for i in range(2)]
            columns.append(stacked(own[:, :WIN], shared(other, back=True)[:, :WIN], between))
        own, own_lon, other, other_lon = out[b, nr - 1, nc - 1]
        back = shared(jnp.stack([other, other_lon]), back=True)
        between = [[out[b, wr, nc - 1][i] for wr in range(nr - 1) for i in (k, k + 2)] for k in range(2)]
        columns.append(stacked(own, back[0], between[0])[:, :half])
        columns.insert(0, along_lon(stacked(own_lon, back[1], between[1]), 1)[:, :half])
        rows_out.append(jnp.concatenate(columns, axis=1))
    returned = jnp.stack(rows_out)
    grad_in = (grad_out.astype(F32) + returned.astype(F32)).astype(BF)
    total_cells = (
        lax.axis_size("dp") * samples * lat_rows * lax.axis_size("lat") * lon_cols * lons
    )
    factor = float(total_cells) ** (-0.5)
    total = reduce_weights(sums[0], sums[1], lons).T * factor
    cut = 3 * width // parts
    return (grad_in, total[:, :cut], total[:, cut:])


def solution(mesh):
    in_specs = (P("dp", "lat", "lon", None), P("dp", "lat", "lon", None), P(), P(), P())
    out_specs = (P("dp", "lat", "lon", None), P("dp", ("lat", "lon")), P("dp", ("lat", "lon")))
    return jax.shard_map(
        per_device, mesh=mesh, in_specs=in_specs, out_specs=out_specs, check_vma=False
    )
```

```python
import functools, math
import jax, jax.numpy as jnp
from jax import lax
from jax.experimental import pallas as pl
from jax.experimental.pallas import tpu as pltpu

from jax.sharding import PartitionSpec as P

HEADS = 6
WIN = 30
SHIFT = 15
EPSILON = 1e-05
BF = jnp.bfloat16
F32 = jnp.float32
LN2 = math.log(2.0)

def mm(a, b):
    return lax.dot_general(a, b, (((1,), (0,)), ((), ())), preferred_element_type=F32)

def mm_t(a, b):
    return lax.dot_general(a, b, (((1,), (1,)), ((), ())), preferred_element_type=F32)

def blocks_of(n, step):
    return [(at, min(step, n - at)) for at in range(0, n, step)]

def window_kernel(head, metas, split, *refs):
    count = len(metas)
    pieces, refs = refs[:count], refs[count:]
    gain_ref, wqkv_ref, wproj_ref = refs[:3]
    refs = refs[3:]
    if split[0]:
        prev, refs = refs[:2], refs[2:]
    d_refs, refs = refs[:count], refs[count:]
    (gq_ref, gp_ref), refs = refs[:2], refs[2:]
    c_ref, nl, q_s, k_s, v_s, b_s, kT, vT, bT, p_s, ds_s, dqkv, attT = refs[:13]
    cells, width = c_ref.shape
    pair = 2 * head
    pairs = width // pair
    qscale = head ** -0.5 / LN2
    at = 0
    starts = []
    for p in pieces:
        starts.append(at)
        c_ref[at:at + p.shape[1]] = p[1]
        at += p.shape[1]
    odd = lax.rem(lax.axis_index("lon"), 2)
    packed = jnp.where((lax.axis_index("lat") == lax.axis_size("lat") - 1) & (odd == 0), 1.0, 0.0)
    oks, seconds = [], []
    for p, (n, pad, other) in zip(pieces, metas):
        place = lax.broadcasted_iota(jnp.int32, (p.shape[1], pair), 0)
        oks.append(jnp.where(lax.rem(place, pad) < n, 1.0, 0.0))
        seconds.append(jnp.full((p.shape[1], pair), packed if other else 0.0, F32))
    valid_col = jnp.concatenate(oks, axis=0)
    second = jnp.concatenate(seconds, axis=0)
    x = jnp.concatenate([p[0] for p in pieces], axis=0).astype(F32)
    mean = jnp.mean(x, axis=1, keepdims=True)
    cen = x - mean
    rstd = lax.rsqrt(jnp.mean(cen * cen, axis=1, keepdims=True) + EPSILON)
    gain = gain_ref[...][None]
    nl[...] = (cen * rstd * gain).astype(BF)
    qb = blocks_of(cells, cells)

    def one_pair(j, _):
        cols = pl.ds(pl.multiple_of(j * pair, pair), pair)
        colk = pl.ds(pl.multiple_of(width + j * pair, pair), pair)
        colv = pl.ds(pl.multiple_of(2 * width + j * pair, pair), pair)
        q_s[...] = (mm(nl[...], wqkv_ref[:, cols]) * qscale).astype(BF)
        k_s[...] = mm(nl[...], wqkv_ref[:, colk]).astype(BF)
        v_s[...] = mm(nl[...], wqkv_ref[:, colv]).astype(BF)
        b_s[...] = mm_t(c_ref[...], wproj_ref[cols, :]).astype(BF)
        kT[...] = k_s[...].T
        vT[...] = v_s[...].T
        bT[...] = b_s[...].T
        lane = lax.broadcasted_iota(jnp.int32, (cells, pair), 1)
        row = lax.broadcasted_iota(jnp.int32, (pair, cells), 0)
        outs = []
        for h in range(2):
            own = (lane >= head) if h else (lane < head)
            own_r = (row >= head) if h else (row < head)
            aug = 0 if h else head
            seen = jnp.where(lane == aug, valid_col * (1.0 - second), valid_col * second)
            two = (lane == aug) | (lane == aug + 1)
            bias = jnp.where(two, (seen - 1.0) * 30000.0, 0.0).astype(BF)
            group = jnp.where(lane == aug, 1.0 - second, second)
            kk = jnp.where(own, k_s[...], bias)
            qq = jnp.where(own, q_s[...], jnp.where(two, group, 0.0).astype(BF))
            vv = jnp.where(own, v_s[...], jnp.where(two, 1.0, 0.0).astype(BF))
            vvT = jnp.where(own_r, vT[...], jnp.where(row == aug, 1.0, 0.0).astype(BF))
            for at, n in qb:
                s = mm_t(kk, qq[at:at + n])
                e = jnp.exp2(s).astype(BF)
                oT = mm(vvT, e)
                total = oT[aug:aug + 1]
                inv = 1.0 / total
                aT = oT * inv
                attT[pl.ds(pl.multiple_of(j * pair + h * head, head), head), at:at + n] = aT[h * head:(h + 1) * head].astype(BF)
                bTn = bT[:, at:at + n].astype(F32)
                ownn = own_r[:, :n]
                rown = row[:, :n]
                rt = jnp.sum(jnp.where(ownn, bTn * aT, 0.0), axis=0, keepdims=True)
                hi = rt.astype(BF).astype(F32)
                lo = rt - hi
                baug = jnp.where(ownn, bTn, jnp.where(rown == aug, -hi, jnp.where(rown == aug + 1, -lo, 0.0))).astype(BF)
                p = e * inv.astype(BF)
                p_s[h, :, at:at + n] = p
                dp = mm(vv, baug).astype(BF)
                ds_s[h, :, at:at + n] = p * dp
            dv = mm(p_s[h], b_s[...])
            dk = mm(ds_s[h], q_s[...]) * LN2
            dqT = mm(kT[...], ds_s[h]) * (head ** -0.5)
            outs.append((dqT, dk, dv))
        dqT = jnp.where(row < head, outs[0][0], outs[1][0]).astype(BF)
        dqkv[:, cols] = dqT.T
        dqkv[:, colk] = jnp.where(lane < head, outs[0][1], outs[1][1]).astype(BF)
        dqkv[:, colv] = jnp.where(lane < head, outs[0][2], outs[1][2]).astype(BF)
        return 0

    lax.fori_loop(0, pairs, one_pair, 0)
    gp = mm(attT[...], c_ref[...])
    gq = mm(nl[...].T, dqkv[...])
    if split[0]:
        gq = gq + prev[0][...]
        gp = gp + prev[1][...]
    if split[1] is None:
        gq_ref[...] = gq
        gp_ref[...] = gp
    else:
        joined = refs[13]
        parts = split[1]
        gqT, gpT = gq.T, gp.T
        dq_rows, dp_rows = gqT.shape[0] // parts, gpT.shape[0] // parts
        for i in range(parts):
            joined[i, :dq_rows] = gqT[i * dq_rows:(i + 1) * dq_rows]
            joined[i, dq_rows:] = gpT[i * dp_rows:(i + 1) * dp_rows]
        me = odd
        for i in range(parts // 2):
            gq_ref[i] = joined[2 * i + me]
            gp_ref[i] = joined[2 * i + 1 - me].astype(BF)
    dn = mm_t(dqkv[...], wqkv_ref[...]) * gain
    normed = cen * rstd
    d = rstd * (dn - jnp.mean(dn, axis=1, keepdims=True) - normed * jnp.mean(dn * normed, axis=1, keepdims=True))
    d = d.astype(BF)
    for ref, at in zip(d_refs, starts):
        ref[...] = d[at:at + ref.shape[0]]


def window_call(pieces, metas, gain, wqkv, wproj, prev, parts):
    width = wproj.shape[0]
    head = width // HEADS
    pair = 2 * head
    sizes = [p.shape[1] for p in pieces]
    cells = sum(sizes)
    deep = 4 * width // parts if parts else 0
    if parts is None:
        sums = (jax.ShapeDtypeStruct((width, 3 * width), F32), jax.ShapeDtypeStruct((width, width), F32))
    else:
        sums = (jax.ShapeDtypeStruct((parts // 2, deep, width), F32),
                jax.ShapeDtypeStruct((parts // 2, deep, width), BF))
    scratch = ([pltpu.VMEM((cells, width), BF)] * 2
               + [pltpu.VMEM((cells, pair), BF)] * 4
               + [pltpu.VMEM((pair, cells), BF)] * 3
               + [pltpu.VMEM((2, cells, cells), BF)] * 2
               + [pltpu.VMEM((cells, 3 * width), BF), pltpu.VMEM((width, cells), BF)])
    if parts is not None:
        scratch.append(pltpu.VMEM((parts, deep, width), F32))
    vmem = pl.BlockSpec(memory_space=pltpu.VMEM)
    args = list(pieces) + [gain, wqkv, wproj] + (list(prev) if prev else [])
    outs = pl.pallas_call(
        functools.partial(window_kernel, head, metas, (prev is not None, parts)),
        out_shape=tuple(jax.ShapeDtypeStruct((n, width), BF) for n in sizes) + sums,
        in_specs=[vmem] * len(args),
        out_specs=[vmem] * (len(sizes) + 2),
        scratch_shapes=scratch,
        cost_estimate=pl.CostEstimate(
            flops=24 * cells * width * width + 12 * cells * cells * width,
            bytes_accessed=8 * 2**20,
            transcendentals=HEADS * cells * cells,
        ),
        compiler_params=pltpu.CompilerParams(vmem_limit_bytes=60 * 2**20),
    )(*args)
    return outs[:len(sizes)], outs[-2:]


def permuted(value, axes, target):
    sizes = [lax.axis_size(a) for a in axes]
    pairs = []
    for source in range(math.prod(sizes)):
        at, rest = [], source
        for size in reversed(sizes):
            at.append(rest % size)
            rest //= size
        goal = target(*reversed(at))
        if goal is None:
            continue
        flat = 0
        for size, place in zip(sizes, goal):
            flat = flat * size + place
        pairs.append((source, flat))
    return lax.ppermute(value, tuple(axes), pairs)


def shared(value, back=False, east=0):
    lats, lons = lax.axis_size("lat"), lax.axis_size("lon")
    pairs = []
    for i in range(lats):
        for j in range(lons):
            if j % 2 == 0:
                goal = (i - 1, j) if i > 0 else None
            else:
                goal = (i + 1, j) if i < lats - 1 else (i, j - 1)
            if goal is not None:
                pair = (i * lons + j, goal[0] * lons + goal[1])
                home = i * lons + (j + east) % lons
                pairs.append((pair[1], home) if back else pair)
    return lax.ppermute(value, ("lat", "lon"), pairs)


def along_lon(value, step):
    count = lax.axis_size("lon")
    return lax.ppermute(value, "lon", [(j, (j + step) % count) for j in range(count)])


def cut_kernel(specs, half, hid_ref, cot_ref, *outs):
    odd = lax.rem(lax.axis_index("lon"), 2)
    top = lax.axis_index("lat") == 0
    end = hid_ref.shape[1] - half
    starts = {"own": (1 - odd) * end, "sent": odd * end}
    zeroed = {"own": top & (odd == 1), "peer": top & (odd == 0)}
    for out, (rows, cols, n, pad, clear) in zip(outs, specs):
        at = starts.get(rows, rows)
        for k, ref in enumerate((hid_ref, cot_ref)):
            for b in range(hid_ref.shape[0]):
                cut = ref[b, pl.ds(at, half)].astype(F32)[:, cols:cols + n]
                if clear:
                    cut = jnp.where(zeroed[clear], 0.0, cut)
                filler = jnp.zeros((half, pad - n, cut.shape[2]), F32)
                out[k, b] = jnp.concatenate([cut, filler], axis=1).astype(BF)


def cut_call(hid, cot, specs, half):
    samples, _, _, width = hid.shape
    vmem = pl.BlockSpec(memory_space=pltpu.VMEM)
    outs = pl.pallas_call(
        functools.partial(cut_kernel, specs, half),
        out_shape=tuple(
            jax.ShapeDtypeStruct((2, samples, half, pad, width), BF) for _, _, _, pad, _ in specs
        ),
        in_specs=[vmem] * 2,
        out_specs=tuple([vmem] * len(specs)),
        cost_estimate=pl.CostEstimate(flops=0, bytes_accessed=4 * hid.size * 2, transcendentals=0),
        compiler_params=pltpu.CompilerParams(vmem_limit_bytes=40 * 2**20),
    )(hid, cot)
    return list(outs)


def scatter_direct(value, axis, dim):
    count = lax.axis_size(axis)
    me = lax.axis_index(axis)
    share = value.shape[dim] // count
    total = lax.dynamic_slice_in_dim(value, me * share, share, dim).astype(F32)
    for step in range(1, count):
        goal = (me + step) % count
        part = lax.dynamic_slice_in_dim(value, goal * share, share, dim).astype(BF)
        got = permuted(part, (axis,), lambda i, s=step: ((i + s) % count,))
        total = total + got.astype(F32)
    return total


def scatter_bit(value, axis, bit, dim):
    me = (lax.axis_index(axis) // bit) % 2
    mine = lax.dynamic_index_in_dim(value, me, dim, keepdims=False).astype(F32)
    other = lax.dynamic_index_in_dim(value, 1 - me, dim, keepdims=False).astype(BF)
    got = permuted(other, (axis,), lambda i: (i ^ bit,))
    return mine + got.astype(F32)


def reduce_weights(keep, send, lons):
    half, deep, width = keep.shape
    got = permuted(send, ("lon",), lambda i: (i ^ 1,))
    lats = lax.axis_size("lat")
    total = (keep + got.astype(F32)).reshape(lats, lons // 2, deep, width)
    bit, left = 2, lons // 2
    while left > 1:
        total = scatter_bit(total.reshape(lats, left // 2, 2, deep, width), "lon", bit, 2)
        left //= 2
        bit *= 2
    total = scatter_direct(total.reshape(lats, deep, width), "dp", 2)
    return scatter_direct(total, "lat", 0)[0]


def per_device(hidden_in, grad_out, norm_gain, w_qkv, w_proj):
    samples, lat_rows, lon_cols, width = hidden_in.shape
    half = WIN // 2
    nr, nc = lat_rows // WIN, lon_cols // WIN
    short = half + (-half) % 16
    wide = WIN + (-WIN) % 16
    lons = lax.axis_size("lon")
    parts = lax.axis_size("lat") * lons
    if lons & (lons - 1) or lons < 2:
        raise ValueError("lon size")

    odd = lax.axis_index("lon") % 2
    inner = [wc * WIN + SHIFT for wc in range(nc - 1)]
    edge = (nc - 1) * WIN + SHIFT
    sent = cut_call(hidden_in, grad_out, [("sent", at, WIN, wide, "") for at in inner], half) if inner else []
    hid, cot, sent = lax.optimization_barrier((hidden_in, grad_out, sent))
    inner_in = [shared(p) for p in sent]
    specs = [("sent", 0, half, short, "peer"), ("own", 0, half, short, "")]
    specs += [("own", edge, half, short, "own"), ("sent", edge, half, short, "")]
    specs += [("own", at, WIN, wide, "own") for at in inner]
    fixed = [(2 * wr + 1 + i) * half for wr in range(nr - 1) for i in range(2)]
    specs += [(r, at, WIN, wide, "") for at in inner for r in fixed]
    specs += [(r, edge, half, short, "") for r in fixed] + [(r, 0, half, short, "") for r in fixed]
    cuts = cut_call(hid, cot, specs, half)
    own_side, side_sent = along_lon(cuts[0], -1), along_lon(cuts[1], -1)
    own_edge, edge_sent = cuts[2:4]
    own_inner, rest = cuts[4:4 + len(inner)], cuts[4 + len(inner):]
    whole_inner = [[rest.pop(0) for _ in fixed] for _ in inner]
    whole_edge = [rest.pop(0) for _ in fixed]
    whole_side = [along_lon(rest.pop(0), -1) for _ in fixed]
    if inner_in:
        edge_sent, side_sent, inner_in = lax.optimization_barrier((edge_sent, side_sent, inner_in))
    edge_in, corner_in = shared(edge_sent), shared(side_sent)

    order = [(b, wr, wc) for b in range(samples) for wc in range(nc) for wr in range(nr)]
    sums = None
    out = {}
    for step, (b, wr, wc) in enumerate(order):
        if wr < nr - 1 and wc < nc - 1:
            cells = whole_inner[wc][2 * wr:2 * wr + 2]
            metas = ((WIN, wide, False),) * 2
        elif wr < nr - 1:
            cells = [f[2 * wr + i] for i in range(2) for f in (whole_edge, whole_side)]
            metas = ((half, short, False),) * 4
        elif wc < nc - 1:
            cells = [own_inner[wc], inner_in[wc]]
            metas = ((WIN, wide, False), (WIN, wide, True))
        else:
            cells = [own_edge, own_side, edge_in, corner_in]
            metas = ((half, short, False),) * 2 + ((half, short, True),) * 2
        cells = [p[:, b].reshape(2, -1, width) for p in cells]
        done, sums = window_call(
            cells, metas, norm_gain, w_qkv, w_proj, sums, parts if step == len(order) - 1 else None
        )
        out[b, wr, wc] = [d.reshape(half, pad, width) for d, (n, pad, _) in zip(done, metas)]

    rows_out = []
    for b in range(samples):
        def stacked(own, back, between, upper):
            above = jnp.where(upper, own, back)
            below = jnp.where(upper, back, own)
            return jnp.concatenate([above] + between + [below], axis=0)

        columns = []
        for wc in range(nc - 1):
            own, other = out[b, nr - 1, wc]
            between = [out[b, wr, wc][i] for wr in range(nr - 1) for i in range(2)]
            columns.append(stacked(own, shared(other, back=True), between, odd == 1)[:, :WIN])
        own, own_lon, other, other_lon = out[b, nr - 1, nc - 1]
        between = [out[b, wr, nc - 1][i] for wr in range(nr - 1) for i in (0, 2)]
        columns.append(stacked(own, shared(other, back=True), between, odd == 1)[:, :half])
        between = [along_lon(out[b, wr, nc - 1][i], 1) for wr in range(nr - 1) for i in (1, 3)]
        near, far = along_lon(own_lon, 1), shared(other_lon, back=True, east=1)
        columns.insert(0, stacked(near, far, between, odd == 0)[:, :half])
        rows_out.append(jnp.concatenate(columns, axis=1))
    returned = jnp.stack(rows_out)
    grad_in = (grad_out.astype(F32) + returned.astype(F32)).astype(BF)
    total_cells = (
        lax.axis_size("dp") * samples * lat_rows * lax.axis_size("lat") * lon_cols * lons
    )
    factor = float(total_cells) ** (-0.5)
    total = reduce_weights(sums[0], sums[1], lons).T * factor
    cut = 3 * width // parts
    return (grad_in, total[:, :cut], total[:, cut:])


def solution(mesh):
    in_specs = (P("dp", "lat", "lon", None), P("dp", "lat", "lon", None), P(), P(), P())
    out_specs = (P("dp", "lat", "lon", None), P("dp", ("lat", "lon")), P("dp", ("lat", "lon")))
    return jax.shard_map(
        per_device, mesh=mesh, in_specs=in_specs, out_specs=out_specs, check_vma=False
    )
```

```python
import functools, math
import jax, jax.numpy as jnp
from jax import lax
from jax.experimental import pallas as pl
from jax.experimental.pallas import tpu as pltpu

from jax.sharding import PartitionSpec as P

HEADS = 6
WIN = 30
SHIFT = 15
EPSILON = 1e-05
BF = jnp.bfloat16
F32 = jnp.float32
LN2 = math.log(2.0)

def mm(a, b):
    return lax.dot_general(a, b, (((1,), (0,)), ((), ())), preferred_element_type=F32)

def mm_t(a, b):
    return lax.dot_general(a, b, (((1,), (1,)), ((), ())), preferred_element_type=F32)

def blocks_of(n, step):
    return [(at, min(step, n - at)) for at in range(0, n, step)]

def window_kernel(head, metas, split, *refs):
    count = len(metas)
    pieces, refs = refs[:count], refs[count:]
    gain_ref, wqkv_ref, wproj_ref = refs[:3]
    refs = refs[3:]
    if split[0]:
        prev, refs = refs[:2], refs[2:]
    d_refs, refs = refs[:count], refs[count:]
    (gq_ref, gp_ref), refs = refs[:2], refs[2:]
    c_ref, nl, q_s, k_s, v_s, b_s, kT, vT, bT, p_s, ds_s, dqkv, attT = refs[:13]
    cells, width = c_ref.shape
    pair = 2 * head
    pairs = width // pair
    qscale = head ** -0.5 / LN2
    at = 0
    starts = []
    for p in pieces:
        starts.append(at)
        c_ref[at:at + p.shape[1]] = p[1]
        at += p.shape[1]
    odd = lax.rem(lax.axis_index("lon"), 2)
    packed = jnp.where((lax.axis_index("lat") == lax.axis_size("lat") - 1) & (odd == 0), 1.0, 0.0)
    oks, seconds = [], []
    for p, (n, pad, other) in zip(pieces, metas):
        place = lax.broadcasted_iota(jnp.int32, (p.shape[1], pair), 0)
        oks.append(jnp.where(lax.rem(place, pad) < n, 1.0, 0.0))
        seconds.append(jnp.full((p.shape[1], pair), packed if other else 0.0, F32))
    valid_col = jnp.concatenate(oks, axis=0)
    second = jnp.concatenate(seconds, axis=0)
    x = jnp.concatenate([p[0] for p in pieces], axis=0).astype(F32)
    mean = jnp.mean(x, axis=1, keepdims=True)
    cen = x - mean
    rstd = lax.rsqrt(jnp.mean(cen * cen, axis=1, keepdims=True) + EPSILON)
    gain = gain_ref[...][None]
    nl[...] = (cen * rstd * gain).astype(BF)
    qb = blocks_of(cells, cells)

    def one_pair(j, _):
        cols = pl.ds(pl.multiple_of(j * pair, pair), pair)
        colk = pl.ds(pl.multiple_of(width + j * pair, pair), pair)
        colv = pl.ds(pl.multiple_of(2 * width + j * pair, pair), pair)
        q_s[...] = (mm(nl[...], wqkv_ref[:, cols]) * qscale).astype(BF)
        k_s[...] = mm(nl[...], wqkv_ref[:, colk]).astype(BF)
        v_s[...] = mm(nl[...], wqkv_ref[:, colv]).astype(BF)
        b_s[...] = mm_t(c_ref[...], wproj_ref[cols, :]).astype(BF)
        kT[...] = k_s[...].T
        vT[...] = v_s[...].T
        bT[...] = b_s[...].T
        lane = lax.broadcasted_iota(jnp.int32, (cells, pair), 1)
        row = lax.broadcasted_iota(jnp.int32, (pair, cells), 0)
        outs = []
        for h in range(2):
            own = (lane >= head) if h else (lane < head)
            own_r = (row >= head) if h else (row < head)
            aug = 0 if h else head
            seen = jnp.where(lane == aug, valid_col * (1.0 - second), valid_col * second)
            two = (lane == aug) | (lane == aug + 1)
            bias = jnp.where(two, (seen - 1.0) * 30000.0, 0.0).astype(BF)
            group = jnp.where(lane == aug, 1.0 - second, second)
            kk = jnp.where(own, k_s[...], bias)
            qq = jnp.where(own, q_s[...], jnp.where(two, group, 0.0).astype(BF))
            vv = jnp.where(own, v_s[...], jnp.where(two, 1.0, 0.0).astype(BF))
            vvT = jnp.where(own_r, vT[...], jnp.where(row == aug, 1.0, 0.0).astype(BF))
            for at, n in qb:
                s = mm_t(kk, qq[at:at + n])
                e = jnp.exp2(s).astype(BF)
                oT = mm(vvT, e)
                total = oT[aug:aug + 1]
                inv = 1.0 / total
                aT = oT * inv
                attT[pl.ds(pl.multiple_of(j * pair + h * head, head), head), at:at + n] = aT[h * head:(h + 1) * head].astype(BF)
                bTn = bT[:, at:at + n].astype(F32)
                ownn = own_r[:, :n]
                rown = row[:, :n]
                rt = jnp.sum(jnp.where(ownn, bTn * aT, 0.0), axis=0, keepdims=True)
                hi = rt.astype(BF).astype(F32)
                lo = rt - hi
                baug = jnp.where(ownn, bTn, jnp.where(rown == aug, -hi, jnp.where(rown == aug + 1, -lo, 0.0))).astype(BF)
                p = e * inv.astype(BF)
                p_s[h, :, at:at + n] = p
                dp = mm(vv, baug).astype(BF)
                ds_s[h, :, at:at + n] = p * dp
            dv = mm(p_s[h], b_s[...])
            dk = mm(ds_s[h], q_s[...]) * LN2
            dqT = mm(kT[...], ds_s[h]) * (head ** -0.5)
            outs.append((dqT, dk, dv))
        dqT = jnp.where(row < head, outs[0][0], outs[1][0]).astype(BF)
        dqkv[:, cols] = dqT.T
        dqkv[:, colk] = jnp.where(lane < head, outs[0][1], outs[1][1]).astype(BF)
        dqkv[:, colv] = jnp.where(lane < head, outs[0][2], outs[1][2]).astype(BF)
        return 0

    lax.fori_loop(0, pairs, one_pair, 0)
    gp = mm(attT[...], c_ref[...])
    gq = mm(nl[...].T, dqkv[...])
    if split[0]:
        gq = gq + prev[0][...]
        gp = gp + prev[1][...]
    if split[1] is None:
        gq_ref[...] = gq
        gp_ref[...] = gp
    else:
        joined = refs[13]
        parts = split[1]
        gqT, gpT = gq.T, gp.T
        dq_rows, dp_rows = gqT.shape[0] // parts, gpT.shape[0] // parts
        for i in range(parts):
            joined[i, :dq_rows] = gqT[i * dq_rows:(i + 1) * dq_rows]
            joined[i, dq_rows:] = gpT[i * dp_rows:(i + 1) * dp_rows]
        me = odd
        for i in range(parts // 2):
            gq_ref[i] = joined[2 * i + me]
            gp_ref[i] = joined[2 * i + 1 - me].astype(BF)
    dn = mm_t(dqkv[...], wqkv_ref[...]) * gain
    normed = cen * rstd
    d = rstd * (dn - jnp.mean(dn, axis=1, keepdims=True) - normed * jnp.mean(dn * normed, axis=1, keepdims=True))
    d = d.astype(BF)
    for ref, at in zip(d_refs, starts):
        ref[...] = d[at:at + ref.shape[0]]


def window_call(pieces, metas, gain, wqkv, wproj, prev, parts):
    width = wproj.shape[0]
    head = width // HEADS
    pair = 2 * head
    sizes = [p.shape[1] for p in pieces]
    cells = sum(sizes)
    deep = 4 * width // parts if parts else 0
    if parts is None:
        sums = (jax.ShapeDtypeStruct((width, 3 * width), F32), jax.ShapeDtypeStruct((width, width), F32))
    else:
        sums = (jax.ShapeDtypeStruct((parts // 2, deep, width), F32),
                jax.ShapeDtypeStruct((parts // 2, deep, width), BF))
    scratch = ([pltpu.VMEM((cells, width), BF)] * 2
               + [pltpu.VMEM((cells, pair), BF)] * 4
               + [pltpu.VMEM((pair, cells), BF)] * 3
               + [pltpu.VMEM((2, cells, cells), BF)] * 2
               + [pltpu.VMEM((cells, 3 * width), BF), pltpu.VMEM((width, cells), BF)])
    if parts is not None:
        scratch.append(pltpu.VMEM((parts, deep, width), F32))
    vmem = pl.BlockSpec(memory_space=pltpu.VMEM)
    args = list(pieces) + [gain, wqkv, wproj] + (list(prev) if prev else [])
    outs = pl.pallas_call(
        functools.partial(window_kernel, head, metas, (prev is not None, parts)),
        out_shape=tuple(jax.ShapeDtypeStruct((n, width), BF) for n in sizes) + sums,
        in_specs=[vmem] * len(args),
        out_specs=[vmem] * (len(sizes) + 2),
        scratch_shapes=scratch,
        cost_estimate=pl.CostEstimate(
            flops=24 * cells * width * width + 12 * cells * cells * width,
            bytes_accessed=8 * 2**20,
            transcendentals=HEADS * cells * cells,
        ),
        compiler_params=pltpu.CompilerParams(vmem_limit_bytes=32 * 2**20),
    )(*args)
    return outs[:len(sizes)], outs[-2:]


def permuted(value, axes, target):
    sizes = [lax.axis_size(a) for a in axes]
    pairs = []
    for source in range(math.prod(sizes)):
        at, rest = [], source
        for size in reversed(sizes):
            at.append(rest % size)
            rest //= size
        goal = target(*reversed(at))
        if goal is None:
            continue
        flat = 0
        for size, place in zip(sizes, goal):
            flat = flat * size + place
        pairs.append((source, flat))
    return lax.ppermute(value, tuple(axes), pairs)


def shared(value, back=False, east=0):
    lats, lons = lax.axis_size("lat"), lax.axis_size("lon")
    pairs = []
    for i in range(lats):
        for j in range(lons):
            if j % 2 == 0:
                goal = (i - 1, j) if i > 0 else None
            else:
                goal = (i + 1, j) if i < lats - 1 else (i, j - 1)
            if goal is not None:
                pair = (i * lons + j, goal[0] * lons + goal[1])
                home = i * lons + (j + east) % lons
                pairs.append((pair[1], home) if back else (home, pair[1]))
    return lax.ppermute(value, ("lat", "lon"), pairs)


def along_lon(value, step):
    count = lax.axis_size("lon")
    return lax.ppermute(value, "lon", [(j, (j + step) % count) for j in range(count)])


def cut_kernel(specs, half, hid_ref, cot_ref, *outs):
    odd = lax.rem(lax.axis_index("lon"), 2)
    top = lax.axis_index("lat") == 0
    end = hid_ref.shape[1] - half
    starts = {"own": (1 - odd) * end, "sent": odd * end}
    zeroed = {"own": top & (odd == 1), "peer": top & (odd == 0)}
    for out, (rows, cols, n, pad, clear) in zip(outs, specs):
        at = starts.get(rows, rows)
        for k, ref in enumerate((hid_ref, cot_ref)):
            for b in range(hid_ref.shape[0]):
                cut = ref[b, pl.ds(at, half)].astype(F32)[:, cols:cols + n]
                if clear:
                    cut = jnp.where(zeroed[clear], 0.0, cut)
                filler = jnp.zeros((half, pad - n, cut.shape[2]), F32)
                out[k, b] = jnp.concatenate([cut, filler], axis=1).astype(BF)


def cut_call(hid, cot, specs, half):
    samples, _, _, width = hid.shape
    vmem = pl.BlockSpec(memory_space=pltpu.VMEM)
    outs = pl.pallas_call(
        functools.partial(cut_kernel, specs, half),
        out_shape=tuple(
            jax.ShapeDtypeStruct((2, samples, half, pad, width), BF) for _, _, _, pad, _ in specs
        ),
        in_specs=[vmem] * 2,
        out_specs=tuple([vmem] * len(specs)),
        cost_estimate=pl.CostEstimate(flops=0, bytes_accessed=4 * hid.size * 2, transcendentals=0),
        compiler_params=pltpu.CompilerParams(vmem_limit_bytes=40 * 2**20),
    )(hid, cot)
    return list(outs)


def scatter_direct(value, axis, dim):
    count = lax.axis_size(axis)
    me = lax.axis_index(axis)
    share = value.shape[dim] // count
    total = lax.dynamic_slice_in_dim(value, me * share, share, dim).astype(F32)
    for step in range(1, count):
        goal = (me + step) % count
        part = lax.dynamic_slice_in_dim(value, goal * share, share, dim).astype(BF)
        got = permuted(part, (axis,), lambda i, s=step: ((i + s) % count,))
        total = total + got.astype(F32)
    return total


def scatter_bit(value, axis, bit, dim):
    me = (lax.axis_index(axis) // bit) % 2
    mine = lax.dynamic_index_in_dim(value, me, dim, keepdims=False).astype(F32)
    other = lax.dynamic_index_in_dim(value, 1 - me, dim, keepdims=False).astype(BF)
    got = permuted(other, (axis,), lambda i: (i ^ bit,))
    return mine + got.astype(F32)


def reduce_weights(keep, send, lons, returns):
    half, deep, width = keep.shape
    lats = lax.axis_size("lat")
    moved, waiting = [], list(returns)

    def release(value, count=1):
        for _ in range(min(count, len(waiting))):
            held, move = waiting.pop(0)
            value, held = lax.optimization_barrier((value, held))
            moved.append(move(held))
        return value

    got = permuted(send, ("lon",), lambda i: (i ^ 1,))
    moved.append(waiting[0][1](waiting.pop(0)[0]))
    total = release((keep + got.astype(F32)).reshape(lats, lons // 2, deep, width))
    bit, left = 2, lons // 2
    while left > 1:
        total = scatter_bit(total.reshape(lats, left // 2, 2, deep, width), "lon", bit, 2)
        left //= 2
        bit *= 2
    total = release(total.reshape(lats, deep, width), len(waiting))
    total = scatter_direct(total, "dp", 2)
    return scatter_direct(total, "lat", 0)[0], moved


def per_device(hidden_in, grad_out, norm_gain, w_qkv, w_proj):
    samples, lat_rows, lon_cols, width = hidden_in.shape
    half = WIN // 2
    nr, nc = lat_rows // WIN, lon_cols // WIN
    short = half + (-half) % 16
    wide = WIN + (-WIN) % 16
    lons = lax.axis_size("lon")
    parts = lax.axis_size("lat") * lons
    if lons & (lons - 1) or lons < 2:
        raise ValueError("lon size")

    odd = lax.axis_index("lon") % 2
    inner = [wc * WIN + SHIFT for wc in range(nc - 1)]
    edge = (nc - 1) * WIN + SHIFT
    sent = cut_call(hidden_in, grad_out, [("sent", at, WIN, wide, "") for at in inner], half) if inner else []
    hid, cot, sent = lax.optimization_barrier((hidden_in, grad_out, sent))
    inner_in = [shared(p) for p in sent]
    specs = [("sent", 0, half, short, "peer"), ("own", 0, half, short, "")]
    specs += [("own", edge, half, short, "own"), ("sent", edge, half, short, "")]
    specs += [("own", at, WIN, wide, "own") for at in inner]
    fixed = [(2 * wr + 1 + i) * half for wr in range(nr - 1) for i in range(2)]
    specs += [(r, at, WIN, wide, "") for at in inner for r in fixed]
    specs += [(r, edge, half, short, "") for r in fixed] + [(r, 0, half, short, "") for r in fixed]
    cuts = cut_call(hid, cot, specs, half)
    side_sent, corner_sent, own_edge, edge_sent = cuts[:4]
    own_inner, rest = cuts[4:4 + len(inner)], cuts[4 + len(inner):]
    whole_inner = [[rest.pop(0) for _ in fixed] for _ in inner]
    whole_edge = [rest.pop(0) for _ in fixed]
    whole_side = [along_lon(rest.pop(0), -1) for _ in fixed]
    if inner_in:
        edge_sent, side_sent, corner_sent, inner_in = lax.optimization_barrier(
            (edge_sent, side_sent, corner_sent, inner_in)
        )
    own_side, edge_in, corner_in = along_lon(side_sent, -1), shared(edge_sent), shared(corner_sent, east=1)

    order = [(b, wr, wc) for b in range(samples) for wc in range(nc) for wr in range(nr)]
    sums = None
    out = {}
    for step, (b, wr, wc) in enumerate(order):
        if wr < nr - 1 and wc < nc - 1:
            cells = whole_inner[wc][2 * wr:2 * wr + 2]
            metas = ((WIN, wide, False),) * 2
        elif wr < nr - 1:
            cells = [f[2 * wr + i] for i in range(2) for f in (whole_edge, whole_side)]
            metas = ((half, short, False),) * 4
        elif wc < nc - 1:
            cells = [own_inner[wc], inner_in[wc]]
            metas = ((WIN, wide, False), (WIN, wide, True))
        else:
            cells = [own_edge, own_side, edge_in, corner_in]
            metas = ((half, short, False),) * 2 + ((half, short, True),) * 2
        cells = [p[:, b].reshape(2, -1, width) for p in cells]
        done, sums = window_call(
            cells, metas, norm_gain, w_qkv, w_proj, sums, parts if step == len(order) - 1 else None
        )
        out[b, wr, wc] = [d.reshape(half, pad, width) for d, (n, pad, _) in zip(done, metas)]

    late = []
    for b in range(samples):
        own, own_lon, other, other_lon = out[b, nr - 1, nc - 1]
        late.append((other, lambda v: shared(v, back=True)))
        late.append((other_lon, lambda v: shared(v, back=True, east=1)))
        late.append((own_lon, lambda v: along_lon(v, 1)))
    total, moved = reduce_weights(sums[0], sums[1], lons, late)

    rows_out = []
    for b in range(samples):
        def stacked(own, back, between, upper):
            above = jnp.where(upper, own, back)
            below = jnp.where(upper, back, own)
            return jnp.concatenate([above] + between + [below], axis=0)

        columns = []
        for wc in range(nc - 1):
            own, other = out[b, nr - 1, wc]
            between = [out[b, wr, wc][i] for wr in range(nr - 1) for i in range(2)]
            columns.append(stacked(own, shared(other, back=True), between, odd == 1)[:, :WIN])
        own = out[b, nr - 1, nc - 1][0]
        back, far, near = moved[3 * b:3 * b + 3]
        between = [out[b, wr, nc - 1][i] for wr in range(nr - 1) for i in (0, 2)]
        columns.append(stacked(own, back, between, odd == 1)[:, :half])
        between = [along_lon(out[b, wr, nc - 1][i], 1) for wr in range(nr - 1) for i in (1, 3)]
        columns.insert(0, stacked(near, far, between, odd == 0)[:, :half])
        rows_out.append(jnp.concatenate(columns, axis=1))
    returned = jnp.stack(rows_out)
    grad_in = (grad_out.astype(F32) + returned.astype(F32)).astype(BF)
    total_cells = (
        lax.axis_size("dp") * samples * lat_rows * lax.axis_size("lat") * lon_cols * lons
    )
    factor = float(total_cells) ** (-0.5)
    total = total.T * factor
    cut = 3 * width // parts
    return (grad_in, total[:, :cut], total[:, cut:])


def solution(mesh):
    in_specs = (P("dp", "lat", "lon", None), P("dp", "lat", "lon", None), P(), P(), P())
    out_specs = (P("dp", "lat", "lon", None), P("dp", ("lat", "lon")), P("dp", ("lat", "lon")))
    return jax.shard_map(
        per_device, mesh=mesh, in_specs=in_specs, out_specs=out_specs, check_vma=False
    )
```

```python
import functools, math
import jax, jax.numpy as jnp
from jax import lax
from jax.experimental import pallas as pl
from jax.experimental.pallas import tpu as pltpu

from jax.sharding import PartitionSpec as P

HEADS = 6
WIN = 30
SHIFT = 15
EPSILON = 1e-05
BF = jnp.bfloat16
F32 = jnp.float32
LN2 = math.log(2.0)

def mm(a, b):
    return lax.dot_general(a, b, (((1,), (0,)), ((), ())), preferred_element_type=F32)

def mm_t(a, b):
    return lax.dot_general(a, b, (((1,), (1,)), ((), ())), preferred_element_type=F32)

def blocks_of(n, step):
    return [(at, min(step, n - at)) for at in range(0, n, step)]

def window_kernel(head, metas, split, *refs):
    count = len(metas)
    pieces, refs = refs[:count], refs[count:]
    gain_ref, wqkv_ref, wproj_ref = refs[:3]
    refs = refs[3:]
    if split[0]:
        prev, refs = refs[:2], refs[2:]
    d_refs, refs = refs[:count], refs[count:]
    (gq_ref, gp_ref), refs = refs[:2], refs[2:]
    c_ref, nl, q_s, k_s, v_s, b_s, kT, vT, bT, p_s, ds_s, dqkv, attT = refs[:13]
    cells, width = c_ref.shape
    pair = 2 * head
    pairs = width // pair
    qscale = head ** -0.5 / LN2
    at = 0
    starts = []
    for p in pieces:
        starts.append(at)
        c_ref[at:at + p.shape[1]] = p[1]
        at += p.shape[1]
    odd = lax.rem(lax.axis_index("lon"), 2)
    packed = jnp.where((lax.axis_index("lat") == lax.axis_size("lat") - 1) & (odd == 0), 1.0, 0.0)
    oks, seconds = [], []
    for p, (n, pad, other) in zip(pieces, metas):
        place = lax.broadcasted_iota(jnp.int32, (p.shape[1], pair), 0)
        oks.append(jnp.where(lax.rem(place, pad) < n, 1.0, 0.0))
        seconds.append(jnp.full((p.shape[1], pair), packed if other else 0.0, F32))
    valid_col = jnp.concatenate(oks, axis=0)
    second = jnp.concatenate(seconds, axis=0)
    x = jnp.concatenate([p[0] for p in pieces], axis=0).astype(F32)
    mean = jnp.mean(x, axis=1, keepdims=True)
    cen = x - mean
    rstd = lax.rsqrt(jnp.mean(cen * cen, axis=1, keepdims=True) + EPSILON)
    gain = gain_ref[...][None]
    nl[...] = (cen * rstd * gain).astype(BF)
    qb = blocks_of(cells, cells)

    def one_pair(j, _):
        cols = pl.ds(pl.multiple_of(j * pair, pair), pair)
        colk = pl.ds(pl.multiple_of(width + j * pair, pair), pair)
        colv = pl.ds(pl.multiple_of(2 * width + j * pair, pair), pair)
        q_s[...] = (mm(nl[...], wqkv_ref[:, cols]) * qscale).astype(BF)
        k_s[...] = mm(nl[...], wqkv_ref[:, colk]).astype(BF)
        v_s[...] = mm(nl[...], wqkv_ref[:, colv]).astype(BF)
        b_s[...] = mm_t(c_ref[...], wproj_ref[cols, :]).astype(BF)
        kT[...] = k_s[...].T
        vT[...] = v_s[...].T
        bT[...] = b_s[...].T
        lane = lax.broadcasted_iota(jnp.int32, (cells, pair), 1)
        row = lax.broadcasted_iota(jnp.int32, (pair, cells), 0)
        outs = []
        for h in range(2):
            own = (lane >= head) if h else (lane < head)
            own_r = (row >= head) if h else (row < head)
            aug = 0 if h else head
            seen = jnp.where(lane == aug, valid_col * (1.0 - second), valid_col * second)
            two = (lane == aug) | (lane == aug + 1)
            bias = jnp.where(two, (seen - 1.0) * 30000.0, 0.0).astype(BF)
            group = jnp.where(lane == aug, 1.0 - second, second)
            kk = jnp.where(own, k_s[...], bias)
            qq = jnp.where(own, q_s[...], jnp.where(two, group, 0.0).astype(BF))
            vv = jnp.where(own, v_s[...], jnp.where(two, 1.0, 0.0).astype(BF))
            vvT = jnp.where(own_r, vT[...], jnp.where(row == aug, 1.0, 0.0).astype(BF))
            for at, n in qb:
                s = mm_t(kk, qq[at:at + n])
                e = jnp.exp2(s).astype(BF)
                oT = mm(vvT, e)
                total = oT[aug:aug + 1]
                inv = 1.0 / total
                aT = oT * inv
                attT[pl.ds(pl.multiple_of(j * pair + h * head, head), head), at:at + n] = aT[h * head:(h + 1) * head].astype(BF)
                bTn = bT[:, at:at + n].astype(F32)
                ownn = own_r[:, :n]
                rown = row[:, :n]
                rt = jnp.sum(jnp.where(ownn, bTn * aT, 0.0), axis=0, keepdims=True)
                hi = rt.astype(BF).astype(F32)
                lo = rt - hi
                baug = jnp.where(ownn, bTn, jnp.where(rown == aug, -hi, jnp.where(rown == aug + 1, -lo, 0.0))).astype(BF)
                p = e * inv.astype(BF)
                p_s[h, :, at:at + n] = p
                dp = mm(vv, baug).astype(BF)
                ds_s[h, :, at:at + n] = p * dp
            dv = mm(p_s[h], b_s[...])
            dk = mm(ds_s[h], q_s[...]) * LN2
            dqT = mm(kT[...], ds_s[h]) * (head ** -0.5)
            outs.append((dqT, dk, dv))
        dqT = jnp.where(row < head, outs[0][0], outs[1][0]).astype(BF)
        dqkv[:, cols] = dqT.T
        dqkv[:, colk] = jnp.where(lane < head, outs[0][1], outs[1][1]).astype(BF)
        dqkv[:, colv] = jnp.where(lane < head, outs[0][2], outs[1][2]).astype(BF)
        return 0

    lax.fori_loop(0, pairs, one_pair, 0)
    gp = mm(attT[...], c_ref[...])
    gq = mm(nl[...].T, dqkv[...])
    if split[0]:
        gq = gq + prev[0][...]
        gp = gp + prev[1][...]
    if split[1] is None:
        gq_ref[...] = gq
        gp_ref[...] = gp
    else:
        joined = refs[13]
        parts = split[1]
        gqT, gpT = gq.T, gp.T
        dq_rows, dp_rows = gqT.shape[0] // parts, gpT.shape[0] // parts
        for i in range(parts):
            joined[i, :dq_rows] = gqT[i * dq_rows:(i + 1) * dq_rows]
            joined[i, dq_rows:] = gpT[i * dp_rows:(i + 1) * dp_rows]
        me = odd
        for i in range(parts // 2):
            gq_ref[i] = joined[2 * i + me]
            gp_ref[i] = joined[2 * i + 1 - me].astype(BF)
    dn = mm_t(dqkv[...], wqkv_ref[...]) * gain
    normed = cen * rstd
    d = rstd * (dn - jnp.mean(dn, axis=1, keepdims=True) - normed * jnp.mean(dn * normed, axis=1, keepdims=True))
    d = d.astype(BF)
    for ref, at in zip(d_refs, starts):
        ref[...] = d[at:at + ref.shape[0]]


def window_call(pieces, metas, gain, wqkv, wproj, prev, parts):
    width = wproj.shape[0]
    head = width // HEADS
    pair = 2 * head
    sizes = [p.shape[1] for p in pieces]
    cells = sum(sizes)
    deep = 4 * width // parts if parts else 0
    if parts is None:
        sums = (jax.ShapeDtypeStruct((width, 3 * width), F32), jax.ShapeDtypeStruct((width, width), F32))
    else:
        sums = (jax.ShapeDtypeStruct((parts // 2, deep, width), F32),
                jax.ShapeDtypeStruct((parts // 2, deep, width), BF))
    scratch = ([pltpu.VMEM((cells, width), BF)] * 2
               + [pltpu.VMEM((cells, pair), BF)] * 4
               + [pltpu.VMEM((pair, cells), BF)] * 3
               + [pltpu.VMEM((2, cells, cells), BF)] * 2
               + [pltpu.VMEM((cells, 3 * width), BF), pltpu.VMEM((width, cells), BF)])
    if parts is not None:
        scratch.append(pltpu.VMEM((parts, deep, width), F32))
    vmem = pl.BlockSpec(memory_space=pltpu.VMEM)
    args = list(pieces) + [gain, wqkv, wproj] + (list(prev) if prev else [])
    outs = pl.pallas_call(
        functools.partial(window_kernel, head, metas, (prev is not None, parts)),
        out_shape=tuple(jax.ShapeDtypeStruct((n, width), BF) for n in sizes) + sums,
        in_specs=[vmem] * len(args),
        out_specs=[vmem] * (len(sizes) + 2),
        scratch_shapes=scratch,
        cost_estimate=pl.CostEstimate(
            flops=24 * cells * width * width + 12 * cells * cells * width,
            bytes_accessed=8 * 2**20,
            transcendentals=HEADS * cells * cells,
        ),
        compiler_params=pltpu.CompilerParams(vmem_limit_bytes=32 * 2**20),
    )(*args)
    return outs[:len(sizes)], outs[-2:]


def permuted(value, axes, target):
    sizes = [lax.axis_size(a) for a in axes]
    pairs = []
    for source in range(math.prod(sizes)):
        at, rest = [], source
        for size in reversed(sizes):
            at.append(rest % size)
            rest //= size
        goal = target(*reversed(at))
        if goal is None:
            continue
        flat = 0
        for size, place in zip(sizes, goal):
            flat = flat * size + place
        pairs.append((source, flat))
    return lax.ppermute(value, tuple(axes), pairs)


def shared(value, back=False, east=0):
    lats, lons = lax.axis_size("lat"), lax.axis_size("lon")
    pairs = []
    for i in range(lats):
        for j in range(lons):
            if j % 2 == 0:
                goal = (i - 1, j) if i > 0 else None
            else:
                goal = (i + 1, j) if i < lats - 1 else (i, j - 1)
            if goal is not None:
                pair = (i * lons + j, goal[0] * lons + goal[1])
                home = i * lons + (j + east) % lons
                pairs.append((pair[1], home) if back else (home, pair[1]))
    return lax.ppermute(value, ("lat", "lon"), pairs)


def along_lon(value, step):
    count = lax.axis_size("lon")
    return lax.ppermute(value, "lon", [(j, (j + step) % count) for j in range(count)])


def cut_kernel(specs, half, hid_ref, cot_ref, *outs):
    odd = lax.rem(lax.axis_index("lon"), 2)
    top = lax.axis_index("lat") == 0
    end = hid_ref.shape[1] - half
    starts = {"own": (1 - odd) * end, "sent": odd * end}
    zeroed = {"own": top & (odd == 1), "peer": top & (odd == 0)}
    for out, (rows, cols, n, pad, clear) in zip(outs, specs):
        at = starts.get(rows, rows)
        for k, ref in enumerate((hid_ref, cot_ref)):
            for b in range(hid_ref.shape[0]):
                cut = ref[b, pl.ds(at, half)].astype(F32)[:, cols:cols + n]
                if clear:
                    cut = jnp.where(zeroed[clear], 0.0, cut)
                filler = jnp.zeros((half, pad - n, cut.shape[2]), F32)
                out[k, b] = jnp.concatenate([cut, filler], axis=1).astype(BF)


def cut_call(hid, cot, specs, half):
    samples, _, _, width = hid.shape
    vmem = pl.BlockSpec(memory_space=pltpu.VMEM)
    outs = pl.pallas_call(
        functools.partial(cut_kernel, specs, half),
        out_shape=tuple(
            jax.ShapeDtypeStruct((2, samples, half, pad, width), BF) for _, _, _, pad, _ in specs
        ),
        in_specs=[vmem] * 2,
        out_specs=tuple([vmem] * len(specs)),
        cost_estimate=pl.CostEstimate(flops=0, bytes_accessed=4 * hid.size * 2, transcendentals=0),
        compiler_params=pltpu.CompilerParams(vmem_limit_bytes=40 * 2**20),
    )(hid, cot)
    return list(outs)


def scatter_direct(value, axis, dim):
    count = lax.axis_size(axis)
    me = lax.axis_index(axis)
    share = value.shape[dim] // count
    total = lax.dynamic_slice_in_dim(value, me * share, share, dim).astype(F32)
    for step in range(1, count):
        goal = (me + step) % count
        part = lax.dynamic_slice_in_dim(value, goal * share, share, dim).astype(BF)
        got = permuted(part, (axis,), lambda i, s=step: ((i + s) % count,))
        total = total + got.astype(F32)
    return total


def scatter_bit(value, axis, bit, dim):
    me = (lax.axis_index(axis) // bit) % 2
    mine = lax.dynamic_index_in_dim(value, me, dim, keepdims=False).astype(F32)
    other = lax.dynamic_index_in_dim(value, 1 - me, dim, keepdims=False).astype(BF)
    got = permuted(other, (axis,), lambda i: (i ^ bit,))
    return mine + got.astype(F32)


def reduce_weights(keep, send, lons, returns):
    half, deep, width = keep.shape
    lats = lax.axis_size("lat")
    moved, waiting = [], list(returns)

    def release(value, count=1):
        for _ in range(min(count, len(waiting))):
            held, move = waiting.pop(0)
            value, held = lax.optimization_barrier((value, held))
            moved.append(move(held))
        return value

    got = permuted(send, ("lon",), lambda i: (i ^ 1,))
    keep = release(keep, len(waiting) // 2)
    early = len(moved)
    total = release((keep + got.astype(F32)).reshape(lats, lons // 2, deep, width), len(waiting))
    bit, left = 2, lons // 2
    while left > 1:
        total = scatter_bit(total.reshape(lats, left // 2, 2, deep, width), "lon", bit, 2)
        left //= 2
        bit *= 2
    total, moved[:early] = lax.optimization_barrier((total.reshape(lats, deep, width), moved[:early]))
    total = scatter_direct(total, "dp", 2)
    total, moved[early:] = lax.optimization_barrier((total, moved[early:]))
    return scatter_direct(total, "lat", 0)[0], moved


def per_device(hidden_in, grad_out, norm_gain, w_qkv, w_proj):
    samples, lat_rows, lon_cols, width = hidden_in.shape
    half = WIN // 2
    nr, nc = lat_rows // WIN, lon_cols // WIN
    short = half + (-half) % 16
    wide = WIN + (-WIN) % 16
    lons = lax.axis_size("lon")
    parts = lax.axis_size("lat") * lons
    if lons & (lons - 1) or lons < 2:
        raise ValueError("lon size")

    odd = lax.axis_index("lon") % 2
    inner = [wc * WIN + SHIFT for wc in range(nc - 1)]
    edge = (nc - 1) * WIN + SHIFT
    sent = cut_call(hidden_in, grad_out, [("sent", at, WIN, wide, "") for at in inner], half) if inner else []
    hid, cot, sent = lax.optimization_barrier((hidden_in, grad_out, sent))
    inner_in = [shared(p) for p in sent]
    specs = [("sent", 0, half, short, "peer"), ("own", 0, half, short, "")]
    specs += [("own", edge, half, short, "own"), ("sent", edge, half, short, "")]
    specs += [("own", at, WIN, wide, "own") for at in inner]
    fixed = [(2 * wr + 1 + i) * half for wr in range(nr - 1) for i in range(2)]
    specs += [(r, at, WIN, wide, "") for at in inner for r in fixed]
    specs += [(r, edge, half, short, "") for r in fixed] + [(r, 0, half, short, "") for r in fixed]
    cuts = cut_call(hid, cot, specs, half)
    side_sent, corner_sent, own_edge, edge_sent = cuts[:4]
    own_inner, rest = cuts[4:4 + len(inner)], cuts[4 + len(inner):]
    whole_inner = [[rest.pop(0) for _ in fixed] for _ in inner]
    whole_edge = [rest.pop(0) for _ in fixed]
    whole_side = [along_lon(rest.pop(0), -1) for _ in fixed]
    own_side, edge_in, corner_in = along_lon(side_sent, -1), shared(edge_sent), shared(corner_sent, east=1)

    order = [(b, wr, wc) for b in range(samples) for wc in range(nc) for wr in range(nr)]
    sums = None
    out = {}
    for step, (b, wr, wc) in enumerate(order):
        if wr < nr - 1 and wc < nc - 1:
            cells = whole_inner[wc][2 * wr:2 * wr + 2]
            metas = ((WIN, wide, False),) * 2
        elif wr < nr - 1:
            cells = [f[2 * wr + i] for i in range(2) for f in (whole_edge, whole_side)]
            metas = ((half, short, False),) * 4
        elif wc < nc - 1:
            cells = [own_inner[wc], inner_in[wc]]
            metas = ((WIN, wide, False), (WIN, wide, True))
        else:
            cells = [own_edge, own_side, edge_in, corner_in]
            metas = ((half, short, False),) * 2 + ((half, short, True),) * 2
        cells = [p[:, b].reshape(2, -1, width) for p in cells]
        done, sums = window_call(
            cells, metas, norm_gain, w_qkv, w_proj, sums, parts if step == len(order) - 1 else None
        )
        out[b, wr, wc] = [d.reshape(half, pad, width) for d, (n, pad, _) in zip(done, metas)]

    late = [(out[b, nr - 1, wc][1], lambda v: shared(v, back=True)) for b in range(samples) for wc in range(nc - 1)]
    for b in range(samples):
        own, own_lon, other, other_lon = out[b, nr - 1, nc - 1]
        late.append((other, lambda v: shared(v, back=True)))
        late.append((other_lon, lambda v: shared(v, back=True, east=1)))
        late.append((own_lon, lambda v: along_lon(v, 1)))
    total, moved = reduce_weights(sums[0], sums[1], lons, late)

    rows_out = []
    for b in range(samples):
        def stacked(own, back, between, upper):
            above = jnp.where(upper, own, back)
            below = jnp.where(upper, back, own)
            return jnp.concatenate([above] + between + [below], axis=0)

        columns = []
        for wc in range(nc - 1):
            own, other = out[b, nr - 1, wc]
            between = [out[b, wr, wc][i] for wr in range(nr - 1) for i in range(2)]
            columns.append(stacked(own, moved[b * (nc - 1) + wc], between, odd == 1)[:, :WIN])
        own = out[b, nr - 1, nc - 1][0]
        back, far, near = moved[samples * (nc - 1) + 3 * b:][:3]
        between = [out[b, wr, nc - 1][i] for wr in range(nr - 1) for i in (0, 2)]
        columns.append(stacked(own, back, between, odd == 1)[:, :half])
        between = [along_lon(out[b, wr, nc - 1][i], 1) for wr in range(nr - 1) for i in (1, 3)]
        columns.insert(0, stacked(near, far, between, odd == 0)[:, :half])
        rows_out.append(jnp.concatenate(columns, axis=1))
    returned = jnp.stack(rows_out)
    grad_in = (grad_out.astype(F32) + returned.astype(F32)).astype(BF)
    total_cells = (
        lax.axis_size("dp") * samples * lat_rows * lax.axis_size("lat") * lon_cols * lons
    )
    factor = float(total_cells) ** (-0.5)
    total = total.T * factor
    cut = 3 * width // parts
    return (grad_in, total[:, :cut], total[:, cut:])


def solution(mesh):
    in_specs = (P("dp", "lat", "lon", None), P("dp", "lat", "lon", None), P(), P(), P())
    out_specs = (P("dp", "lat", "lon", None), P("dp", ("lat", "lon")), P("dp", ("lat", "lon")))
    return jax.shard_map(
        per_device, mesh=mesh, in_specs=in_specs, out_specs=out_specs, check_vma=False
    )
```

```python
import functools, math
import jax, jax.numpy as jnp
from jax import lax
from jax.experimental import pallas as pl
from jax.experimental.pallas import tpu as pltpu

from jax.sharding import PartitionSpec as P

HEADS = 6
WIN = 30
SHIFT = 15
EPSILON = 1e-05
BF = jnp.bfloat16
F32 = jnp.float32
LN2 = math.log(2.0)

def mm(a, b):
    return lax.dot_general(a, b, (((1,), (0,)), ((), ())), preferred_element_type=F32)

def mm_t(a, b):
    return lax.dot_general(a, b, (((1,), (1,)), ((), ())), preferred_element_type=F32)

def blocks_of(n, step):
    return [(at, min(step, n - at)) for at in range(0, n, step)]

def window_kernel(head, metas, split, *refs):
    count = len(metas)
    pieces, refs = refs[:count], refs[count:]
    gain_ref, wqkv_ref, wproj_ref = refs[:3]
    refs = refs[3:]
    if split[0]:
        prev, refs = refs[:2], refs[2:]
    d_refs, refs = refs[:count], refs[count:]
    (gq_ref, gp_ref), refs = refs[:2], refs[2:]
    c_ref, nl, q_s, k_s, v_s, b_s, kT, vT, bT, p_s, ds_s, dqkv, attT = refs[:13]
    cells, width = c_ref.shape
    pair = 2 * head
    pairs = width // pair
    qscale = head ** -0.5 / LN2
    at = 0
    starts = []
    for p in pieces:
        starts.append(at)
        c_ref[at:at + p.shape[1]] = p[1]
        at += p.shape[1]
    odd = lax.rem(lax.axis_index("lon"), 2)
    packed = jnp.where((lax.axis_index("lat") == lax.axis_size("lat") - 1) & (odd == 0), 1.0, 0.0)
    oks, seconds = [], []
    for p, (n, pad, other) in zip(pieces, metas):
        place = lax.broadcasted_iota(jnp.int32, (p.shape[1], pair), 0)
        oks.append(jnp.where(lax.rem(place, pad) < n, 1.0, 0.0))
        seconds.append(jnp.full((p.shape[1], pair), packed if other else 0.0, F32))
    valid_col = jnp.concatenate(oks, axis=0)
    second = jnp.concatenate(seconds, axis=0)
    x = jnp.concatenate([p[0] for p in pieces], axis=0).astype(F32)
    mean = jnp.mean(x, axis=1, keepdims=True)
    cen = x - mean
    rstd = lax.rsqrt(jnp.mean(cen * cen, axis=1, keepdims=True) + EPSILON)
    gain = gain_ref[...][None]
    nl[...] = (cen * rstd * gain).astype(BF)
    qb = blocks_of(cells, cells)

    def one_pair(j, _):
        cols = pl.ds(pl.multiple_of(j * pair, pair), pair)
        colk = pl.ds(pl.multiple_of(width + j * pair, pair), pair)
        colv = pl.ds(pl.multiple_of(2 * width + j * pair, pair), pair)
        q_s[...] = (mm(nl[...], wqkv_ref[:, cols]) * qscale).astype(BF)
        k_s[...] = mm(nl[...], wqkv_ref[:, colk]).astype(BF)
        v_s[...] = mm(nl[...], wqkv_ref[:, colv]).astype(BF)
        b_s[...] = mm_t(c_ref[...], wproj_ref[cols, :]).astype(BF)
        kT[...] = k_s[...].T
        vT[...] = v_s[...].T
        bT[...] = b_s[...].T
        lane = lax.broadcasted_iota(jnp.int32, (cells, pair), 1)
        row = lax.broadcasted_iota(jnp.int32, (pair, cells), 0)
        outs = []
        for h in range(2):
            own = (lane >= head) if h else (lane < head)
            own_r = (row >= head) if h else (row < head)
            aug = 0 if h else head
            seen = jnp.where(lane == aug, valid_col * (1.0 - second), valid_col * second)
            two = (lane == aug) | (lane == aug + 1)
            bias = jnp.where(two, (seen - 1.0) * 30000.0, 0.0).astype(BF)
            group = jnp.where(lane == aug, 1.0 - second, second)
            kk = jnp.where(own, k_s[...], bias)
            qq = jnp.where(own, q_s[...], jnp.where(two, group, 0.0).astype(BF))
            vv = jnp.where(own, v_s[...], jnp.where(two, 1.0, 0.0).astype(BF))
            vvT = jnp.where(own_r, vT[...], jnp.where(row == aug, 1.0, 0.0).astype(BF))
            for at, n in qb:
                s = mm_t(kk, qq[at:at + n])
                e = jnp.exp2(s).astype(BF)
                oT = mm(vvT, e)
                total = oT[aug:aug + 1]
                inv = 1.0 / total
                aT = oT * inv
                attT[pl.ds(pl.multiple_of(j * pair + h * head, head), head), at:at + n] = aT[h * head:(h + 1) * head].astype(BF)
                bTn = bT[:, at:at + n].astype(F32)
                ownn = own_r[:, :n]
                rown = row[:, :n]
                rt = jnp.sum(jnp.where(ownn, bTn * aT, 0.0), axis=0, keepdims=True)
                hi = rt.astype(BF).astype(F32)
                lo = rt - hi
                baug = jnp.where(ownn, bTn, jnp.where(rown == aug, -hi, jnp.where(rown == aug + 1, -lo, 0.0))).astype(BF)
                p = e * inv.astype(BF)
                p_s[h, :, at:at + n] = p
                dp = mm(vv, baug).astype(BF)
                ds_s[h, :, at:at + n] = p * dp
            dv = mm(p_s[h], b_s[...])
            dk = mm(ds_s[h], q_s[...]) * LN2
            dqT = mm(kT[...], ds_s[h]) * (head ** -0.5)
            outs.append((dqT, dk, dv))
        dqT = jnp.where(row < head, outs[0][0], outs[1][0]).astype(BF)
        dqkv[:, cols] = dqT.T
        dqkv[:, colk] = jnp.where(lane < head, outs[0][1], outs[1][1]).astype(BF)
        dqkv[:, colv] = jnp.where(lane < head, outs[0][2], outs[1][2]).astype(BF)
        return 0

    lax.fori_loop(0, pairs, one_pair, 0)
    gp = mm(attT[...], c_ref[...])
    gq = mm(nl[...].T, dqkv[...])
    if split[0]:
        gq = gq + prev[0][...]
        gp = gp + prev[1][...]
    if split[1] is None:
        gq_ref[...] = gq
        gp_ref[...] = gp
    else:
        joined = refs[13]
        parts = split[1]
        gqT, gpT = gq.T, gp.T
        dq_rows, dp_rows = gqT.shape[0] // parts, gpT.shape[0] // parts
        for i in range(parts):
            joined[i, :dq_rows] = gqT[i * dq_rows:(i + 1) * dq_rows]
            joined[i, dq_rows:] = gpT[i * dp_rows:(i + 1) * dp_rows]
        me = odd
        for i in range(parts // 2):
            gq_ref[i] = joined[2 * i + me]
            gp_ref[i] = joined[2 * i + 1 - me].astype(BF)
    dn = mm_t(dqkv[...], wqkv_ref[...]) * gain
    normed = cen * rstd
    d = rstd * (dn - jnp.mean(dn, axis=1, keepdims=True) - normed * jnp.mean(dn * normed, axis=1, keepdims=True))
    d = d.astype(BF)
    for ref, at in zip(d_refs, starts):
        ref[...] = d[at:at + ref.shape[0]]


def window_call(pieces, metas, gain, wqkv, wproj, prev, parts):
    width = wproj.shape[0]
    head = width // HEADS
    pair = 2 * head
    sizes = [p.shape[1] for p in pieces]
    cells = sum(sizes)
    deep = 4 * width // parts if parts else 0
    if parts is None:
        sums = (jax.ShapeDtypeStruct((width, 3 * width), F32), jax.ShapeDtypeStruct((width, width), F32))
    else:
        sums = (jax.ShapeDtypeStruct((parts // 2, deep, width), F32),
                jax.ShapeDtypeStruct((parts // 2, deep, width), BF))
    scratch = ([pltpu.VMEM((cells, width), BF)] * 2
               + [pltpu.VMEM((cells, pair), BF)] * 4
               + [pltpu.VMEM((pair, cells), BF)] * 3
               + [pltpu.VMEM((2, cells, cells), BF)] * 2
               + [pltpu.VMEM((cells, 3 * width), BF), pltpu.VMEM((width, cells), BF)])
    if parts is not None:
        scratch.append(pltpu.VMEM((parts, deep, width), F32))
    vmem = pl.BlockSpec(memory_space=pltpu.VMEM)
    args = list(pieces) + [gain, wqkv, wproj] + (list(prev) if prev else [])
    outs = pl.pallas_call(
        functools.partial(window_kernel, head, metas, (prev is not None, parts)),
        out_shape=tuple(jax.ShapeDtypeStruct((n, width), BF) for n in sizes) + sums,
        in_specs=[vmem] * len(args),
        out_specs=[vmem] * (len(sizes) + 2),
        scratch_shapes=scratch,
        cost_estimate=pl.CostEstimate(
            flops=24 * cells * width * width + 12 * cells * cells * width,
            bytes_accessed=8 * 2**20,
            transcendentals=HEADS * cells * cells,
        ),
        compiler_params=pltpu.CompilerParams(vmem_limit_bytes=32 * 2**20),
    )(*args)
    return outs[:len(sizes)], outs[-2:]


def permuted(value, axes, target):
    sizes = [lax.axis_size(a) for a in axes]
    pairs = []
    for source in range(math.prod(sizes)):
        at, rest = [], source
        for size in reversed(sizes):
            at.append(rest % size)
            rest //= size
        goal = target(*reversed(at))
        if goal is None:
            continue
        flat = 0
        for size, place in zip(sizes, goal):
            flat = flat * size + place
        pairs.append((source, flat))
    return lax.ppermute(value, tuple(axes), pairs)


def shared(value, back=False, east=0):
    lats, lons = lax.axis_size("lat"), lax.axis_size("lon")
    pairs = []
    for i in range(lats):
        for j in range(lons):
            if j % 2 == 0:
                goal = (i - 1, j) if i > 0 else None
            else:
                goal = (i + 1, j) if i < lats - 1 else (i, j - 1)
            if goal is not None:
                pair = (i * lons + j, goal[0] * lons + goal[1])
                home = i * lons + (j + east) % lons
                pairs.append((pair[1], home) if back else (home, pair[1]))
    return lax.ppermute(value, ("lat", "lon"), pairs)


def along_lon(value, step):
    count = lax.axis_size("lon")
    return lax.ppermute(value, "lon", [(j, (j + step) % count) for j in range(count)])


def cut_kernel(specs, half, hid_ref, cot_ref, *outs):
    odd = lax.rem(lax.axis_index("lon"), 2)
    top = lax.axis_index("lat") == 0
    end = hid_ref.shape[1] - half
    starts = {"own": (1 - odd) * end, "sent": odd * end}
    zeroed = {"own": top & (odd == 1), "peer": top & (odd == 0)}
    for out, (rows, cols, n, pad, clear) in zip(outs, specs):
        at = starts.get(rows, rows)
        for k, ref in enumerate((hid_ref, cot_ref)):
            for b in range(hid_ref.shape[0]):
                cut = ref[b, pl.ds(at, half)].astype(F32)[:, cols:cols + n]
                if clear:
                    cut = jnp.where(zeroed[clear], 0.0, cut)
                filler = jnp.zeros((half, pad - n, cut.shape[2]), F32)
                out[k, b] = jnp.concatenate([cut, filler], axis=1).astype(BF)


def cut_call(hid, cot, specs, half):
    samples, _, _, width = hid.shape
    vmem = pl.BlockSpec(memory_space=pltpu.VMEM)
    outs = pl.pallas_call(
        functools.partial(cut_kernel, specs, half),
        out_shape=tuple(
            jax.ShapeDtypeStruct((2, samples, half, pad, width), BF) for _, _, _, pad, _ in specs
        ),
        in_specs=[vmem] * 2,
        out_specs=tuple([vmem] * len(specs)),
        cost_estimate=pl.CostEstimate(flops=0, bytes_accessed=4 * hid.size * 2, transcendentals=0),
        compiler_params=pltpu.CompilerParams(vmem_limit_bytes=40 * 2**20),
    )(hid, cot)
    return list(outs)


def scatter_bit(value, axis, bit, dim):
    me = (lax.axis_index(axis) // bit) % 2
    mine = lax.dynamic_index_in_dim(value, me, dim, keepdims=False).astype(F32)
    other = lax.dynamic_index_in_dim(value, 1 - me, dim, keepdims=False).astype(BF)
    got = permuted(other, (axis,), lambda i: (i ^ bit,))
    return mine + got.astype(F32)


def reduce_weights(keep, send, lons, returns):
    half, deep, width = keep.shape
    lats = lax.axis_size("lat")
    moved, waiting = [], list(returns)

    def release(value, count=1):
        for _ in range(min(count, len(waiting))):
            held, move = waiting.pop(0)
            value, held = lax.optimization_barrier((value, held))
            moved.append(move(held))
        return value

    got = permuted(send, ("lon",), lambda i: (i ^ 1,))
    keep = release(keep, len(waiting) // 2)
    early = len(moved)
    total = release((keep + got.astype(F32)).reshape(lats, lons // 2, deep, width), len(waiting))
    bit, left = 2, lons // 2
    while left > 1:
        total = scatter_bit(total.reshape(lats, left // 2, 2, deep, width), "lon", bit, 2)
        left //= 2
        bit *= 2
    total, moved[:early] = lax.optimization_barrier((total.reshape(lats, deep, width), moved[:early]))
    dps = lax.axis_size("dp")
    blocks = total.astype(BF).reshape(lats, deep, dps, width // dps).transpose(2, 0, 1, 3)
    blocks, moved[early:] = lax.optimization_barrier((blocks, moved[early:]))
    blocks = blocks.reshape(dps * lats, deep, width // dps)
    return lax.all_to_all(blocks, ("dp", "lat"), 0, 0, tiled=True), moved


def finish_kernel(factor, cut, in_ref, gq_ref, gp_ref):
    total = in_ref[0].astype(F32)
    for i in range(1, in_ref.shape[0]):
        total = total + in_ref[i].astype(F32)
    total = (total * factor).T
    gq_ref[...] = total[:, :cut]
    gp_ref[...] = total[:, cut:]


def finish_call(blocks, factor, cut):
    _, deep, rows = blocks.shape
    vmem = pl.BlockSpec(memory_space=pltpu.VMEM)
    return pl.pallas_call(
        functools.partial(finish_kernel, factor, cut),
        out_shape=(jax.ShapeDtypeStruct((rows, cut), F32), jax.ShapeDtypeStruct((rows, deep - cut), F32)),
        in_specs=[vmem],
        out_specs=(vmem, vmem),
        compiler_params=pltpu.CompilerParams(vmem_limit_bytes=16 * 2**20),
    )(blocks)


def per_device(hidden_in, grad_out, norm_gain, w_qkv, w_proj):
    samples, lat_rows, lon_cols, width = hidden_in.shape
    half = WIN // 2
    nr, nc = lat_rows // WIN, lon_cols // WIN
    short = half + (-half) % 16
    wide = WIN + (-WIN) % 16
    lons = lax.axis_size("lon")
    parts = lax.axis_size("lat") * lons
    if lons & (lons - 1) or lons < 2:
        raise ValueError("lon size")

    odd = lax.axis_index("lon") % 2
    inner = [wc * WIN + SHIFT for wc in range(nc - 1)]
    edge = (nc - 1) * WIN + SHIFT
    sent = cut_call(hidden_in, grad_out, [("sent", at, WIN, wide, "") for at in inner], half) if inner else []
    hid, cot, sent = lax.optimization_barrier((hidden_in, grad_out, sent))
    inner_in = [shared(p) for p in sent]
    specs = [("sent", 0, half, short, "peer"), ("own", 0, half, short, "")]
    specs += [("own", edge, half, short, "own"), ("sent", edge, half, short, "")]
    specs += [("own", at, WIN, wide, "own") for at in inner]
    fixed = [(2 * wr + 1 + i) * half for wr in range(nr - 1) for i in range(2)]
    specs += [(r, at, WIN, wide, "") for at in inner for r in fixed]
    specs += [(r, edge, half, short, "") for r in fixed] + [(r, 0, half, short, "") for r in fixed]
    cuts = cut_call(hid, cot, specs, half)
    side_sent, corner_sent, own_edge, edge_sent = cuts[:4]
    own_inner, rest = cuts[4:4 + len(inner)], cuts[4 + len(inner):]
    whole_inner = [[rest.pop(0) for _ in fixed] for _ in inner]
    whole_edge = [rest.pop(0) for _ in fixed]
    whole_side = [along_lon(rest.pop(0), -1) for _ in fixed]
    own_side, edge_in, corner_in = along_lon(side_sent, -1), shared(edge_sent), shared(corner_sent, east=1)

    order = [(b, wr, wc) for b in range(samples) for wc in range(nc) for wr in range(nr)]
    sums = None
    out = {}
    for step, (b, wr, wc) in enumerate(order):
        if wr < nr - 1 and wc < nc - 1:
            cells = whole_inner[wc][2 * wr:2 * wr + 2]
            metas = ((WIN, wide, False),) * 2
        elif wr < nr - 1:
            cells = [f[2 * wr + i] for i in range(2) for f in (whole_edge, whole_side)]
            metas = ((half, short, False),) * 4
        elif wc < nc - 1:
            cells = [own_inner[wc], inner_in[wc]]
            metas = ((WIN, wide, False), (WIN, wide, True))
        else:
            cells = [own_edge, own_side, edge_in, corner_in]
            metas = ((half, short, False),) * 2 + ((half, short, True),) * 2
        cells = [p[:, b].reshape(2, -1, width) for p in cells]
        done, sums = window_call(
            cells, metas, norm_gain, w_qkv, w_proj, sums, parts if step == len(order) - 1 else None
        )
        out[b, wr, wc] = [d.reshape(half, pad, width) for d, (n, pad, _) in zip(done, metas)]

    late = [(out[b, nr - 1, wc][1], lambda v: shared(v, back=True)) for b in range(samples) for wc in range(nc - 1)]
    for b in range(samples):
        own, own_lon, other, other_lon = out[b, nr - 1, nc - 1]
        late.append((other, lambda v: shared(v, back=True)))
        late.append((other_lon, lambda v: shared(v, back=True, east=1)))
        late.append((own_lon, lambda v: along_lon(v, 1)))
    total, moved = reduce_weights(sums[0], sums[1], lons, late)

    rows_out = []
    for b in range(samples):
        def stacked(own, back, between, upper):
            above = jnp.where(upper, own, back)
            below = jnp.where(upper, back, own)
            return jnp.concatenate([above] + between + [below], axis=0)

        columns = []
        for wc in range(nc - 1):
            own, other = out[b, nr - 1, wc]
            between = [out[b, wr, wc][i] for wr in range(nr - 1) for i in range(2)]
            columns.append(stacked(own, moved[b * (nc - 1) + wc], between, odd == 1)[:, :WIN])
        own = out[b, nr - 1, nc - 1][0]
        back, far, near = moved[samples * (nc - 1) + 3 * b:][:3]
        between = [out[b, wr, nc - 1][i] for wr in range(nr - 1) for i in (0, 2)]
        columns.append(stacked(own, back, between, odd == 1)[:, :half])
        between = [along_lon(out[b, wr, nc - 1][i], 1) for wr in range(nr - 1) for i in (1, 3)]
        columns.insert(0, stacked(near, far, between, odd == 0)[:, :half])
        rows_out.append(jnp.concatenate(columns, axis=1))
    returned = jnp.stack(rows_out)
    grad_in = (grad_out.astype(F32) + returned.astype(F32)).astype(BF)
    total_cells = (
        lax.axis_size("dp") * samples * lat_rows * lax.axis_size("lat") * lon_cols * lons
    )
    factor = float(total_cells) ** (-0.5)
    gq, gp = finish_call(total, factor, 3 * width // parts)
    return (grad_in, gq, gp)


def solution(mesh):
    in_specs = (P("dp", "lat", "lon", None), P("dp", "lat", "lon", None), P(), P(), P())
    out_specs = (P("dp", "lat", "lon", None), P("dp", ("lat", "lon")), P("dp", ("lat", "lon")))
    return jax.shard_map(
        per_device, mesh=mesh, in_specs=in_specs, out_specs=out_specs, check_vma=False
    )
```

```python
import functools, math
import jax, jax.numpy as jnp
from jax import lax
from jax.experimental import pallas as pl
from jax.experimental.pallas import tpu as pltpu

from jax.sharding import PartitionSpec as P

HEADS = 6
WIN = 30
SHIFT = 15
EPSILON = 1e-05
BF = jnp.bfloat16
F32 = jnp.float32
LN2 = math.log(2.0)

def mm(a, b):
    return lax.dot_general(a, b, (((1,), (0,)), ((), ())), preferred_element_type=F32)

def mm_t(a, b):
    return lax.dot_general(a, b, (((1,), (1,)), ((), ())), preferred_element_type=F32)

def blocks_of(n, step):
    return [(at, min(step, n - at)) for at in range(0, n, step)]

def window_kernel(head, metas, split, *refs):
    count = len(metas)
    pieces, refs = refs[:count], refs[count:]
    gain_ref, wqkv_ref, wproj_ref = refs[:3]
    refs = refs[3:]
    if split[0]:
        prev, refs = refs[:2], refs[2:]
    d_refs, refs = refs[:count], refs[count:]
    (gq_ref, gp_ref), refs = refs[:2], refs[2:]
    c_ref, nl, q_s, k_s, v_s, b_s, kT, vT, bT, p_s, ds_s, dqkv, attT = refs[:13]
    cells, width = c_ref.shape
    pair = 2 * head
    pairs = width // pair
    qscale = head ** -0.5 / LN2
    at = 0
    starts = []
    for p in pieces:
        starts.append(at)
        c_ref[at:at + p.shape[1]] = p[1]
        at += p.shape[1]
    odd = lax.rem(lax.axis_index("lon"), 2)
    packed = jnp.where((lax.axis_index("lat") == lax.axis_size("lat") - 1) & (odd == 0), 1.0, 0.0)
    oks, seconds = [], []
    for p, (n, pad, other) in zip(pieces, metas):
        place = lax.broadcasted_iota(jnp.int32, (p.shape[1], pair), 0)
        oks.append(jnp.where(lax.rem(place, pad) < n, 1.0, 0.0))
        seconds.append(jnp.full((p.shape[1], pair), packed if other else 0.0, F32))
    valid_col = jnp.concatenate(oks, axis=0)
    second = jnp.concatenate(seconds, axis=0)
    x = jnp.concatenate([p[0] for p in pieces], axis=0).astype(F32)
    mean = jnp.mean(x, axis=1, keepdims=True)
    cen = x - mean
    rstd = lax.rsqrt(jnp.mean(cen * cen, axis=1, keepdims=True) + EPSILON)
    gain = gain_ref[...][None]
    nl[...] = (cen * rstd * gain).astype(BF)
    qb = blocks_of(cells, cells)

    def one_pair(j, _):
        cols = pl.ds(pl.multiple_of(j * pair, pair), pair)
        colk = pl.ds(pl.multiple_of(width + j * pair, pair), pair)
        colv = pl.ds(pl.multiple_of(2 * width + j * pair, pair), pair)
        q_s[...] = (mm(nl[...], wqkv_ref[:, cols]) * qscale).astype(BF)
        k_s[...] = mm(nl[...], wqkv_ref[:, colk]).astype(BF)
        v_s[...] = mm(nl[...], wqkv_ref[:, colv]).astype(BF)
        b_s[...] = mm_t(c_ref[...], wproj_ref[cols, :]).astype(BF)
        kT[...] = k_s[...].T
        vT[...] = v_s[...].T
        bT[...] = b_s[...].T
        lane = lax.broadcasted_iota(jnp.int32, (cells, pair), 1)
        row = lax.broadcasted_iota(jnp.int32, (pair, cells), 0)
        outs = []
        for h in range(2):
            own = (lane >= head) if h else (lane < head)
            own_r = (row >= head) if h else (row < head)
            aug = 0 if h else head
            seen = jnp.where(lane == aug, valid_col * (1.0 - second), valid_col * second)
            two = (lane == aug) | (lane == aug + 1)
            bias = jnp.where(two, (seen - 1.0) * 30000.0, 0.0).astype(BF)
            group = jnp.where(lane == aug, 1.0 - second, second)
            kk = jnp.where(own, k_s[...], bias)
            qq = jnp.where(own, q_s[...], jnp.where(two, group, 0.0).astype(BF))
            vv = jnp.where(own, v_s[...], jnp.where(two, 1.0, 0.0).astype(BF))
            vvT = jnp.where(own_r, vT[...], jnp.where(row == aug, 1.0, 0.0).astype(BF))
            for at, n in qb:
                s = mm_t(kk, qq[at:at + n])
                e = jnp.exp2(s).astype(BF)
                oT = mm(vvT, e)
                total = oT[aug:aug + 1]
                inv = 1.0 / total
                aT = oT * inv
                attT[pl.ds(pl.multiple_of(j * pair + h * head, head), head), at:at + n] = aT[h * head:(h + 1) * head].astype(BF)
                bTn = bT[:, at:at + n].astype(F32)
                ownn = own_r[:, :n]
                rown = row[:, :n]
                rt = jnp.sum(jnp.where(ownn, bTn * aT, 0.0), axis=0, keepdims=True)
                hi = rt.astype(BF).astype(F32)
                lo = rt - hi
                baug = jnp.where(ownn, bTn, jnp.where(rown == aug, -hi, jnp.where(rown == aug + 1, -lo, 0.0))).astype(BF)
                p = e * inv.astype(BF)
                p_s[h, :, at:at + n] = p
                dp = mm(vv, baug).astype(BF)
                ds_s[h, :, at:at + n] = p * dp
            dv = mm(p_s[h], b_s[...])
            dk = mm(ds_s[h], q_s[...]) * LN2
            dqT = mm(kT[...], ds_s[h]) * (head ** -0.5)
            outs.append((dqT, dk, dv))
        dqT = jnp.where(row < head, outs[0][0], outs[1][0]).astype(BF)
        dqkv[:, cols] = dqT.T
        dqkv[:, colk] = jnp.where(lane < head, outs[0][1], outs[1][1]).astype(BF)
        dqkv[:, colv] = jnp.where(lane < head, outs[0][2], outs[1][2]).astype(BF)
        return 0

    lax.fori_loop(0, pairs, one_pair, 0)
    gp = mm(attT[...], c_ref[...])
    gq = mm(nl[...].T, dqkv[...])
    if split[0]:
        gq = gq + prev[0][...]
        gp = gp + prev[1][...]
    if split[1] is None:
        gq_ref[...] = gq
        gp_ref[...] = gp
    else:
        joined = refs[13]
        parts = split[1]
        gqT, gpT = gq.T, gp.T
        dq_rows, dp_rows = gqT.shape[0] // parts, gpT.shape[0] // parts
        for i in range(parts):
            joined[i, :dq_rows] = gqT[i * dq_rows:(i + 1) * dq_rows]
            joined[i, dq_rows:] = gpT[i * dp_rows:(i + 1) * dp_rows]
        me = odd
        for i in range(parts // 2):
            gq_ref[i] = joined[2 * i + me]
            gp_ref[i] = joined[2 * i + 1 - me].astype(BF)
    dn = mm_t(dqkv[...], wqkv_ref[...]) * gain
    normed = cen * rstd
    d = rstd * (dn - jnp.mean(dn, axis=1, keepdims=True) - normed * jnp.mean(dn * normed, axis=1, keepdims=True))
    d = d.astype(BF)
    for ref, at in zip(d_refs, starts):
        ref[...] = d[at:at + ref.shape[0]]


def window_call(pieces, metas, gain, wqkv, wproj, prev, parts):
    width = wproj.shape[0]
    head = width // HEADS
    pair = 2 * head
    sizes = [p.shape[1] for p in pieces]
    cells = sum(sizes)
    deep = 4 * width // parts if parts else 0
    if parts is None:
        sums = (jax.ShapeDtypeStruct((width, 3 * width), F32), jax.ShapeDtypeStruct((width, width), F32))
    else:
        sums = (jax.ShapeDtypeStruct((parts // 2, deep, width), F32),
                jax.ShapeDtypeStruct((parts // 2, deep, width), BF))
    scratch = ([pltpu.VMEM((cells, width), BF)] * 2
               + [pltpu.VMEM((cells, pair), BF)] * 4
               + [pltpu.VMEM((pair, cells), BF)] * 3
               + [pltpu.VMEM((2, cells, cells), BF)] * 2
               + [pltpu.VMEM((cells, 3 * width), BF), pltpu.VMEM((width, cells), BF)])
    if parts is not None:
        scratch.append(pltpu.VMEM((parts, deep, width), F32))
    vmem = pl.BlockSpec(memory_space=pltpu.VMEM)
    args = list(pieces) + [gain, wqkv, wproj] + (list(prev) if prev else [])
    outs = pl.pallas_call(
        functools.partial(window_kernel, head, metas, (prev is not None, parts)),
        out_shape=tuple(jax.ShapeDtypeStruct((n, width), BF) for n in sizes) + sums,
        in_specs=[vmem] * len(args),
        out_specs=[vmem] * (len(sizes) + 2),
        scratch_shapes=scratch,
        cost_estimate=pl.CostEstimate(
            flops=24 * cells * width * width + 12 * cells * cells * width,
            bytes_accessed=8 * 2**20,
            transcendentals=HEADS * cells * cells,
        ),
        compiler_params=pltpu.CompilerParams(vmem_limit_bytes=32 * 2**20),
    )(*args)
    return outs[:len(sizes)], outs[-2:]


def permuted(value, axes, target):
    sizes = [lax.axis_size(a) for a in axes]
    pairs = []
    for source in range(math.prod(sizes)):
        at, rest = [], source
        for size in reversed(sizes):
            at.append(rest % size)
            rest //= size
        goal = target(*reversed(at))
        if goal is None:
            continue
        flat = 0
        for size, place in zip(sizes, goal):
            flat = flat * size + place
        pairs.append((source, flat))
    return lax.ppermute(value, tuple(axes), pairs)


def shared(value, back=False, east=0):
    lats, lons = lax.axis_size("lat"), lax.axis_size("lon")
    pairs = []
    for i in range(lats):
        for j in range(lons):
            if j % 2 == 0:
                goal = (i - 1, j) if i > 0 else None
            else:
                goal = (i + 1, j) if i < lats - 1 else (i, j - 1)
            if goal is not None:
                pair = (i * lons + j, goal[0] * lons + goal[1])
                home = i * lons + (j + east) % lons
                pairs.append((pair[1], home) if back else (home, pair[1]))
    return lax.ppermute(value, ("lat", "lon"), pairs)


def along_lon(value, step):
    count = lax.axis_size("lon")
    return lax.ppermute(value, "lon", [(j, (j + step) % count) for j in range(count)])


def cut_kernel(specs, half, hid_ref, cot_ref, *outs):
    odd = lax.rem(lax.axis_index("lon"), 2)
    top = lax.axis_index("lat") == 0
    end = hid_ref.shape[1] - half
    starts = {"own": (1 - odd) * end, "sent": odd * end}
    zeroed = {"own": top & (odd == 1), "peer": top & (odd == 0)}
    for out, (rows, cols, n, pad, clear) in zip(outs, specs):
        at = starts.get(rows, rows)
        for k, ref in enumerate((hid_ref, cot_ref)):
            for b in range(hid_ref.shape[0]):
                cut = ref[b, pl.ds(at, half)].astype(F32)[:, cols:cols + n]
                if clear:
                    cut = jnp.where(zeroed[clear], 0.0, cut)
                filler = jnp.zeros((half, pad - n, cut.shape[2]), F32)
                out[k, b] = jnp.concatenate([cut, filler], axis=1).astype(BF)


def cut_call(hid, cot, specs, half):
    samples, _, _, width = hid.shape
    vmem = pl.BlockSpec(memory_space=pltpu.VMEM)
    outs = pl.pallas_call(
        functools.partial(cut_kernel, specs, half),
        out_shape=tuple(
            jax.ShapeDtypeStruct((2, samples, half, pad, width), BF) for _, _, _, pad, _ in specs
        ),
        in_specs=[vmem] * 2,
        out_specs=tuple([vmem] * len(specs)),
        cost_estimate=pl.CostEstimate(flops=0, bytes_accessed=4 * hid.size * 2, transcendentals=0),
        compiler_params=pltpu.CompilerParams(vmem_limit_bytes=40 * 2**20),
    )(hid, cot)
    return list(outs)


def scatter_direct(value, axis, dim):
    count = lax.axis_size(axis)
    me = lax.axis_index(axis)
    share = value.shape[dim] // count
    total = lax.dynamic_slice_in_dim(value, me * share, share, dim).astype(F32)
    for step in range(1, count):
        goal = (me + step) % count
        part = lax.dynamic_slice_in_dim(value, goal * share, share, dim).astype(BF)
        got = permuted(part, (axis,), lambda i, s=step: ((i + s) % count,))
        total = total + got.astype(F32)
    return total


def scatter_bit(value, axis, bit, dim):
    me = (lax.axis_index(axis) // bit) % 2
    mine = lax.dynamic_index_in_dim(value, me, dim, keepdims=False).astype(F32)
    other = lax.dynamic_index_in_dim(value, 1 - me, dim, keepdims=False).astype(BF)
    got = permuted(other, (axis,), lambda i: (i ^ bit,))
    return mine + got.astype(F32)


def reduce_weights(keep, send, lons, inner_moved, returns):
    half, deep, width = keep.shape
    lats = lax.axis_size("lat")
    moved, waiting = [], list(returns)

    def release(value, count=1):
        for _ in range(min(count, len(waiting))):
            held, move = waiting.pop(0)
            value, held = lax.optimization_barrier((value, held))
            moved.append(move(held))
        return value

    got = permuted(send, ("lon",), lambda i: (i ^ 1,))
    keep = release(keep, len(waiting) // 3)
    early = len(moved)
    total = (keep + got.astype(F32)).reshape(lats, lons // 2, deep, width)
    total, inner_moved = lax.optimization_barrier((total, inner_moved))
    bit, left = 2, lons // 2
    while left > 1:
        total = scatter_bit(total.reshape(lats, left // 2, 2, deep, width), "lon", bit, 2)
        left //= 2
        bit *= 2
    total, moved[:early] = lax.optimization_barrier((total.reshape(lats, deep, width), moved[:early]))
    total = release(total, len(waiting))
    total = scatter_direct(total, "dp", 2)
    total, moved[early:] = lax.optimization_barrier((total, moved[early:]))
    moved = inner_moved + moved
    return scatter_direct(total, "lat", 0)[0], moved


def per_device(hidden_in, grad_out, norm_gain, w_qkv, w_proj):
    samples, lat_rows, lon_cols, width = hidden_in.shape
    half = WIN // 2
    nr, nc = lat_rows // WIN, lon_cols // WIN
    short = half + (-half) % 16
    wide = WIN + (-WIN) % 16
    lons = lax.axis_size("lon")
    parts = lax.axis_size("lat") * lons
    if lons & (lons - 1) or lons < 2:
        raise ValueError("lon size")

    odd = lax.axis_index("lon") % 2
    inner = [wc * WIN + SHIFT for wc in range(nc - 1)]
    edge = (nc - 1) * WIN + SHIFT
    sent = cut_call(hidden_in, grad_out, [("sent", at, WIN, wide, "") for at in inner], half) if inner else []
    hid, cot, sent = lax.optimization_barrier((hidden_in, grad_out, sent))
    inner_in = [shared(p) for p in sent]
    specs = [("sent", 0, half, short, "peer"), ("own", 0, half, short, "")]
    specs += [("own", edge, half, short, "own"), ("sent", edge, half, short, "")]
    specs += [("own", at, WIN, wide, "own") for at in inner]
    fixed = [(2 * wr + 1 + i) * half for wr in range(nr - 1) for i in range(2)]
    specs += [(r, at, WIN, wide, "") for at in inner for r in fixed]
    specs += [(r, edge, half, short, "") for r in fixed] + [(r, 0, half, short, "") for r in fixed]
    cuts = cut_call(hid, cot, specs, half)
    side_sent, corner_sent, own_edge, edge_sent = cuts[:4]
    own_inner, rest = cuts[4:4 + len(inner)], cuts[4 + len(inner):]
    whole_inner = [[rest.pop(0) for _ in fixed] for _ in inner]
    whole_edge = [rest.pop(0) for _ in fixed]
    whole_side = [along_lon(rest.pop(0), -1) for _ in fixed]
    own_side, edge_in, corner_in = along_lon(side_sent, -1), shared(edge_sent), shared(corner_sent, east=1)

    order = [(b, wr, wc) for b in range(samples) for wc in range(nc) for wr in range(nr)]
    sums = None
    out = {}
    for step, (b, wr, wc) in enumerate(order):
        if wr < nr - 1 and wc < nc - 1:
            cells = whole_inner[wc][2 * wr:2 * wr + 2]
            metas = ((WIN, wide, False),) * 2
        elif wr < nr - 1:
            cells = [f[2 * wr + i] for i in range(2) for f in (whole_edge, whole_side)]
            metas = ((half, short, False),) * 4
        elif wc < nc - 1:
            cells = [own_inner[wc], inner_in[wc]]
            metas = ((WIN, wide, False), (WIN, wide, True))
        else:
            cells = [own_edge, own_side, edge_in, corner_in]
            metas = ((half, short, False),) * 2 + ((half, short, True),) * 2
        cells = [p[:, b].reshape(2, -1, width) for p in cells]
        done, sums = window_call(
            cells, metas, norm_gain, w_qkv, w_proj, sums, parts if step == len(order) - 1 else None
        )
        out[b, wr, wc] = [d.reshape(half, pad, width) for d, (n, pad, _) in zip(done, metas)]

    inner_moved = [
        shared(out[b, nr - 1, wc][1], back=True) for b in range(samples) for wc in range(nc - 1)
    ]
    late = []
    for b in range(samples):
        own, own_lon, other, other_lon = out[b, nr - 1, nc - 1]
        late.insert(b, (other, lambda v: shared(v, back=True)))
        late.append((other_lon, lambda v: shared(v, back=True, east=1)))
        late.append((own_lon, lambda v: along_lon(v, 1)))
    total, moved = reduce_weights(sums[0], sums[1], lons, inner_moved, late)

    edge_moved = moved[samples * (nc - 1):]
    rows_out = []
    for b in range(samples):
        def stacked(own, back, between, upper):
            above = jnp.where(upper, own, back)
            below = jnp.where(upper, back, own)
            return jnp.concatenate([above] + between + [below], axis=0)

        columns = []
        for wc in range(nc - 1):
            own, other = out[b, nr - 1, wc]
            between = [out[b, wr, wc][i] for wr in range(nr - 1) for i in range(2)]
            columns.append(stacked(own, moved[b * (nc - 1) + wc], between, odd == 1)[:, :WIN])
        own = out[b, nr - 1, nc - 1][0]
        back = edge_moved[b]
        far, near = edge_moved[samples + 2 * b:][:2]
        between = [out[b, wr, nc - 1][i] for wr in range(nr - 1) for i in (0, 2)]
        columns.append(stacked(own, back, between, odd == 1)[:, :half])
        between = [along_lon(out[b, wr, nc - 1][i], 1) for wr in range(nr - 1) for i in (1, 3)]
        columns.insert(0, stacked(near, far, between, odd == 0)[:, :half])
        rows_out.append(jnp.concatenate(columns, axis=1))
    returned = jnp.stack(rows_out)
    grad_in = (grad_out.astype(F32) + returned.astype(F32)).astype(BF)
    total_cells = (
        lax.axis_size("dp") * samples * lat_rows * lax.axis_size("lat") * lon_cols * lons
    )
    factor = float(total_cells) ** (-0.5)
    total = total.T * factor
    cut = 3 * width // parts
    return (grad_in, total[:, :cut], total[:, cut:])


def solution(mesh):
    in_specs = (P("dp", "lat", "lon", None), P("dp", "lat", "lon", None), P(), P(), P())
    out_specs = (P("dp", "lat", "lon", None), P("dp", ("lat", "lon")), P("dp", ("lat", "lon")))
    return jax.shard_map(
        per_device, mesh=mesh, in_specs=in_specs, out_specs=out_specs, check_vma=False
    )
```

```python
import functools, math
import jax, jax.numpy as jnp
from jax import lax
from jax.experimental import pallas as pl
from jax.experimental.pallas import tpu as pltpu

from jax.sharding import PartitionSpec as P

HEADS = 6
WIN = 30
SHIFT = 15
EPSILON = 1e-05
BF = jnp.bfloat16
F32 = jnp.float32
LN2 = math.log(2.0)

def mm(a, b):
    return lax.dot_general(a, b, (((1,), (0,)), ((), ())), preferred_element_type=F32)

def mm_t(a, b):
    return lax.dot_general(a, b, (((1,), (1,)), ((), ())), preferred_element_type=F32)

def blocks_of(n, step):
    return [(at, min(step, n - at)) for at in range(0, n, step)]

def window_kernel(head, metas, split, *refs):
    count = len(metas)
    pieces, refs = refs[:count], refs[count:]
    gain_ref, wqkv_ref, wproj_ref = refs[:3]
    refs = refs[3:]
    if split[0]:
        prev, refs = refs[:2], refs[2:]
    d_refs, refs = refs[:count], refs[count:]
    (gq_ref, gp_ref), refs = refs[:2], refs[2:]
    c_ref, nl, q_s, k_s, v_s, b_s, kT, vT, bT, p_s, ds_s, dqkv, attT = refs[:13]
    cells, width = c_ref.shape
    pair = 2 * head
    pairs = width // pair
    qscale = head ** -0.5 / LN2
    at = 0
    starts = []
    for p in pieces:
        starts.append(at)
        c_ref[at:at + p.shape[1]] = p[1]
        at += p.shape[1]
    odd = lax.rem(lax.axis_index("lon"), 2)
    packed = jnp.where((lax.axis_index("lat") == lax.axis_size("lat") - 1) & (odd == 0), 1.0, 0.0)
    oks, seconds = [], []
    for p, (n, pad, other) in zip(pieces, metas):
        place = lax.broadcasted_iota(jnp.int32, (p.shape[1], pair), 0)
        oks.append(jnp.where(lax.rem(place, pad) < n, 1.0, 0.0))
        seconds.append(jnp.full((p.shape[1], pair), packed if other else 0.0, F32))
    valid_col = jnp.concatenate(oks, axis=0)
    second = jnp.concatenate(seconds, axis=0)
    x = jnp.concatenate([p[0] for p in pieces], axis=0).astype(F32)
    mean = jnp.mean(x, axis=1, keepdims=True)
    cen = x - mean
    rstd = lax.rsqrt(jnp.mean(cen * cen, axis=1, keepdims=True) + EPSILON)
    gain = gain_ref[...][None]
    nl[...] = (cen * rstd * gain).astype(BF)
    qb = blocks_of(cells, cells)

    def one_pair(j, _):
        cols = pl.ds(pl.multiple_of(j * pair, pair), pair)
        colk = pl.ds(pl.multiple_of(width + j * pair, pair), pair)
        colv = pl.ds(pl.multiple_of(2 * width + j * pair, pair), pair)
        q_s[...] = (mm(nl[...], wqkv_ref[:, cols]) * qscale).astype(BF)
        k_s[...] = mm(nl[...], wqkv_ref[:, colk]).astype(BF)
        v_s[...] = mm(nl[...], wqkv_ref[:, colv]).astype(BF)
        b_s[...] = mm_t(c_ref[...], wproj_ref[cols, :]).astype(BF)
        kT[...] = k_s[...].T
        vT[...] = v_s[...].T
        bT[...] = b_s[...].T
        lane = lax.broadcasted_iota(jnp.int32, (cells, pair), 1)
        row = lax.broadcasted_iota(jnp.int32, (pair, cells), 0)
        outs = []
        for h in range(2):
            own = (lane >= head) if h else (lane < head)
            own_r = (row >= head) if h else (row < head)
            aug = 0 if h else head
            seen = jnp.where(lane == aug, valid_col * (1.0 - second), valid_col * second)
            two = (lane == aug) | (lane == aug + 1)
            bias = jnp.where(two, (seen - 1.0) * 30000.0, 0.0).astype(BF)
            group = jnp.where(lane == aug, 1.0 - second, second)
            kk = jnp.where(own, k_s[...], bias)
            qq = jnp.where(own, q_s[...], jnp.where(two, group, 0.0).astype(BF))
            vv = jnp.where(own, v_s[...], jnp.where(two, 1.0, 0.0).astype(BF))
            vvT = jnp.where(own_r, vT[...], jnp.where(row == aug, 1.0, 0.0).astype(BF))
            for at, n in qb:
                s = mm_t(kk, qq[at:at + n])
                e = jnp.exp2(s).astype(BF)
                oT = mm(vvT, e)
                total = oT[aug:aug + 1]
                inv = 1.0 / total
                aT = oT * inv
                attT[pl.ds(pl.multiple_of(j * pair + h * head, head), head), at:at + n] = aT[h * head:(h + 1) * head].astype(BF)
                bTn = bT[:, at:at + n].astype(F32)
                ownn = own_r[:, :n]
                rown = row[:, :n]
                rt = jnp.sum(jnp.where(ownn, bTn * aT, 0.0), axis=0, keepdims=True)
                hi = rt.astype(BF).astype(F32)
                lo = rt - hi
                baug = jnp.where(ownn, bTn, jnp.where(rown == aug, -hi, jnp.where(rown == aug + 1, -lo, 0.0))).astype(BF)
                p = e * inv.astype(BF)
                p_s[h, :, at:at + n] = p
                dp = mm(vv, baug).astype(BF)
                ds_s[h, :, at:at + n] = p * dp
            dv = mm(p_s[h], b_s[...])
            dk = mm(ds_s[h], q_s[...]) * LN2
            dqT = mm(kT[...], ds_s[h]) * (head ** -0.5)
            outs.append((dqT, dk, dv))
        dqT = jnp.where(row < head, outs[0][0], outs[1][0]).astype(BF)
        dqkv[:, cols] = dqT.T
        dqkv[:, colk] = jnp.where(lane < head, outs[0][1], outs[1][1]).astype(BF)
        dqkv[:, colv] = jnp.where(lane < head, outs[0][2], outs[1][2]).astype(BF)
        return 0

    lax.fori_loop(0, pairs, one_pair, 0)
    gp = mm(attT[...], c_ref[...])
    gq = mm(nl[...].T, dqkv[...])
    if split[0]:
        gq = gq + prev[0][...]
        gp = gp + prev[1][...]
    if split[1] is None:
        gq_ref[...] = gq
        gp_ref[...] = gp
    else:
        joined = refs[13]
        parts = split[1]
        gqT, gpT = gq.T, gp.T
        dq_rows, dp_rows = gqT.shape[0] // parts, gpT.shape[0] // parts
        for i in range(parts):
            joined[i, :dq_rows] = gqT[i * dq_rows:(i + 1) * dq_rows]
            joined[i, dq_rows:] = gpT[i * dp_rows:(i + 1) * dp_rows]
        me = odd
        for i in range(parts // 2):
            gq_ref[i] = joined[2 * i + me]
            gp_ref[i] = joined[2 * i + 1 - me].astype(BF)
    dn = mm_t(dqkv[...], wqkv_ref[...]) * gain
    normed = cen * rstd
    d = rstd * (dn - jnp.mean(dn, axis=1, keepdims=True) - normed * jnp.mean(dn * normed, axis=1, keepdims=True))
    d = d.astype(BF)
    for ref, at in zip(d_refs, starts):
        ref[...] = d[at:at + ref.shape[0]]


def window_call(pieces, metas, gain, wqkv, wproj, prev, parts):
    width = wproj.shape[0]
    head = width // HEADS
    pair = 2 * head
    sizes = [p.shape[1] for p in pieces]
    cells = sum(sizes)
    deep = 4 * width // parts if parts else 0
    if parts is None:
        sums = (jax.ShapeDtypeStruct((width, 3 * width), F32), jax.ShapeDtypeStruct((width, width), F32))
    else:
        sums = (jax.ShapeDtypeStruct((parts // 2, deep, width), F32),
                jax.ShapeDtypeStruct((parts // 2, deep, width), BF))
    scratch = ([pltpu.VMEM((cells, width), BF)] * 2
               + [pltpu.VMEM((cells, pair), BF)] * 4
               + [pltpu.VMEM((pair, cells), BF)] * 3
               + [pltpu.VMEM((2, cells, cells), BF)] * 2
               + [pltpu.VMEM((cells, 3 * width), BF), pltpu.VMEM((width, cells), BF)])
    if parts is not None:
        scratch.append(pltpu.VMEM((parts, deep, width), F32))
    vmem = pl.BlockSpec(memory_space=pltpu.VMEM)
    args = list(pieces) + [gain, wqkv, wproj] + (list(prev) if prev else [])
    outs = pl.pallas_call(
        functools.partial(window_kernel, head, metas, (prev is not None, parts)),
        out_shape=tuple(jax.ShapeDtypeStruct((n, width), BF) for n in sizes) + sums,
        in_specs=[vmem] * len(args),
        out_specs=[vmem] * (len(sizes) + 2),
        scratch_shapes=scratch,
        cost_estimate=pl.CostEstimate(
            flops=24 * cells * width * width + 12 * cells * cells * width,
            bytes_accessed=8 * 2**20,
            transcendentals=HEADS * cells * cells,
        ),
        compiler_params=pltpu.CompilerParams(vmem_limit_bytes=32 * 2**20),
    )(*args)
    return outs[:len(sizes)], outs[-2:]


def permuted(value, axes, target):
    sizes = [lax.axis_size(a) for a in axes]
    pairs = []
    for source in range(math.prod(sizes)):
        at, rest = [], source
        for size in reversed(sizes):
            at.append(rest % size)
            rest //= size
        goal = target(*reversed(at))
        if goal is None:
            continue
        flat = 0
        for size, place in zip(sizes, goal):
            flat = flat * size + place
        pairs.append((source, flat))
    return lax.ppermute(value, tuple(axes), pairs)


def shared(value, back=False, east=0):
    lats, lons = lax.axis_size("lat"), lax.axis_size("lon")
    pairs = []
    for i in range(lats):
        for j in range(lons):
            if j % 2 == 0:
                goal = (i - 1, j) if i > 0 else None
            else:
                goal = (i + 1, j) if i < lats - 1 else (i, j - 1)
            if goal is not None:
                pair = (i * lons + j, goal[0] * lons + goal[1])
                home = i * lons + (j + east) % lons
                pairs.append((pair[1], home) if back else (home, pair[1]))
    return lax.ppermute(value, ("lat", "lon"), pairs)


def along_lon(value, step):
    count = lax.axis_size("lon")
    return lax.ppermute(value, "lon", [(j, (j + step) % count) for j in range(count)])


def cut_kernel(specs, half, hid_ref, cot_ref, *outs):
    odd = lax.rem(lax.axis_index("lon"), 2)
    top = lax.axis_index("lat") == 0
    end = hid_ref.shape[1] - half
    starts = {"own": (1 - odd) * end, "sent": odd * end}
    zeroed = {"own": top & (odd == 1), "peer": top & (odd == 0)}
    for out, (rows, cols, n, pad, clear) in zip(outs, specs):
        at = starts.get(rows, rows)
        for k, ref in enumerate((hid_ref, cot_ref)):
            for b in range(hid_ref.shape[0]):
                cut = ref[b, pl.ds(at, half)].astype(F32)[:, cols:cols + n]
                if clear:
                    cut = jnp.where(zeroed[clear], 0.0, cut)
                filler = jnp.zeros((half, pad - n, cut.shape[2]), F32)
                out[k, b] = jnp.concatenate([cut, filler], axis=1).astype(BF)


def cut_call(hid, cot, specs, half):
    samples, _, _, width = hid.shape
    vmem = pl.BlockSpec(memory_space=pltpu.VMEM)
    outs = pl.pallas_call(
        functools.partial(cut_kernel, specs, half),
        out_shape=tuple(
            jax.ShapeDtypeStruct((2, samples, half, pad, width), BF) for _, _, _, pad, _ in specs
        ),
        in_specs=[vmem] * 2,
        out_specs=tuple([vmem] * len(specs)),
        cost_estimate=pl.CostEstimate(flops=0, bytes_accessed=4 * hid.size * 2, transcendentals=0),
        compiler_params=pltpu.CompilerParams(vmem_limit_bytes=40 * 2**20),
    )(hid, cot)
    return list(outs)


def cut_sent_kernel(specs, half, hid_ref, cot_ref, *refs):
    outs, (held, sems) = refs[:len(specs)], refs[len(specs):]
    samples = hid_ref.shape[0]
    at = lax.rem(lax.axis_index("lon"), 2) * (hid_ref.shape[1] - half)
    copies = [
        (k, b, pltpu.make_async_copy(ref.at[b, pl.ds(at, half)], held.at[k, b], sems.at[k, b]))
        for b in range(samples)
        for k, ref in enumerate((hid_ref, cot_ref))
    ]
    for _, _, copy in copies:
        copy.start()
    for k, b, copy in copies:
        copy.wait()
        rows = held[k, b].astype(F32)
        for out, (cols, n, pad) in zip(outs, specs):
            filler = jnp.zeros((half, pad - n, rows.shape[2]), F32)
            out[k, b] = jnp.concatenate([rows[:, cols:cols + n], filler], axis=1).astype(BF)


def cut_sent_call(hid, cot, specs, half):
    samples, _, lon_cols, width = hid.shape
    outs = pl.pallas_call(
        functools.partial(cut_sent_kernel, specs, half),
        out_shape=tuple(jax.ShapeDtypeStruct((2, samples, half, pad, width), BF) for _, _, pad in specs),
        in_specs=[pl.BlockSpec(memory_space=pl.ANY)] * 2,
        out_specs=tuple([pl.BlockSpec(memory_space=pltpu.VMEM)] * len(specs)),
        scratch_shapes=[
            pltpu.VMEM((2, samples, half, lon_cols, width), BF),
            pltpu.SemaphoreType.DMA((2, samples)),
        ],
        compiler_params=pltpu.CompilerParams(vmem_limit_bytes=60 * 2**20),
    )(hid, cot)
    return list(outs)


def scatter_direct(value, axis, dim):
    count = lax.axis_size(axis)
    me = lax.axis_index(axis)
    share = value.shape[dim] // count
    total = lax.dynamic_slice_in_dim(value, me * share, share, dim).astype(F32)
    for step in range(1, count):
        goal = (me + step) % count
        part = lax.dynamic_slice_in_dim(value, goal * share, share, dim).astype(BF)
        got = permuted(part, (axis,), lambda i, s=step: ((i + s) % count,))
        total = total + got.astype(F32)
    return total


def scatter_bit(value, axis, bit, dim):
    me = (lax.axis_index(axis) // bit) % 2
    mine = lax.dynamic_index_in_dim(value, me, dim, keepdims=False).astype(F32)
    other = lax.dynamic_index_in_dim(value, 1 - me, dim, keepdims=False).astype(BF)
    got = permuted(other, (axis,), lambda i: (i ^ bit,))
    return mine + got.astype(F32)


def reduce_weights(keep, send, lons, samples, returns):
    half, deep, width = keep.shape
    lats = lax.axis_size("lat")
    moved, waiting = [], list(returns)

    def release(value, count=1):
        for _ in range(min(count, len(waiting))):
            held, move = waiting.pop(0)
            value, held = lax.optimization_barrier((value, held))
            moved.append(move(held))
        return value

    got = permuted(send, ("lon",), lambda i: (i ^ 1,))
    keep = release(keep, len(waiting) - 2 * samples)
    early = len(moved)
    total = release((keep + got.astype(F32)).reshape(lats, lons // 2, deep, width), len(waiting) - samples)
    bit, left = 2, lons // 2
    while left > 1:
        total = scatter_bit(total.reshape(lats, left // 2, 2, deep, width), "lon", bit, 2)
        left //= 2
        bit *= 2
    total, moved[:early] = lax.optimization_barrier((total.reshape(lats, deep, width), moved[:early]))
    total = release(total, len(waiting))
    total = scatter_direct(total, "dp", 2)
    total, moved[early:] = lax.optimization_barrier((total, moved[early:]))
    return scatter_direct(total, "lat", 0)[0], moved


def per_device(hidden_in, grad_out, norm_gain, w_qkv, w_proj):
    samples, lat_rows, lon_cols, width = hidden_in.shape
    half = WIN // 2
    nr, nc = lat_rows // WIN, lon_cols // WIN
    short = half + (-half) % 16
    wide = WIN + (-WIN) % 16
    lons = lax.axis_size("lon")
    parts = lax.axis_size("lat") * lons
    if lons & (lons - 1) or lons < 2:
        raise ValueError("lon size")

    odd = lax.axis_index("lon") % 2
    inner = [wc * WIN + SHIFT for wc in range(nc - 1)]
    edge = (nc - 1) * WIN + SHIFT
    sent = cut_sent_call(hidden_in, grad_out, [(at, WIN, wide) for at in inner], half) if inner else []
    hid, cot, sent = lax.optimization_barrier((hidden_in, grad_out, sent))
    inner_in = [shared(p) for p in sent]
    specs = [("sent", 0, half, short, "peer"), ("own", 0, half, short, "")]
    specs += [("own", edge, half, short, "own"), ("sent", edge, half, short, "")]
    specs += [("own", at, WIN, wide, "own") for at in inner]
    fixed = [(2 * wr + 1 + i) * half for wr in range(nr - 1) for i in range(2)]
    specs += [(r, at, WIN, wide, "") for at in inner for r in fixed]
    specs += [(r, edge, half, short, "") for r in fixed] + [(r, 0, half, short, "") for r in fixed]
    cuts = cut_call(hid, cot, specs, half)
    side_sent, corner_sent, own_edge, edge_sent = cuts[:4]
    own_inner, rest = cuts[4:4 + len(inner)], cuts[4 + len(inner):]
    whole_inner = [[rest.pop(0) for _ in fixed] for _ in inner]
    whole_edge = [rest.pop(0) for _ in fixed]
    whole_side = [along_lon(rest.pop(0), -1) for _ in fixed]
    own_side, edge_in, corner_in = along_lon(side_sent, -1), shared(edge_sent), shared(corner_sent, east=1)

    order = [(b, wr, wc) for b in range(samples) for wc in range(nc) for wr in range(nr)]
    sums = None
    out = {}
    for step, (b, wr, wc) in enumerate(order):
        if wr < nr - 1 and wc < nc - 1:
            cells = whole_inner[wc][2 * wr:2 * wr + 2]
            metas = ((WIN, wide, False),) * 2
        elif wr < nr - 1:
            cells = [f[2 * wr + i] for i in range(2) for f in (whole_edge, whole_side)]
            metas = ((half, short, False),) * 4
        elif wc < nc - 1:
            cells = [own_inner[wc], inner_in[wc]]
            metas = ((WIN, wide, False), (WIN, wide, True))
        else:
            cells = [own_edge, own_side, edge_in, corner_in]
            metas = ((half, short, False),) * 2 + ((half, short, True),) * 2
        cells = [p[:, b].reshape(2, -1, width) for p in cells]
        done, sums = window_call(
            cells, metas, norm_gain, w_qkv, w_proj, sums, parts if step == len(order) - 1 else None
        )
        out[b, wr, wc] = [d.reshape(half, pad, width) for d, (n, pad, _) in zip(done, metas)]

    late = [(out[b, nr - 1, wc][1], lambda v: shared(v, back=True)) for b in range(samples) for wc in range(nc - 1)]
    corners = [out[b, nr - 1, nc - 1] for b in range(samples)]
    late += [(c[2], lambda v: shared(v, back=True)) for c in corners]
    late += [(c[3], lambda v: shared(v, back=True, east=1)) for c in corners]
    late += [(c[1], lambda v: along_lon(v, 1)) for c in corners]
    total, moved = reduce_weights(sums[0], sums[1], lons, samples, late)

    rows_out = []
    for b in range(samples):
        def stacked(own, back, between, upper):
            above = jnp.where(upper, own, back)
            below = jnp.where(upper, back, own)
            return jnp.concatenate([above] + between + [below], axis=0)

        columns = []
        for wc in range(nc - 1):
            own, other = out[b, nr - 1, wc]
            between = [out[b, wr, wc][i] for wr in range(nr - 1) for i in range(2)]
            columns.append(stacked(own, moved[b * (nc - 1) + wc], between, odd == 1)[:, :WIN])
        own = out[b, nr - 1, nc - 1][0]
        back, far, near = moved[samples * (nc - 1) + b::samples]
        between = [out[b, wr, nc - 1][i] for wr in range(nr - 1) for i in (0, 2)]
        columns.append(stacked(own, back, between, odd == 1)[:, :half])
        between = [along_lon(out[b, wr, nc - 1][i], 1) for wr in range(nr - 1) for i in (1, 3)]
        columns.insert(0, stacked(near, far, between, odd == 0)[:, :half])
        rows_out.append(jnp.concatenate(columns, axis=1))
    returned = jnp.stack(rows_out)
    grad_in = (grad_out.astype(F32) + returned.astype(F32)).astype(BF)
    total_cells = (
        lax.axis_size("dp") * samples * lat_rows * lax.axis_size("lat") * lon_cols * lons
    )
    factor = float(total_cells) ** (-0.5)
    total = total.T * factor
    cut = 3 * width // parts
    return (grad_in, total[:, :cut], total[:, cut:])


def solution(mesh):
    in_specs = (P("dp", "lat", "lon", None), P("dp", "lat", "lon", None), P(), P(), P())
    out_specs = (P("dp", "lat", "lon", None), P("dp", ("lat", "lon")), P("dp", ("lat", "lon")))
    return jax.shard_map(
        per_device, mesh=mesh, in_specs=in_specs, out_specs=out_specs, check_vma=False
    )
```

```python
import functools, math
import jax, jax.numpy as jnp
from jax import lax
from jax.experimental import pallas as pl
from jax.experimental.pallas import tpu as pltpu

from jax.sharding import PartitionSpec as P

HEADS = 6
WIN = 30
SHIFT = 15
EPSILON = 1e-05
BF = jnp.bfloat16
F32 = jnp.float32
LN2 = math.log(2.0)

def mm(a, b):
    return lax.dot_general(a, b, (((1,), (0,)), ((), ())), preferred_element_type=F32)

def mm_t(a, b):
    return lax.dot_general(a, b, (((1,), (1,)), ((), ())), preferred_element_type=F32)

def blocks_of(n, step):
    return [(at, min(step, n - at)) for at in range(0, n, step)]

def window_kernel(head, metas, split, *refs):
    count = len(metas)
    pieces, refs = refs[:count], refs[count:]
    gain_ref, wqkv_ref, wproj_ref = refs[:3]
    refs = refs[3:]
    if split[0]:
        prev, refs = refs[:2], refs[2:]
    d_refs, refs = refs[:count], refs[count:]
    (gq_ref, gp_ref), refs = refs[:2], refs[2:]
    c_ref, nl, q_s, k_s, v_s, b_s, kT, vT, bT, p_s, ds_s, dqkv, attT = refs[:13]
    cells, width = c_ref.shape
    pair = 2 * head
    pairs = width // pair
    qscale = head ** -0.5 / LN2
    at = 0
    starts = []
    for p in pieces:
        starts.append(at)
        c_ref[at:at + p.shape[1]] = p[1]
        at += p.shape[1]
    odd = lax.rem(lax.axis_index("lon"), 2)
    packed = jnp.where((lax.axis_index("lat") == lax.axis_size("lat") - 1) & (odd == 0), 1.0, 0.0)
    oks, seconds = [], []
    for p, (n, pad, other) in zip(pieces, metas):
        place = lax.broadcasted_iota(jnp.int32, (p.shape[1], pair), 0)
        oks.append(jnp.where(lax.rem(place, pad) < n, 1.0, 0.0))
        seconds.append(jnp.full((p.shape[1], pair), packed if other else 0.0, F32))
    valid_col = jnp.concatenate(oks, axis=0)
    second = jnp.concatenate(seconds, axis=0)
    x = jnp.concatenate([p[0] for p in pieces], axis=0).astype(F32)
    mean = jnp.mean(x, axis=1, keepdims=True)
    cen = x - mean
    rstd = lax.rsqrt(jnp.mean(cen * cen, axis=1, keepdims=True) + EPSILON)
    gain = gain_ref[...][None]
    nl[...] = (cen * rstd * gain).astype(BF)
    qb = blocks_of(cells, cells)

    def one_pair(j, _):
        cols = pl.ds(pl.multiple_of(j * pair, pair), pair)
        colk = pl.ds(pl.multiple_of(width + j * pair, pair), pair)
        colv = pl.ds(pl.multiple_of(2 * width + j * pair, pair), pair)
        q_s[...] = (mm(nl[...], wqkv_ref[:, cols]) * qscale).astype(BF)
        k_s[...] = mm(nl[...], wqkv_ref[:, colk]).astype(BF)
        v_s[...] = mm(nl[...], wqkv_ref[:, colv]).astype(BF)
        b_s[...] = mm_t(c_ref[...], wproj_ref[cols, :]).astype(BF)
        kT[...] = k_s[...].T
        vT[...] = v_s[...].T
        bT[...] = b_s[...].T
        lane = lax.broadcasted_iota(jnp.int32, (cells, pair), 1)
        row = lax.broadcasted_iota(jnp.int32, (pair, cells), 0)
        outs = []
        for h in range(2):
            own = (lane >= head) if h else (lane < head)
            own_r = (row >= head) if h else (row < head)
            aug = 0 if h else head
            seen = jnp.where(lane == aug, valid_col * (1.0 - second), valid_col * second)
            two = (lane == aug) | (lane == aug + 1)
            bias = jnp.where(two, (seen - 1.0) * 30000.0, 0.0).astype(BF)
            group = jnp.where(lane == aug, 1.0 - second, second)
            kk = jnp.where(own, k_s[...], bias)
            qq = jnp.where(own, q_s[...], jnp.where(two, group, 0.0).astype(BF))
            vv = jnp.where(own, v_s[...], jnp.where(two, 1.0, 0.0).astype(BF))
            vvT = jnp.where(own_r, vT[...], jnp.where(row == aug, 1.0, 0.0).astype(BF))
            for at, n in qb:
                s = mm_t(kk, qq[at:at + n])
                e = jnp.exp2(s).astype(BF)
                oT = mm(vvT, e)
                total = oT[aug:aug + 1]
                inv = 1.0 / total
                aT = oT * inv
                attT[pl.ds(pl.multiple_of(j * pair + h * head, head), head), at:at + n] = aT[h * head:(h + 1) * head].astype(BF)
                bTn = bT[:, at:at + n].astype(F32)
                ownn = own_r[:, :n]
                rown = row[:, :n]
                rt = jnp.sum(jnp.where(ownn, bTn * aT, 0.0), axis=0, keepdims=True)
                hi = rt.astype(BF).astype(F32)
                lo = rt - hi
                baug = jnp.where(ownn, bTn, jnp.where(rown == aug, -hi, jnp.where(rown == aug + 1, -lo, 0.0))).astype(BF)
                p = e * inv.astype(BF)
                p_s[h, :, at:at + n] = p
                dp = mm(vv, baug).astype(BF)
                ds_s[h, :, at:at + n] = p * dp
            dv = mm(p_s[h], b_s[...])
            dk = mm(ds_s[h], q_s[...]) * LN2
            dqT = mm(kT[...], ds_s[h]) * (head ** -0.5)
            outs.append((dqT, dk, dv))
        dqT = jnp.where(row < head, outs[0][0], outs[1][0]).astype(BF)
        dqkv[:, cols] = dqT.T
        dqkv[:, colk] = jnp.where(lane < head, outs[0][1], outs[1][1]).astype(BF)
        dqkv[:, colv] = jnp.where(lane < head, outs[0][2], outs[1][2]).astype(BF)
        return 0

    lax.fori_loop(0, pairs, one_pair, 0)
    gp = mm(attT[...], c_ref[...])
    gq = mm(nl[...].T, dqkv[...])
    if split[0]:
        gq = gq + prev[0][...]
        gp = gp + prev[1][...]
    if split[1] is None:
        gq_ref[...] = gq
        gp_ref[...] = gp
    else:
        joined = refs[13]
        parts = split[1]
        gqT, gpT = gq.T, gp.T
        dq_rows, dp_rows = gqT.shape[0] // parts, gpT.shape[0] // parts
        for i in range(parts):
            joined[i, :dq_rows] = gqT[i * dq_rows:(i + 1) * dq_rows]
            joined[i, dq_rows:] = gpT[i * dp_rows:(i + 1) * dp_rows]
        lats, lons = lax.axis_size("lat"), lax.axis_size("lon")
        own_lon, own_lat = lax.axis_index("lon") // 2, lax.axis_index("lat")
        for p in range(lons // 2):
            for step in range(lats):
                source = lax.rem(own_lat + step, lats) * lons + 2 * (own_lon ^ p)
                gq_ref[p * lats + step] = joined[source + odd]
                gp_ref[p * lats + step] = joined[source + 1 - odd].astype(BF)
    dn = mm_t(dqkv[...], wqkv_ref[...]) * gain
    normed = cen * rstd
    d = rstd * (dn - jnp.mean(dn, axis=1, keepdims=True) - normed * jnp.mean(dn * normed, axis=1, keepdims=True))
    d = d.astype(BF)
    for ref, at in zip(d_refs, starts):
        ref[...] = d[at:at + ref.shape[0]]


def window_call(pieces, metas, gain, wqkv, wproj, prev, parts):
    width = wproj.shape[0]
    head = width // HEADS
    pair = 2 * head
    sizes = [p.shape[1] for p in pieces]
    cells = sum(sizes)
    deep = 4 * width // parts if parts else 0
    if parts is None:
        sums = (jax.ShapeDtypeStruct((width, 3 * width), F32), jax.ShapeDtypeStruct((width, width), F32))
    else:
        sums = (jax.ShapeDtypeStruct((parts // 2, deep, width), F32),
                jax.ShapeDtypeStruct((parts // 2, deep, width), BF))
    scratch = ([pltpu.VMEM((cells, width), BF)] * 2
               + [pltpu.VMEM((cells, pair), BF)] * 4
               + [pltpu.VMEM((pair, cells), BF)] * 3
               + [pltpu.VMEM((2, cells, cells), BF)] * 2
               + [pltpu.VMEM((cells, 3 * width), BF), pltpu.VMEM((width, cells), BF)])
    if parts is not None:
        scratch.append(pltpu.VMEM((parts, deep, width), F32))
    vmem = pl.BlockSpec(memory_space=pltpu.VMEM)
    args = list(pieces) + [gain, wqkv, wproj] + (list(prev) if prev else [])
    outs = pl.pallas_call(
        functools.partial(window_kernel, head, metas, (prev is not None, parts)),
        out_shape=tuple(jax.ShapeDtypeStruct((n, width), BF) for n in sizes) + sums,
        in_specs=[vmem] * len(args),
        out_specs=[vmem] * (len(sizes) + 2),
        scratch_shapes=scratch,
        cost_estimate=pl.CostEstimate(
            flops=24 * cells * width * width + 12 * cells * cells * width,
            bytes_accessed=8 * 2**20,
            transcendentals=HEADS * cells * cells,
        ),
        compiler_params=pltpu.CompilerParams(vmem_limit_bytes=32 * 2**20),
    )(*args)
    return outs[:len(sizes)], outs[-2:]


def permuted(value, axes, target):
    sizes = [lax.axis_size(a) for a in axes]
    pairs = []
    for source in range(math.prod(sizes)):
        at, rest = [], source
        for size in reversed(sizes):
            at.append(rest % size)
            rest //= size
        goal = target(*reversed(at))
        if goal is None:
            continue
        flat = 0
        for size, place in zip(sizes, goal):
            flat = flat * size + place
        pairs.append((source, flat))
    return lax.ppermute(value, tuple(axes), pairs)


def shared(value, back=False, east=0):
    lats, lons = lax.axis_size("lat"), lax.axis_size("lon")
    pairs = []
    for i in range(lats):
        for j in range(lons):
            if j % 2 == 0:
                goal = (i - 1, j) if i > 0 else None
            else:
                goal = (i + 1, j) if i < lats - 1 else (i, j - 1)
            if goal is not None:
                pair = (i * lons + j, goal[0] * lons + goal[1])
                home = i * lons + (j + east) % lons
                pairs.append((pair[1], home) if back else (home, pair[1]))
    return lax.ppermute(value, ("lat", "lon"), pairs)


def along_lon(value, step):
    count = lax.axis_size("lon")
    return lax.ppermute(value, "lon", [(j, (j + step) % count) for j in range(count)])


def cut_kernel(specs, half, hid_ref, cot_ref, *outs):
    odd = lax.rem(lax.axis_index("lon"), 2)
    top = lax.axis_index("lat") == 0
    end = hid_ref.shape[1] - half
    starts = {"own": (1 - odd) * end, "sent": odd * end}
    zeroed = {"own": top & (odd == 1), "peer": top & (odd == 0)}
    for out, (rows, cols, n, pad, clear) in zip(outs, specs):
        at = starts.get(rows, rows)
        for k, ref in enumerate((hid_ref, cot_ref)):
            for b in range(hid_ref.shape[0]):
                cut = ref[b, pl.ds(at, half)].astype(F32)[:, cols:cols + n]
                if clear:
                    cut = jnp.where(zeroed[clear], 0.0, cut)
                filler = jnp.zeros((half, pad - n, cut.shape[2]), F32)
                out[k, b] = jnp.concatenate([cut, filler], axis=1).astype(BF)


def cut_call(hid, cot, specs, half):
    samples, _, _, width = hid.shape
    vmem = pl.BlockSpec(memory_space=pltpu.VMEM)
    outs = pl.pallas_call(
        functools.partial(cut_kernel, specs, half),
        out_shape=tuple(
            jax.ShapeDtypeStruct((2, samples, half, pad, width), BF) for _, _, _, pad, _ in specs
        ),
        in_specs=[vmem] * 2,
        out_specs=tuple([vmem] * len(specs)),
        cost_estimate=pl.CostEstimate(flops=0, bytes_accessed=4 * hid.size * 2, transcendentals=0),
        compiler_params=pltpu.CompilerParams(vmem_limit_bytes=40 * 2**20),
    )(hid, cot)
    return list(outs)


def reduce_weights(keep, send, lons, returns):
    _, _, width = keep.shape
    lats, dps = lax.axis_size("lat"), lax.axis_size("dp")
    moved, waiting = [], list(returns)

    def release(value, count):
        for _ in range(min(count, len(waiting))):
            held, move = waiting.pop(0)
            value, held = lax.optimization_barrier((value, held))
            moved.append(move(held))
        return value

    got = permuted(send, ("lon",), lambda i: (i ^ 1,))
    keep = release(keep, len(waiting) // 2)
    early = len(moved)
    got = release(got, len(waiting))
    total = [keep[i * lats:(i + 1) * lats] + got[i * lats:(i + 1) * lats].astype(F32) for i in range(lons // 2)]
    while len(total) > 1:
        left = len(total) // 2
        payload = jnp.concatenate(total[left:], axis=0).astype(BF)
        got = permuted(payload, ("lon",), lambda i, bit=2 * left: (i ^ bit,))
        if left == 1:
            got, moved[:early] = lax.optimization_barrier((got, moved[:early]))
        total = [total[i] + got[i * lats:(i + 1) * lats].astype(F32) for i in range(left)]
    total = total[0]

    share = width // dps
    me, mine = lax.axis_index("dp"), None
    for step in range(1, dps):
        part = lax.dynamic_slice_in_dim(total, ((me + step) % dps) * share, share, 2).astype(BF)
        got = permuted(part, ("dp",), lambda i, step=step: ((i + step) % dps,))
        if step == dps - 1:
            got, moved[early:] = lax.optimization_barrier((got, moved[early:]))
        mine = got.astype(F32) if mine is None else mine + got.astype(F32)
    own = lax.dynamic_slice_in_dim(total, me * share, share, 2)
    total = own if mine is None else own + mine

    mine = total[0]
    for step in range(1, lats):
        got = permuted(total[step].astype(BF), ("lat",), lambda i, step=step: ((i + step) % lats,))
        mine = mine + got.astype(F32)
    return mine, moved


def per_device(hidden_in, grad_out, norm_gain, w_qkv, w_proj):
    samples, lat_rows, lon_cols, width = hidden_in.shape
    half = WIN // 2
    nr, nc = lat_rows // WIN, lon_cols // WIN
    short = half + (-half) % 16
    wide = WIN + (-WIN) % 16
    lons = lax.axis_size("lon")
    parts = lax.axis_size("lat") * lons
    if lons & (lons - 1) or lons < 2:
        raise ValueError("lon size")

    odd = lax.axis_index("lon") % 2
    inner = [wc * WIN + SHIFT for wc in range(nc - 1)]
    edge = (nc - 1) * WIN + SHIFT
    sent = cut_call(hidden_in, grad_out, [("sent", at, WIN, wide, "") for at in inner], half) if inner else []
    hid, cot, sent = lax.optimization_barrier((hidden_in, grad_out, sent))
    inner_in = [shared(p) for p in sent]
    specs = [("sent", 0, half, short, "peer"), ("own", 0, half, short, "")]
    specs += [("own", edge, half, short, "own"), ("sent", edge, half, short, "")]
    specs += [("own", at, WIN, wide, "own") for at in inner]
    fixed = [(2 * wr + 1 + i) * half for wr in range(nr - 1) for i in range(2)]
    specs += [(r, at, WIN, wide, "") for at in inner for r in fixed]
    specs += [(r, edge, half, short, "") for r in fixed] + [(r, 0, half, short, "") for r in fixed]
    cuts = cut_call(hid, cot, specs, half)
    side_sent, corner_sent, own_edge, edge_sent = cuts[:4]
    own_inner, rest = cuts[4:4 + len(inner)], cuts[4 + len(inner):]
    whole_inner = [[rest.pop(0) for _ in fixed] for _ in inner]
    whole_edge = [rest.pop(0) for _ in fixed]
    whole_side = [along_lon(rest.pop(0), -1) for _ in fixed]
    own_side, edge_in, corner_in = along_lon(side_sent, -1), shared(edge_sent), shared(corner_sent, east=1)

    order = [(b, wr, wc) for b in range(samples) for wc in range(nc) for wr in range(nr)]
    sums = None
    out = {}
    for step, (b, wr, wc) in enumerate(order):
        if wr < nr - 1 and wc < nc - 1:
            cells = whole_inner[wc][2 * wr:2 * wr + 2]
            metas = ((WIN, wide, False),) * 2
        elif wr < nr - 1:
            cells = [f[2 * wr + i] for i in range(2) for f in (whole_edge, whole_side)]
            metas = ((half, short, False),) * 4
        elif wc < nc - 1:
            cells = [own_inner[wc], inner_in[wc]]
            metas = ((WIN, wide, False), (WIN, wide, True))
        else:
            cells = [own_edge, own_side, edge_in, corner_in]
            metas = ((half, short, False),) * 2 + ((half, short, True),) * 2
        cells = [p[:, b].reshape(2, -1, width) for p in cells]
        done, sums = window_call(
            cells, metas, norm_gain, w_qkv, w_proj, sums, parts if step == len(order) - 1 else None
        )
        out[b, wr, wc] = [d.reshape(half, pad, width) for d, (n, pad, _) in zip(done, metas)]

    late = [(out[b, nr - 1, wc][1], lambda v: shared(v, back=True)) for b in range(samples) for wc in range(nc - 1)]
    for b in range(samples):
        own, own_lon, other, other_lon = out[b, nr - 1, nc - 1]
        late.append((other, lambda v: shared(v, back=True)))
        late.append((other_lon, lambda v: shared(v, back=True, east=1)))
        late.append((own_lon, lambda v: along_lon(v, 1)))
    total, moved = reduce_weights(sums[0], sums[1], lons, late)

    rows_out = []
    for b in range(samples):
        def stacked(own, back, between, upper):
            above = jnp.where(upper, own, back)
            below = jnp.where(upper, back, own)
            return jnp.concatenate([above] + between + [below], axis=0)

        columns = []
        for wc in range(nc - 1):
            own, other = out[b, nr - 1, wc]
            between = [out[b, wr, wc][i] for wr in range(nr - 1) for i in range(2)]
            columns.append(stacked(own, moved[b * (nc - 1) + wc], between, odd == 1)[:, :WIN])
        own = out[b, nr - 1, nc - 1][0]
        back, far, near = moved[samples * (nc - 1) + 3 * b:][:3]
        between = [out[b, wr, nc - 1][i] for wr in range(nr - 1) for i in (0, 2)]
        columns.append(stacked(own, back, between, odd == 1)[:, :half])
        between = [along_lon(out[b, wr, nc - 1][i], 1) for wr in range(nr - 1) for i in (1, 3)]
        columns.insert(0, stacked(near, far, between, odd == 0)[:, :half])
        rows_out.append(jnp.concatenate(columns, axis=1))
    returned = jnp.stack(rows_out)
    grad_in = (grad_out.astype(F32) + returned.astype(F32)).astype(BF)
    total_cells = (
        lax.axis_size("dp") * samples * lat_rows * lax.axis_size("lat") * lon_cols * lons
    )
    factor = float(total_cells) ** (-0.5)
    cut = 3 * width // parts
    return (grad_in, total[:cut].T * factor, total[cut:].T * factor)


def solution(mesh):
    in_specs = (P("dp", "lat", "lon", None), P("dp", "lat", "lon", None), P(), P(), P())
    out_specs = (P("dp", "lat", "lon", None), P("dp", ("lat", "lon")), P("dp", ("lat", "lon")))
    return jax.shard_map(
        per_device, mesh=mesh, in_specs=in_specs, out_specs=out_specs, check_vma=False
    )
```

```python
import functools, math
import jax, jax.numpy as jnp
from jax import lax
from jax.experimental import pallas as pl
from jax.experimental.pallas import tpu as pltpu

from jax.sharding import PartitionSpec as P

HEADS = 6
WIN = 30
SHIFT = 15
EPSILON = 1e-05
BF = jnp.bfloat16
F32 = jnp.float32
LN2 = math.log(2.0)

def mm(a, b):
    return lax.dot_general(a, b, (((1,), (0,)), ((), ())), preferred_element_type=F32)

def mm_t(a, b):
    return lax.dot_general(a, b, (((1,), (1,)), ((), ())), preferred_element_type=F32)

def blocks_of(n, step):
    return [(at, min(step, n - at)) for at in range(0, n, step)]

def window_kernel(head, metas, split, *refs):
    count = len(metas)
    pieces, refs = refs[:count], refs[count:]
    gain_ref, wqkv_ref, wproj_ref = refs[:3]
    refs = refs[3:]
    if split[0]:
        prev, refs = refs[:2], refs[2:]
    d_refs, refs = refs[:count], refs[count:]
    (gq_ref, gp_ref), refs = refs[:2], refs[2:]
    c_ref, nl, q_s, k_s, v_s, b_s, kT, vT, bT, p_s, ds_s, dqkv, attT = refs[:13]
    cells, width = c_ref.shape
    pair = 2 * head
    pairs = width // pair
    qscale = head ** -0.5 / LN2
    at = 0
    starts = []
    for p in pieces:
        starts.append(at)
        c_ref[at:at + p.shape[1]] = p[1]
        at += p.shape[1]
    odd = lax.rem(lax.axis_index("lon"), 2)
    packed = jnp.where((lax.axis_index("lat") == lax.axis_size("lat") - 1) & (odd == 0), 1.0, 0.0)
    oks, seconds = [], []
    for p, (n, pad, other) in zip(pieces, metas):
        place = lax.broadcasted_iota(jnp.int32, (p.shape[1], pair), 0)
        oks.append(jnp.where(lax.rem(place, pad) < n, 1.0, 0.0))
        seconds.append(jnp.full((p.shape[1], pair), packed if other else 0.0, F32))
    valid_col = jnp.concatenate(oks, axis=0)
    second = jnp.concatenate(seconds, axis=0)
    x = jnp.concatenate([p[0] for p in pieces], axis=0).astype(F32)
    mean = jnp.mean(x, axis=1, keepdims=True)
    cen = x - mean
    rstd = lax.rsqrt(jnp.mean(cen * cen, axis=1, keepdims=True) + EPSILON)
    gain = gain_ref[...][None]
    nl[...] = (cen * rstd * gain).astype(BF)
    qb = blocks_of(cells, cells)

    def one_pair(j, _):
        cols = pl.ds(pl.multiple_of(j * pair, pair), pair)
        colk = pl.ds(pl.multiple_of(width + j * pair, pair), pair)
        colv = pl.ds(pl.multiple_of(2 * width + j * pair, pair), pair)
        q_s[...] = (mm(nl[...], wqkv_ref[:, cols]) * qscale).astype(BF)
        k_s[...] = mm(nl[...], wqkv_ref[:, colk]).astype(BF)
        v_s[...] = mm(nl[...], wqkv_ref[:, colv]).astype(BF)
        b_s[...] = mm_t(c_ref[...], wproj_ref[cols, :]).astype(BF)
        kT[...] = k_s[...].T
        vT[...] = v_s[...].T
        bT[...] = b_s[...].T
        lane = lax.broadcasted_iota(jnp.int32, (cells, pair), 1)
        row = lax.broadcasted_iota(jnp.int32, (pair, cells), 0)
        outs = []
        for h in range(2):
            own = (lane >= head) if h else (lane < head)
            own_r = (row >= head) if h else (row < head)
            aug = 0 if h else head
            seen = jnp.where(lane == aug, valid_col * (1.0 - second), valid_col * second)
            two = (lane == aug) | (lane == aug + 1)
            bias = jnp.where(two, (seen - 1.0) * 30000.0, 0.0).astype(BF)
            group = jnp.where(lane == aug, 1.0 - second, second)
            kk = jnp.where(own, k_s[...], bias)
            qq = jnp.where(own, q_s[...], jnp.where(two, group, 0.0).astype(BF))
            vv = jnp.where(own, v_s[...], jnp.where(two, 1.0, 0.0).astype(BF))
            vvT = jnp.where(own_r, vT[...], jnp.where(row == aug, 1.0, 0.0).astype(BF))
            for at, n in qb:
                s = mm_t(kk, qq[at:at + n])
                e = jnp.exp2(s).astype(BF)
                oT = mm(vvT, e)
                total = oT[aug:aug + 1]
                inv = 1.0 / total
                aT = oT * inv
                attT[pl.ds(pl.multiple_of(j * pair + h * head, head), head), at:at + n] = aT[h * head:(h + 1) * head].astype(BF)
                bTn = bT[:, at:at + n].astype(F32)
                ownn = own_r[:, :n]
                rown = row[:, :n]
                rt = jnp.sum(jnp.where(ownn, bTn * aT, 0.0), axis=0, keepdims=True)
                hi = rt.astype(BF).astype(F32)
                lo = rt - hi
                baug = jnp.where(ownn, bTn, jnp.where(rown == aug, -hi, jnp.where(rown == aug + 1, -lo, 0.0))).astype(BF)
                p = e * inv.astype(BF)
                p_s[h, :, at:at + n] = p
                dp = mm(vv, baug).astype(BF)
                ds_s[h, :, at:at + n] = p * dp
            dv = mm(p_s[h], b_s[...])
            dk = mm(ds_s[h], q_s[...]) * LN2
            dqT = mm(kT[...], ds_s[h]) * (head ** -0.5)
            outs.append((dqT, dk, dv))
        dqT = jnp.where(row < head, outs[0][0], outs[1][0]).astype(BF)
        dqkv[:, cols] = dqT.T
        dqkv[:, colk] = jnp.where(lane < head, outs[0][1], outs[1][1]).astype(BF)
        dqkv[:, colv] = jnp.where(lane < head, outs[0][2], outs[1][2]).astype(BF)
        return 0

    lax.fori_loop(0, pairs, one_pair, 0)
    gp = mm(attT[...], c_ref[...])
    gq = mm(nl[...].T, dqkv[...])
    if split[0]:
        gq = gq + prev[0][...]
        gp = gp + prev[1][...]
    if split[1] is None:
        gq_ref[...] = gq
        gp_ref[...] = gp
    else:
        joined = refs[13]
        parts = split[1]
        gqT, gpT = gq.T, gp.T
        dq_rows, dp_rows = gqT.shape[0] // parts, gpT.shape[0] // parts
        for i in range(parts):
            joined[i, :dq_rows] = gqT[i * dq_rows:(i + 1) * dq_rows]
            joined[i, dq_rows:] = gpT[i * dp_rows:(i + 1) * dp_rows]
        lats, lons = lax.axis_size("lat"), lax.axis_size("lon")
        own_lon, own_lat = lax.axis_index("lon") // 2, lax.axis_index("lat")
        for p in range(lons // 2):
            for step in range(lats):
                source = lax.rem(own_lat + step, lats) * lons + 2 * (own_lon ^ p)
                gq_ref[p * lats + step] = joined[source + odd]
                gp_ref[p * lats + step] = joined[source + 1 - odd].astype(BF)
    dn = mm_t(dqkv[...], wqkv_ref[...]) * gain
    normed = cen * rstd
    d = rstd * (dn - jnp.mean(dn, axis=1, keepdims=True) - normed * jnp.mean(dn * normed, axis=1, keepdims=True))
    d = d.astype(BF)
    for ref, at in zip(d_refs, starts):
        ref[...] = d[at:at + ref.shape[0]]


def window_call(pieces, metas, gain, wqkv, wproj, prev, parts):
    width = wproj.shape[0]
    head = width // HEADS
    pair = 2 * head
    sizes = [p.shape[1] for p in pieces]
    cells = sum(sizes)
    deep = 4 * width // parts if parts else 0
    if parts is None:
        sums = (jax.ShapeDtypeStruct((width, 3 * width), F32), jax.ShapeDtypeStruct((width, width), F32))
    else:
        sums = (jax.ShapeDtypeStruct((parts // 2, deep, width), F32),
                jax.ShapeDtypeStruct((parts // 2, deep, width), BF))
    scratch = ([pltpu.VMEM((cells, width), BF)] * 2
               + [pltpu.VMEM((cells, pair), BF)] * 4
               + [pltpu.VMEM((pair, cells), BF)] * 3
               + [pltpu.VMEM((2, cells, cells), BF)] * 2
               + [pltpu.VMEM((cells, 3 * width), BF), pltpu.VMEM((width, cells), BF)])
    if parts is not None:
        scratch.append(pltpu.VMEM((parts, deep, width), F32))
    vmem = pl.BlockSpec(memory_space=pltpu.VMEM)
    args = list(pieces) + [gain, wqkv, wproj] + (list(prev) if prev else [])
    outs = pl.pallas_call(
        functools.partial(window_kernel, head, metas, (prev is not None, parts)),
        out_shape=tuple(jax.ShapeDtypeStruct((n, width), BF) for n in sizes) + sums,
        in_specs=[vmem] * len(args),
        out_specs=[vmem] * (len(sizes) + 2),
        scratch_shapes=scratch,
        cost_estimate=pl.CostEstimate(
            flops=24 * cells * width * width + 12 * cells * cells * width,
            bytes_accessed=8 * 2**20,
            transcendentals=HEADS * cells * cells,
        ),
        compiler_params=pltpu.CompilerParams(vmem_limit_bytes=32 * 2**20),
    )(*args)
    return outs[:len(sizes)], outs[-2:]


def permuted(value, axes, target):
    sizes = [lax.axis_size(a) for a in axes]
    pairs = []
    for source in range(math.prod(sizes)):
        at, rest = [], source
        for size in reversed(sizes):
            at.append(rest % size)
            rest //= size
        goal = target(*reversed(at))
        if goal is None:
            continue
        flat = 0
        for size, place in zip(sizes, goal):
            flat = flat * size + place
        pairs.append((source, flat))
    return lax.ppermute(value, tuple(axes), pairs)


def shared(value, back=False, east=0):
    lats, lons = lax.axis_size("lat"), lax.axis_size("lon")
    pairs = []
    for i in range(lats):
        for j in range(lons):
            if j % 2 == 0:
                goal = (i - 1, j) if i > 0 else None
            else:
                goal = (i + 1, j) if i < lats - 1 else (i, j - 1)
            if goal is not None:
                pair = (i * lons + j, goal[0] * lons + goal[1])
                home = i * lons + (j + east) % lons
                pairs.append((pair[1], home) if back else (home, pair[1]))
    return lax.ppermute(value, ("lat", "lon"), pairs)


def along_lon(value, step):
    count = lax.axis_size("lon")
    return lax.ppermute(value, "lon", [(j, (j + step) % count) for j in range(count)])


def cut_kernel(specs, half, hid_ref, cot_ref, *outs):
    odd = lax.rem(lax.axis_index("lon"), 2)
    top = lax.axis_index("lat") == 0
    end = hid_ref.shape[1] - half
    starts = {"own": (1 - odd) * end, "sent": odd * end}
    zeroed = {"own": top & (odd == 1), "peer": top & (odd == 0)}
    for out, (rows, cols, n, pad, clear) in zip(outs, specs):
        at = starts.get(rows, rows)
        for k, ref in enumerate((hid_ref, cot_ref)):
            for b in range(hid_ref.shape[0]):
                cut = ref[b, pl.ds(at, half)].astype(F32)[:, cols:cols + n]
                if clear:
                    cut = jnp.where(zeroed[clear], 0.0, cut)
                filler = jnp.zeros((half, pad - n, cut.shape[2]), F32)
                out[k, b] = jnp.concatenate([cut, filler], axis=1).astype(BF)


def cut_call(hid, cot, specs, half):
    samples, _, _, width = hid.shape
    vmem = pl.BlockSpec(memory_space=pltpu.VMEM)
    outs = pl.pallas_call(
        functools.partial(cut_kernel, specs, half),
        out_shape=tuple(
            jax.ShapeDtypeStruct((2, samples, half, pad, width), BF) for _, _, _, pad, _ in specs
        ),
        in_specs=[vmem] * 2,
        out_specs=tuple([vmem] * len(specs)),
        cost_estimate=pl.CostEstimate(flops=0, bytes_accessed=4 * hid.size * 2, transcendentals=0),
        compiler_params=pltpu.CompilerParams(vmem_limit_bytes=40 * 2**20),
    )(hid, cot)
    return list(outs)


def reduce_weights(keep, send, lons, returns):
    _, _, width = keep.shape
    lats, dps = lax.axis_size("lat"), lax.axis_size("dp")
    moved, waiting = [], list(returns)

    def release(value, count):
        for _ in range(min(count, len(waiting))):
            held, move = waiting.pop(0)
            value, held = lax.optimization_barrier((value, held))
            moved.append(move(held))
        return value

    got = permuted(send, ("lon",), lambda i: (i ^ 1,))
    keep = release(keep, len(waiting) // 2)
    got = release(got, len(waiting))
    total = [keep[i * lats:(i + 1) * lats] + got[i * lats:(i + 1) * lats].astype(F32) for i in range(lons // 2)]
    while len(total) > 2:
        left = len(total) // 2
        payload = jnp.concatenate(total[left:], axis=0).astype(BF)
        got = permuted(payload, ("lon",), lambda i, bit=2 * left: (i ^ bit,))
        total = [total[i] + got[i * lats:(i + 1) * lats].astype(F32) for i in range(left)]

    share = width // dps
    me = lax.axis_index("dp")
    arrived = []
    for pair in range(len(total)):
        for step in range(dps):
            if pair == 0 and step == 0:
                continue
            part = lax.dynamic_slice_in_dim(total[pair], ((me + step) % dps) * share, share, 2).astype(BF)
            arrived.append(
                permuted(part, ("dp", "lon"), lambda d, j, s=step, p=pair: ((d + s) % dps, j ^ (2 * p)))
            )
    arrived, moved = lax.optimization_barrier((arrived, moved))
    total = lax.dynamic_slice_in_dim(total[0], me * share, share, 2)
    for got in arrived:
        total = total + got.astype(F32)

    mine = total[0]
    for step in range(1, lats):
        got = permuted(total[step].astype(BF), ("lat",), lambda i, step=step: ((i + step) % lats,))
        mine = mine + got.astype(F32)
    return mine, moved


def per_device(hidden_in, grad_out, norm_gain, w_qkv, w_proj):
    samples, lat_rows, lon_cols, width = hidden_in.shape
    half = WIN // 2
    nr, nc = lat_rows // WIN, lon_cols // WIN
    short = half + (-half) % 16
    wide = WIN + (-WIN) % 16
    lons = lax.axis_size("lon")
    parts = lax.axis_size("lat") * lons
    if lons & (lons - 1) or lons < 2:
        raise ValueError("lon size")

    odd = lax.axis_index("lon") % 2
    inner = [wc * WIN + SHIFT for wc in range(nc - 1)]
    edge = (nc - 1) * WIN + SHIFT
    sent = cut_call(hidden_in, grad_out, [("sent", at, WIN, wide, "") for at in inner], half) if inner else []
    hid, cot, sent = lax.optimization_barrier((hidden_in, grad_out, sent))
    inner_in = [shared(p) for p in sent]
    specs = [("sent", 0, half, short, "peer"), ("own", 0, half, short, "")]
    specs += [("own", edge, half, short, "own"), ("sent", edge, half, short, "")]
    specs += [("own", at, WIN, wide, "own") for at in inner]
    fixed = [(2 * wr + 1 + i) * half for wr in range(nr - 1) for i in range(2)]
    specs += [(r, at, WIN, wide, "") for at in inner for r in fixed]
    specs += [(r, edge, half, short, "") for r in fixed] + [(r, 0, half, short, "") for r in fixed]
    cuts = cut_call(hid, cot, specs, half)
    side_sent, corner_sent, own_edge, edge_sent = cuts[:4]
    own_inner, rest = cuts[4:4 + len(inner)], cuts[4 + len(inner):]
    whole_inner = [[rest.pop(0) for _ in fixed] for _ in inner]
    whole_edge = [rest.pop(0) for _ in fixed]
    whole_side = [along_lon(rest.pop(0), -1) for _ in fixed]
    own_side, edge_in, corner_in = along_lon(side_sent, -1), shared(edge_sent), shared(corner_sent, east=1)

    order = [(b, wr, wc) for b in range(samples) for wc in range(nc) for wr in range(nr)]
    sums = None
    out = {}
    for step, (b, wr, wc) in enumerate(order):
        if wr < nr - 1 and wc < nc - 1:
            cells = whole_inner[wc][2 * wr:2 * wr + 2]
            metas = ((WIN, wide, False),) * 2
        elif wr < nr - 1:
            cells = [f[2 * wr + i] for i in range(2) for f in (whole_edge, whole_side)]
            metas = ((half, short, False),) * 4
        elif wc < nc - 1:
            cells = [own_inner[wc], inner_in[wc]]
            metas = ((WIN, wide, False), (WIN, wide, True))
        else:
            cells = [own_edge, own_side, edge_in, corner_in]
            metas = ((half, short, False),) * 2 + ((half, short, True),) * 2
        cells = [p[:, b].reshape(2, -1, width) for p in cells]
        done, sums = window_call(
            cells, metas, norm_gain, w_qkv, w_proj, sums, parts if step == len(order) - 1 else None
        )
        out[b, wr, wc] = [d.reshape(half, pad, width) for d, (n, pad, _) in zip(done, metas)]

    late = [(out[b, nr - 1, wc][1], lambda v: shared(v, back=True)) for b in range(samples) for wc in range(nc - 1)]
    for b in range(samples):
        own, own_lon, other, other_lon = out[b, nr - 1, nc - 1]
        late.append((other, lambda v: shared(v, back=True)))
        late.append((other_lon, lambda v: shared(v, back=True, east=1)))
        late.append((own_lon, lambda v: along_lon(v, 1)))
    total, moved = reduce_weights(sums[0], sums[1], lons, late)

    rows_out = []
    for b in range(samples):
        def stacked(own, back, between, upper):
            above = jnp.where(upper, own, back)
            below = jnp.where(upper, back, own)
            return jnp.concatenate([above] + between + [below], axis=0)

        columns = []
        for wc in range(nc - 1):
            own, other = out[b, nr - 1, wc]
            between = [out[b, wr, wc][i] for wr in range(nr - 1) for i in range(2)]
            columns.append(stacked(own, moved[b * (nc - 1) + wc], between, odd == 1)[:, :WIN])
        own = out[b, nr - 1, nc - 1][0]
        back, far, near = moved[samples * (nc - 1) + 3 * b:][:3]
        between = [out[b, wr, nc - 1][i] for wr in range(nr - 1) for i in (0, 2)]
        columns.append(stacked(own, back, between, odd == 1)[:, :half])
        between = [along_lon(out[b, wr, nc - 1][i], 1) for wr in range(nr - 1) for i in (1, 3)]
        columns.insert(0, stacked(near, far, between, odd == 0)[:, :half])
        rows_out.append(jnp.concatenate(columns, axis=1))
    returned = jnp.stack(rows_out)
    grad_in = (grad_out.astype(F32) + returned.astype(F32)).astype(BF)
    total_cells = (
        lax.axis_size("dp") * samples * lat_rows * lax.axis_size("lat") * lon_cols * lons
    )
    factor = float(total_cells) ** (-0.5)
    cut = 3 * width // parts
    return (grad_in, total[:cut].T * factor, total[cut:].T * factor)


def solution(mesh):
    in_specs = (P("dp", "lat", "lon", None), P("dp", "lat", "lon", None), P(), P(), P())
    out_specs = (P("dp", "lat", "lon", None), P("dp", ("lat", "lon")), P("dp", ("lat", "lon")))
    return jax.shard_map(
        per_device, mesh=mesh, in_specs=in_specs, out_specs=out_specs, check_vma=False
    )
```

```python
import functools, math
import jax, jax.numpy as jnp
from jax import lax
from jax.experimental import pallas as pl
from jax.experimental.pallas import tpu as pltpu

from jax.sharding import PartitionSpec as P

HEADS = 6
WIN = 30
SHIFT = 15
EPSILON = 1e-05
BF = jnp.bfloat16
F32 = jnp.float32
LN2 = math.log(2.0)

def mm(a, b):
    return lax.dot_general(a, b, (((1,), (0,)), ((), ())), preferred_element_type=F32)

def mm_t(a, b):
    return lax.dot_general(a, b, (((1,), (1,)), ((), ())), preferred_element_type=F32)

def blocks_of(n, step):
    return [(at, min(step, n - at)) for at in range(0, n, step)]

def window_kernel(head, metas, split, *refs):
    count = len(metas)
    pieces, refs = refs[:count], refs[count:]
    gain_ref, wqkv_ref, wproj_ref = refs[:3]
    refs = refs[3:]
    if split[0]:
        prev, refs = refs[:2], refs[2:]
    d_refs, refs = refs[:count], refs[count:]
    (gq_ref, gp_ref), refs = refs[:2], refs[2:]
    c_ref, nl, q_s, k_s, v_s, b_s, kT, vT, bT, p_s, ds_s, dqkv, attT = refs[:13]
    cells, width = c_ref.shape
    pair = 2 * head
    pairs = width // pair
    qscale = head ** -0.5 / LN2
    at = 0
    starts = []
    for p in pieces:
        starts.append(at)
        c_ref[at:at + p.shape[1]] = p[1]
        at += p.shape[1]
    odd = lax.rem(lax.axis_index("lon"), 2)
    packed = jnp.where((lax.axis_index("lat") == lax.axis_size("lat") - 1) & (odd == 0), 1.0, 0.0)
    oks, seconds = [], []
    for p, (n, pad, other) in zip(pieces, metas):
        place = lax.broadcasted_iota(jnp.int32, (p.shape[1], pair), 0)
        oks.append(jnp.where(lax.rem(place, pad) < n, 1.0, 0.0))
        seconds.append(jnp.full((p.shape[1], pair), packed if other else 0.0, F32))
    valid_col = jnp.concatenate(oks, axis=0)
    second = jnp.concatenate(seconds, axis=0)
    x = jnp.concatenate([p[0] for p in pieces], axis=0).astype(F32)
    mean = jnp.mean(x, axis=1, keepdims=True)
    cen = x - mean
    rstd = lax.rsqrt(jnp.mean(cen * cen, axis=1, keepdims=True) + EPSILON)
    gain = gain_ref[...][None]
    nl[...] = (cen * rstd * gain).astype(BF)
    qb = blocks_of(cells, cells)

    def one_pair(j, _):
        cols = pl.ds(pl.multiple_of(j * pair, pair), pair)
        colk = pl.ds(pl.multiple_of(width + j * pair, pair), pair)
        colv = pl.ds(pl.multiple_of(2 * width + j * pair, pair), pair)
        q_s[...] = (mm(nl[...], wqkv_ref[:, cols]) * qscale).astype(BF)
        k_s[...] = mm(nl[...], wqkv_ref[:, colk]).astype(BF)
        v_s[...] = mm(nl[...], wqkv_ref[:, colv]).astype(BF)
        b_s[...] = mm_t(c_ref[...], wproj_ref[cols, :]).astype(BF)
        kT[...] = k_s[...].T
        vT[...] = v_s[...].T
        bT[...] = b_s[...].T
        lane = lax.broadcasted_iota(jnp.int32, (cells, pair), 1)
        row = lax.broadcasted_iota(jnp.int32, (pair, cells), 0)
        outs = []
        for h in range(2):
            own = (lane >= head) if h else (lane < head)
            own_r = (row >= head) if h else (row < head)
            aug = 0 if h else head
            seen = jnp.where(lane == aug, valid_col * (1.0 - second), valid_col * second)
            two = (lane == aug) | (lane == aug + 1)
            bias = jnp.where(two, (seen - 1.0) * 30000.0, 0.0).astype(BF)
            group = jnp.where(lane == aug, 1.0 - second, second)
            kk = jnp.where(own, k_s[...], bias)
            qq = jnp.where(own, q_s[...], jnp.where(two, group, 0.0).astype(BF))
            vv = jnp.where(own, v_s[...], jnp.where(two, 1.0, 0.0).astype(BF))
            vvT = jnp.where(own_r, vT[...], jnp.where(row == aug, 1.0, 0.0).astype(BF))
            for at, n in qb:
                s = mm_t(kk, qq[at:at + n])
                e = jnp.exp2(s).astype(BF)
                oT = mm(vvT, e)
                total = oT[aug:aug + 1]
                inv = 1.0 / total
                aT = oT * inv
                attT[pl.ds(pl.multiple_of(j * pair + h * head, head), head), at:at + n] = aT[h * head:(h + 1) * head].astype(BF)
                bTn = bT[:, at:at + n].astype(F32)
                ownn = own_r[:, :n]
                rown = row[:, :n]
                rt = jnp.sum(jnp.where(ownn, bTn * aT, 0.0), axis=0, keepdims=True)
                hi = rt.astype(BF).astype(F32)
                lo = rt - hi
                baug = jnp.where(ownn, bTn, jnp.where(rown == aug, -hi, jnp.where(rown == aug + 1, -lo, 0.0))).astype(BF)
                p = e * inv.astype(BF)
                p_s[h, :, at:at + n] = p
                dp = mm(vv, baug).astype(BF)
                ds_s[h, :, at:at + n] = p * dp
            dv = mm(p_s[h], b_s[...])
            dk = mm(ds_s[h], q_s[...]) * LN2
            dqT = mm(kT[...], ds_s[h]) * (head ** -0.5)
            outs.append((dqT, dk, dv))
        dqT = jnp.where(row < head, outs[0][0], outs[1][0]).astype(BF)
        dqkv[:, cols] = dqT.T
        dqkv[:, colk] = jnp.where(lane < head, outs[0][1], outs[1][1]).astype(BF)
        dqkv[:, colv] = jnp.where(lane < head, outs[0][2], outs[1][2]).astype(BF)
        return 0

    lax.fori_loop(0, pairs, one_pair, 0)
    gp = mm(attT[...], c_ref[...])
    gq = mm(nl[...].T, dqkv[...])
    if split[0]:
        gq = gq + prev[0][...]
        gp = gp + prev[1][...]
    if split[1] is None:
        gq_ref[...] = gq
        gp_ref[...] = gp
    else:
        joined = refs[13]
        parts = split[1]
        gqT, gpT = gq.T, gp.T
        dq_rows, dp_rows = gqT.shape[0] // parts, gpT.shape[0] // parts
        for i in range(parts):
            joined[i, :dq_rows] = gqT[i * dq_rows:(i + 1) * dq_rows]
            joined[i, dq_rows:] = gpT[i * dp_rows:(i + 1) * dp_rows]
        lats, lons = lax.axis_size("lat"), lax.axis_size("lon")
        own_lon, own_lat = lax.axis_index("lon") // 2, lax.axis_index("lat")
        for p in range(lons // 2):
            for step in range(lats):
                source = lax.rem(own_lat + step, lats) * lons + 2 * (own_lon ^ p)
                gq_ref[p * lats + step] = joined[source + odd]
                gp_ref[p * lats + step] = joined[source + 1 - odd].astype(BF)
    dn = mm_t(dqkv[...], wqkv_ref[...]) * gain
    normed = cen * rstd
    d = rstd * (dn - jnp.mean(dn, axis=1, keepdims=True) - normed * jnp.mean(dn * normed, axis=1, keepdims=True))
    d = d.astype(BF)
    for ref, at in zip(d_refs, starts):
        ref[...] = d[at:at + ref.shape[0]]


def window_call(pieces, metas, gain, wqkv, wproj, prev, parts):
    width = wproj.shape[0]
    head = width // HEADS
    pair = 2 * head
    sizes = [p.shape[1] for p in pieces]
    cells = sum(sizes)
    deep = 4 * width // parts if parts else 0
    if parts is None:
        sums = (jax.ShapeDtypeStruct((width, 3 * width), F32), jax.ShapeDtypeStruct((width, width), F32))
    else:
        sums = (jax.ShapeDtypeStruct((parts // 2, deep, width), F32),
                jax.ShapeDtypeStruct((parts // 2, deep, width), BF))
    scratch = ([pltpu.VMEM((cells, width), BF)] * 2
               + [pltpu.VMEM((cells, pair), BF)] * 4
               + [pltpu.VMEM((pair, cells), BF)] * 3
               + [pltpu.VMEM((2, cells, cells), BF)] * 2
               + [pltpu.VMEM((cells, 3 * width), BF), pltpu.VMEM((width, cells), BF)])
    if parts is not None:
        scratch.append(pltpu.VMEM((parts, deep, width), F32))
    vmem = pl.BlockSpec(memory_space=pltpu.VMEM)
    args = list(pieces) + [gain, wqkv, wproj] + (list(prev) if prev else [])
    outs = pl.pallas_call(
        functools.partial(window_kernel, head, metas, (prev is not None, parts)),
        out_shape=tuple(jax.ShapeDtypeStruct((n, width), BF) for n in sizes) + sums,
        in_specs=[vmem] * len(args),
        out_specs=[vmem] * (len(sizes) + 2),
        scratch_shapes=scratch,
        cost_estimate=pl.CostEstimate(
            flops=24 * cells * width * width + 12 * cells * cells * width,
            bytes_accessed=8 * 2**20,
            transcendentals=HEADS * cells * cells,
        ),
        compiler_params=pltpu.CompilerParams(vmem_limit_bytes=32 * 2**20),
    )(*args)
    return outs[:len(sizes)], outs[-2:]


def permuted(value, axes, target):
    sizes = [lax.axis_size(a) for a in axes]
    pairs = []
    for source in range(math.prod(sizes)):
        at, rest = [], source
        for size in reversed(sizes):
            at.append(rest % size)
            rest //= size
        goal = target(*reversed(at))
        if goal is None:
            continue
        flat = 0
        for size, place in zip(sizes, goal):
            flat = flat * size + place
        pairs.append((source, flat))
    return lax.ppermute(value, tuple(axes), pairs)


def shared(value, back=False, east=0):
    lats, lons = lax.axis_size("lat"), lax.axis_size("lon")
    pairs = []
    for i in range(lats):
        for j in range(lons):
            if j % 2 == 0:
                goal = (i - 1, j) if i > 0 else None
            else:
                goal = (i + 1, j) if i < lats - 1 else (i, j - 1)
            if goal is not None:
                pair = (i * lons + j, goal[0] * lons + goal[1])
                home = i * lons + (j + east) % lons
                pairs.append((pair[1], home) if back else (home, pair[1]))
    return lax.ppermute(value, ("lat", "lon"), pairs)


def along_lon(value, step):
    count = lax.axis_size("lon")
    return lax.ppermute(value, "lon", [(j, (j + step) % count) for j in range(count)])


def cut_kernel(specs, half, hid_ref, cot_ref, *outs):
    odd = lax.rem(lax.axis_index("lon"), 2)
    top = lax.axis_index("lat") == 0
    end = hid_ref.shape[1] - half
    starts = {"own": (1 - odd) * end, "sent": odd * end}
    zeroed = {"own": top & (odd == 1), "peer": top & (odd == 0)}
    for out, (rows, cols, n, pad, clear) in zip(outs, specs):
        at = starts.get(rows, rows)
        for k, ref in enumerate((hid_ref, cot_ref)):
            for b in range(hid_ref.shape[0]):
                cut = ref[b, pl.ds(at, half)].astype(F32)[:, cols:cols + n]
                if clear:
                    cut = jnp.where(zeroed[clear], 0.0, cut)
                filler = jnp.zeros((half, pad - n, cut.shape[2]), F32)
                out[k, b] = jnp.concatenate([cut, filler], axis=1).astype(BF)


def cut_call(hid, cot, specs, half):
    samples, _, _, width = hid.shape
    vmem = pl.BlockSpec(memory_space=pltpu.VMEM)
    outs = pl.pallas_call(
        functools.partial(cut_kernel, specs, half),
        out_shape=tuple(
            jax.ShapeDtypeStruct((2, samples, half, pad, width), BF) for _, _, _, pad, _ in specs
        ),
        in_specs=[vmem] * 2,
        out_specs=tuple([vmem] * len(specs)),
        cost_estimate=pl.CostEstimate(flops=0, bytes_accessed=4 * hid.size * 2, transcendentals=0),
        compiler_params=pltpu.CompilerParams(vmem_limit_bytes=40 * 2**20),
    )(hid, cot)
    return list(outs)


def reduce_weights(keep, send, lons, returns):
    _, _, width = keep.shape
    lats, dps = lax.axis_size("lat"), lax.axis_size("dp")
    moved, waiting = [], list(returns)

    def release(value, count):
        for _ in range(min(count, len(waiting))):
            held, move = waiting.pop(0)
            value, held = lax.optimization_barrier((value, held))
            moved.append(move(held))
        return value

    got = permuted(send, ("lon",), lambda i: (i ^ 1,))
    keep = release(keep, len(waiting) // 2)
    early = len(moved)
    got = release(got, len(waiting))
    total = [keep[i * lats:(i + 1) * lats] + got[i * lats:(i + 1) * lats].astype(F32) for i in range(lons // 2)]
    while len(total) > 1:
        left = len(total) // 2
        payload = jnp.concatenate(total[left:], axis=0).astype(BF)
        got = permuted(payload, ("lon",), lambda i, bit=2 * left: (i ^ bit,))
        if left == 1:
            got, moved[:early] = lax.optimization_barrier((got, moved[:early]))
        total = [total[i] + got[i * lats:(i + 1) * lats].astype(F32) for i in range(left)]
    total = total[0]

    share = width // dps
    me, mine = lax.axis_index("dp"), None
    for step in range(1, dps):
        part = lax.dynamic_slice_in_dim(total, ((me + step) % dps) * share, share, 2).astype(BF)
        got = permuted(part, ("dp",), lambda i, step=step: ((i + step) % dps,))
        if step == dps - 1:
            got, moved[early:] = lax.optimization_barrier((got, moved[early:]))
        mine = got.astype(F32) if mine is None else mine + got.astype(F32)
    own = lax.dynamic_slice_in_dim(total, me * share, share, 2)
    total = own if mine is None else own + mine

    mine = total[0]
    for step in range(1, lats):
        got = permuted(total[step].astype(BF), ("lat",), lambda i, step=step: ((i + step) % lats,))
        mine = mine + got.astype(F32)
    return mine, moved


def per_device(hidden_in, grad_out, norm_gain, w_qkv, w_proj):
    samples, lat_rows, lon_cols, width = hidden_in.shape
    half = WIN // 2
    nr, nc = lat_rows // WIN, lon_cols // WIN
    short = half + (-half) % 16
    wide = WIN + (-WIN) % 16
    lons = lax.axis_size("lon")
    parts = lax.axis_size("lat") * lons
    if lons & (lons - 1) or lons < 2:
        raise ValueError("lon size")

    odd = lax.axis_index("lon") % 2
    inner = [wc * WIN + SHIFT for wc in range(nc - 1)]
    edge = (nc - 1) * WIN + SHIFT
    sent = cut_call(hidden_in, grad_out, [("sent", at, WIN, wide, "") for at in inner], half) if inner else []
    hid, cot, sent = lax.optimization_barrier((hidden_in, grad_out, sent))
    inner_in = [shared(p) for p in sent]
    specs = [("sent", 0, half, short, "peer"), ("own", 0, half, short, "")]
    specs += [("own", edge, half, short, "own"), ("sent", edge, half, short, "")]
    specs += [("own", at, WIN, wide, "own") for at in inner]
    fixed = [(2 * wr + 1 + i) * half for wr in range(nr - 1) for i in range(2)]
    specs += [(r, at, WIN, wide, "") for at in inner for r in fixed]
    specs += [(r, edge, half, short, "") for r in fixed] + [(r, 0, half, short, "") for r in fixed]
    cuts = cut_call(hid, cot, specs, half)
    side_sent, corner_sent, own_edge, edge_sent = cuts[:4]
    own_inner, rest = cuts[4:4 + len(inner)], cuts[4 + len(inner):]
    whole_inner = [[rest.pop(0) for _ in fixed] for _ in inner]
    whole_edge = [rest.pop(0) for _ in fixed]
    whole_side = [along_lon(rest.pop(0), -1) for _ in fixed]
    own_side = along_lon(side_sent, -1)
    if inner_in:
        edge_sent, corner_sent, inner_in = lax.optimization_barrier((edge_sent, corner_sent, inner_in))
    edge_in, corner_in = shared(edge_sent), shared(corner_sent, east=1)

    order = [(b, wr, wc) for b in range(samples) for wc in range(nc) for wr in range(nr)]
    sums = None
    out = {}
    for step, (b, wr, wc) in enumerate(order):
        if wr < nr - 1 and wc < nc - 1:
            cells = whole_inner[wc][2 * wr:2 * wr + 2]
            metas = ((WIN, wide, False),) * 2
        elif wr < nr - 1:
            cells = [f[2 * wr + i] for i in range(2) for f in (whole_edge, whole_side)]
            metas = ((half, short, False),) * 4
        elif wc < nc - 1:
            cells = [own_inner[wc], inner_in[wc]]
            metas = ((WIN, wide, False), (WIN, wide, True))
        else:
            cells = [own_edge, own_side, edge_in, corner_in]
            metas = ((half, short, False),) * 2 + ((half, short, True),) * 2
        cells = [p[:, b].reshape(2, -1, width) for p in cells]
        done, sums = window_call(
            cells, metas, norm_gain, w_qkv, w_proj, sums, parts if step == len(order) - 1 else None
        )
        out[b, wr, wc] = [d.reshape(half, pad, width) for d, (n, pad, _) in zip(done, metas)]

    late = [(out[b, nr - 1, wc][1], lambda v: shared(v, back=True)) for b in range(samples) for wc in range(nc - 1)]
    for b in range(samples):
        own, own_lon, other, other_lon = out[b, nr - 1, nc - 1]
        late.append((other, lambda v: shared(v, back=True)))
        late.append((other_lon, lambda v: shared(v, back=True, east=1)))
        late.append((own_lon, lambda v: along_lon(v, 1)))
    total, moved = reduce_weights(sums[0], sums[1], lons, late)

    rows_out = []
    for b in range(samples):
        def stacked(own, back, between, upper):
            above = jnp.where(upper, own, back)
            below = jnp.where(upper, back, own)
            return jnp.concatenate([above] + between + [below], axis=0)

        columns = []
        for wc in range(nc - 1):
            own, other = out[b, nr - 1, wc]
            between = [out[b, wr, wc][i] for wr in range(nr - 1) for i in range(2)]
            columns.append(stacked(own, moved[b * (nc - 1) + wc], between, odd == 1)[:, :WIN])
        own = out[b, nr - 1, nc - 1][0]
        back, far, near = moved[samples * (nc - 1) + 3 * b:][:3]
        between = [out[b, wr, nc - 1][i] for wr in range(nr - 1) for i in (0, 2)]
        columns.append(stacked(own, back, between, odd == 1)[:, :half])
        between = [along_lon(out[b, wr, nc - 1][i], 1) for wr in range(nr - 1) for i in (1, 3)]
        columns.insert(0, stacked(near, far, between, odd == 0)[:, :half])
        rows_out.append(jnp.concatenate(columns, axis=1))
    returned = jnp.stack(rows_out)
    grad_in = (grad_out.astype(F32) + returned.astype(F32)).astype(BF)
    total_cells = (
        lax.axis_size("dp") * samples * lat_rows * lax.axis_size("lat") * lon_cols * lons
    )
    factor = float(total_cells) ** (-0.5)
    cut = 3 * width // parts
    return (grad_in, total[:cut].T * factor, total[cut:].T * factor)


def solution(mesh):
    in_specs = (P("dp", "lat", "lon", None), P("dp", "lat", "lon", None), P(), P(), P())
    out_specs = (P("dp", "lat", "lon", None), P("dp", ("lat", "lon")), P("dp", ("lat", "lon")))
    return jax.shard_map(
        per_device, mesh=mesh, in_specs=in_specs, out_specs=out_specs, check_vma=False
    )
```

```python
import functools, math
import jax, jax.numpy as jnp
from jax import lax
from jax.experimental import pallas as pl
from jax.experimental.pallas import tpu as pltpu

from jax.sharding import PartitionSpec as P

HEADS = 6
WIN = 30
SHIFT = 15
EPSILON = 1e-05
BF = jnp.bfloat16
F32 = jnp.float32
LN2 = math.log(2.0)

def mm(a, b):
    return lax.dot_general(a, b, (((1,), (0,)), ((), ())), preferred_element_type=F32)

def mm_t(a, b):
    return lax.dot_general(a, b, (((1,), (1,)), ((), ())), preferred_element_type=F32)

def blocks_of(n, step):
    return [(at, min(step, n - at)) for at in range(0, n, step)]

def window_kernel(head, metas, split, *refs):
    count = len(metas)
    pieces, refs = refs[:count], refs[count:]
    gain_ref, wqkv_ref, wproj_ref = refs[:3]
    refs = refs[3:]
    if split[0]:
        prev, refs = refs[:2], refs[2:]
    d_refs, refs = refs[:count], refs[count:]
    (gq_ref, gp_ref), refs = refs[:2], refs[2:]
    c_ref, nl, q_s, k_s, v_s, b_s, kT, vT, bT, p_s, ds_s, dqkv, attT = refs[:13]
    cells, width = c_ref.shape
    pair = 2 * head
    pairs = width // pair
    qscale = head ** -0.5 / LN2
    at = 0
    starts = []
    for p in pieces:
        starts.append(at)
        c_ref[at:at + p.shape[1]] = p[1]
        at += p.shape[1]
    odd = lax.rem(lax.axis_index("lon"), 2)
    packed = jnp.where((lax.axis_index("lat") == lax.axis_size("lat") - 1) & (odd == 0), 1.0, 0.0)
    oks, seconds = [], []
    for p, (n, pad, other) in zip(pieces, metas):
        place = lax.broadcasted_iota(jnp.int32, (p.shape[1], pair), 0)
        oks.append(jnp.where(lax.rem(place, pad) < n, 1.0, 0.0))
        seconds.append(jnp.full((p.shape[1], pair), packed if other else 0.0, F32))
    valid_col = jnp.concatenate(oks, axis=0)
    second = jnp.concatenate(seconds, axis=0)
    x = jnp.concatenate([p[0] for p in pieces], axis=0).astype(F32)
    mean = jnp.mean(x, axis=1, keepdims=True)
    cen = x - mean
    rstd = lax.rsqrt(jnp.mean(cen * cen, axis=1, keepdims=True) + EPSILON)
    gain = gain_ref[...][None]
    nl[...] = (cen * rstd * gain).astype(BF)
    qb = blocks_of(cells, cells)

    def one_pair(j, _):
        cols = pl.ds(pl.multiple_of(j * pair, pair), pair)
        colk = pl.ds(pl.multiple_of(width + j * pair, pair), pair)
        colv = pl.ds(pl.multiple_of(2 * width + j * pair, pair), pair)
        q_s[...] = (mm(nl[...], wqkv_ref[:, cols]) * qscale).astype(BF)
        k_s[...] = mm(nl[...], wqkv_ref[:, colk]).astype(BF)
        v_s[...] = mm(nl[...], wqkv_ref[:, colv]).astype(BF)
        b_s[...] = mm_t(c_ref[...], wproj_ref[cols, :]).astype(BF)
        kT[...] = k_s[...].T
        vT[...] = v_s[...].T
        bT[...] = b_s[...].T
        lane = lax.broadcasted_iota(jnp.int32, (cells, pair), 1)
        row = lax.broadcasted_iota(jnp.int32, (pair, cells), 0)
        outs = []
        for h in range(2):
            own = (lane >= head) if h else (lane < head)
            own_r = (row >= head) if h else (row < head)
            aug = 0 if h else head
            seen = jnp.where(lane == aug, valid_col * (1.0 - second), valid_col * second)
            two = (lane == aug) | (lane == aug + 1)
            bias = jnp.where(two, (seen - 1.0) * 30000.0, 0.0).astype(BF)
            group = jnp.where(lane == aug, 1.0 - second, second)
            kk = jnp.where(own, k_s[...], bias)
            qq = jnp.where(own, q_s[...], jnp.where(two, group, 0.0).astype(BF))
            vv = jnp.where(own, v_s[...], jnp.where(two, 1.0, 0.0).astype(BF))
            vvT = jnp.where(own_r, vT[...], jnp.where(row == aug, 1.0, 0.0).astype(BF))
            for at, n in qb:
                s = mm_t(kk, qq[at:at + n])
                e = jnp.exp2(s).astype(BF)
                oT = mm(vvT, e)
                total = oT[aug:aug + 1]
                inv = 1.0 / total
                aT = oT * inv
                attT[pl.ds(pl.multiple_of(j * pair + h * head, head), head), at:at + n] = aT[h * head:(h + 1) * head].astype(BF)
                bTn = bT[:, at:at + n].astype(F32)
                ownn = own_r[:, :n]
                rown = row[:, :n]
                rt = jnp.sum(jnp.where(ownn, bTn * aT, 0.0), axis=0, keepdims=True)
                hi = rt.astype(BF).astype(F32)
                lo = rt - hi
                baug = jnp.where(ownn, bTn, jnp.where(rown == aug, -hi, jnp.where(rown == aug + 1, -lo, 0.0))).astype(BF)
                p = e * inv.astype(BF)
                p_s[h, :, at:at + n] = p
                dp = mm(vv, baug).astype(BF)
                ds_s[h, :, at:at + n] = p * dp
            dv = mm(p_s[h], b_s[...])
            dk = mm(ds_s[h], q_s[...]) * LN2
            dqT = mm(kT[...], ds_s[h]) * (head ** -0.5)
            outs.append((dqT, dk, dv))
        dqT = jnp.where(row < head, outs[0][0], outs[1][0]).astype(BF)
        dqkv[:, cols] = dqT.T
        dqkv[:, colk] = jnp.where(lane < head, outs[0][1], outs[1][1]).astype(BF)
        dqkv[:, colv] = jnp.where(lane < head, outs[0][2], outs[1][2]).astype(BF)
        return 0

    lax.fori_loop(0, pairs, one_pair, 0)
    gp = mm(attT[...], c_ref[...])
    gq = mm(nl[...].T, dqkv[...])
    if split[0]:
        gq = gq + prev[0][...]
        gp = gp + prev[1][...]
    if split[1] is None:
        gq_ref[...] = gq
        gp_ref[...] = gp
    else:
        joined = refs[13]
        parts = split[1]
        gqT, gpT = gq.T, gp.T
        dq_rows, dp_rows = gqT.shape[0] // parts, gpT.shape[0] // parts
        for i in range(parts):
            joined[i, :dq_rows] = gqT[i * dq_rows:(i + 1) * dq_rows]
            joined[i, dq_rows:] = gpT[i * dp_rows:(i + 1) * dp_rows]
        lats, lons = lax.axis_size("lat"), lax.axis_size("lon")
        own_lon, own_lat = lax.axis_index("lon") // 2, lax.axis_index("lat")
        for p in range(lons // 2):
            for step in range(lats):
                source = lax.rem(own_lat + step, lats) * lons + 2 * (own_lon ^ p)
                gq_ref[p * lats + step] = joined[source + odd]
                gp_ref[p * lats + step] = joined[source + 1 - odd].astype(BF)
    dn = mm_t(dqkv[...], wqkv_ref[...]) * gain
    normed = cen * rstd
    d = rstd * (dn - jnp.mean(dn, axis=1, keepdims=True) - normed * jnp.mean(dn * normed, axis=1, keepdims=True))
    d = d.astype(BF)
    for ref, at in zip(d_refs, starts):
        ref[...] = d[at:at + ref.shape[0]]


def window_call(pieces, metas, gain, wqkv, wproj, prev, parts):
    width = wproj.shape[0]
    head = width // HEADS
    pair = 2 * head
    sizes = [p.shape[1] for p in pieces]
    cells = sum(sizes)
    deep = 4 * width // parts if parts else 0
    if parts is None:
        sums = (jax.ShapeDtypeStruct((width, 3 * width), F32), jax.ShapeDtypeStruct((width, width), F32))
    else:
        sums = (jax.ShapeDtypeStruct((parts // 2, deep, width), F32),
                jax.ShapeDtypeStruct((parts // 2, deep, width), BF))
    scratch = ([pltpu.VMEM((cells, width), BF)] * 2
               + [pltpu.VMEM((cells, pair), BF)] * 4
               + [pltpu.VMEM((pair, cells), BF)] * 3
               + [pltpu.VMEM((2, cells, cells), BF)] * 2
               + [pltpu.VMEM((cells, 3 * width), BF), pltpu.VMEM((width, cells), BF)])
    if parts is not None:
        scratch.append(pltpu.VMEM((parts, deep, width), F32))
    vmem = pl.BlockSpec(memory_space=pltpu.VMEM)
    args = list(pieces) + [gain, wqkv, wproj] + (list(prev) if prev else [])
    outs = pl.pallas_call(
        functools.partial(window_kernel, head, metas, (prev is not None, parts)),
        out_shape=tuple(jax.ShapeDtypeStruct((n, width), BF) for n in sizes) + sums,
        in_specs=[vmem] * len(args),
        out_specs=[vmem] * (len(sizes) + 2),
        scratch_shapes=scratch,
        cost_estimate=pl.CostEstimate(
            flops=24 * cells * width * width + 12 * cells * cells * width,
            bytes_accessed=8 * 2**20,
            transcendentals=HEADS * cells * cells,
        ),
        compiler_params=pltpu.CompilerParams(vmem_limit_bytes=26 * 2**20),
    )(*args)
    return outs[:len(sizes)], outs[-2:]


def permuted(value, axes, target):
    sizes = [lax.axis_size(a) for a in axes]
    pairs = []
    for source in range(math.prod(sizes)):
        at, rest = [], source
        for size in reversed(sizes):
            at.append(rest % size)
            rest //= size
        goal = target(*reversed(at))
        if goal is None:
            continue
        flat = 0
        for size, place in zip(sizes, goal):
            flat = flat * size + place
        pairs.append((source, flat))
    return lax.ppermute(value, tuple(axes), pairs)


def shared(value, back=False, east=0):
    lats, lons = lax.axis_size("lat"), lax.axis_size("lon")
    pairs = []
    for i in range(lats):
        for j in range(lons):
            if j % 2 == 0:
                goal = (i - 1, j) if i > 0 else None
            else:
                goal = (i + 1, j) if i < lats - 1 else (i, j - 1)
            if goal is not None:
                pair = (i * lons + j, goal[0] * lons + goal[1])
                home = i * lons + (j + east) % lons
                pairs.append((pair[1], home) if back else (home, pair[1]))
    return lax.ppermute(value, ("lat", "lon"), pairs)


def along_lon(value, step):
    count = lax.axis_size("lon")
    return lax.ppermute(value, "lon", [(j, (j + step) % count) for j in range(count)])


def cut_kernel(specs, half, hid_ref, cot_ref, *outs):
    odd = lax.rem(lax.axis_index("lon"), 2)
    top = lax.axis_index("lat") == 0
    end = hid_ref.shape[1] - half
    starts = {"own": (1 - odd) * end, "sent": odd * end}
    zeroed = {"own": top & (odd == 1), "peer": top & (odd == 0)}
    for out, (rows, cols, n, pad, clear) in zip(outs, specs):
        at = starts.get(rows, rows)
        for k, ref in enumerate((hid_ref, cot_ref)):
            for b in range(hid_ref.shape[0]):
                cut = ref[b, pl.ds(at, half)].astype(F32)[:, cols:cols + n]
                if clear:
                    cut = jnp.where(zeroed[clear], 0.0, cut)
                filler = jnp.zeros((half, pad - n, cut.shape[2]), F32)
                out[k, b] = jnp.concatenate([cut, filler], axis=1).astype(BF)


def cut_call(hid, cot, specs, half):
    samples, _, _, width = hid.shape
    vmem = pl.BlockSpec(memory_space=pltpu.VMEM)
    outs = pl.pallas_call(
        functools.partial(cut_kernel, specs, half),
        out_shape=tuple(
            jax.ShapeDtypeStruct((2, samples, half, pad, width), BF) for _, _, _, pad, _ in specs
        ),
        in_specs=[vmem] * 2,
        out_specs=tuple([vmem] * len(specs)),
        cost_estimate=pl.CostEstimate(flops=0, bytes_accessed=4 * hid.size * 2, transcendentals=0),
        compiler_params=pltpu.CompilerParams(vmem_limit_bytes=40 * 2**20),
    )(hid, cot)
    return list(outs)


def reduce_weights(keep, send, lons, returns):
    _, _, width = keep.shape
    lats, dps = lax.axis_size("lat"), lax.axis_size("dp")
    moved, waiting = [], list(returns)

    def release(value, count):
        for _ in range(min(count, len(waiting))):
            held, move = waiting.pop(0)
            value, held = lax.optimization_barrier((value, held))
            moved.append(move(held))
        return value

    got = permuted(send, ("lon",), lambda i: (i ^ 1,))
    keep = release(keep, len(waiting) // 2)
    early = len(moved)
    got = release(got, len(waiting))
    total = [keep[i * lats:(i + 1) * lats] + got[i * lats:(i + 1) * lats].astype(F32) for i in range(lons // 2)]
    while len(total) > 1:
        left = len(total) // 2
        payload = jnp.concatenate(total[left:], axis=0).astype(BF)
        got = permuted(payload, ("lon",), lambda i, bit=2 * left: (i ^ bit,))
        if left == 1:
            got, moved[:early] = lax.optimization_barrier((got, moved[:early]))
        total = [total[i] + got[i * lats:(i + 1) * lats].astype(F32) for i in range(left)]
    total = total[0]

    share = width // dps
    me, mine = lax.axis_index("dp"), None
    for step in range(1, dps):
        part = lax.dynamic_slice_in_dim(total, ((me + step) % dps) * share, share, 2).astype(BF)
        got = permuted(part, ("dp",), lambda i, step=step: ((i + step) % dps,))
        if step == dps - 1:
            got, moved[early:] = lax.optimization_barrier((got, moved[early:]))
        mine = got.astype(F32) if mine is None else mine + got.astype(F32)
    own = lax.dynamic_slice_in_dim(total, me * share, share, 2)
    total = own if mine is None else own + mine

    mine = total[0]
    for step in range(1, lats):
        got = permuted(total[step].astype(BF), ("lat",), lambda i, step=step: ((i + step) % lats,))
        mine = mine + got.astype(F32)
    return mine, moved


def per_device(hidden_in, grad_out, norm_gain, w_qkv, w_proj):
    samples, lat_rows, lon_cols, width = hidden_in.shape
    half = WIN // 2
    nr, nc = lat_rows // WIN, lon_cols // WIN
    short = half + (-half) % 16
    wide = WIN + (-WIN) % 16
    lons = lax.axis_size("lon")
    parts = lax.axis_size("lat") * lons
    if lons & (lons - 1) or lons < 2:
        raise ValueError("lon size")

    odd = lax.axis_index("lon") % 2
    inner = [wc * WIN + SHIFT for wc in range(nc - 1)]
    edge = (nc - 1) * WIN + SHIFT
    sent = cut_call(hidden_in, grad_out, [("sent", at, WIN, wide, "") for at in inner], half) if inner else []
    hid, cot, sent = lax.optimization_barrier((hidden_in, grad_out, sent))
    inner_in = [shared(p) for p in sent]
    specs = [("sent", 0, half, short, "peer"), ("own", 0, half, short, "")]
    specs += [("own", edge, half, short, "own"), ("sent", edge, half, short, "")]
    specs += [("own", at, WIN, wide, "own") for at in inner]
    fixed = [(2 * wr + 1 + i) * half for wr in range(nr - 1) for i in range(2)]
    specs += [(r, at, WIN, wide, "") for at in inner for r in fixed]
    specs += [(r, edge, half, short, "") for r in fixed] + [(r, 0, half, short, "") for r in fixed]
    cuts = cut_call(hid, cot, specs, half)
    side_sent, corner_sent, own_edge, edge_sent = cuts[:4]
    own_inner, rest = cuts[4:4 + len(inner)], cuts[4 + len(inner):]
    whole_inner = [[rest.pop(0) for _ in fixed] for _ in inner]
    whole_edge = [rest.pop(0) for _ in fixed]
    whole_side = [along_lon(rest.pop(0), -1) for _ in fixed]
    own_side, edge_in, corner_in = along_lon(side_sent, -1), shared(edge_sent), shared(corner_sent, east=1)

    order = [(b, wr, wc) for b in range(samples) for wc in range(nc) for wr in range(nr)]
    sums = None
    out = {}
    for step, (b, wr, wc) in enumerate(order):
        if wr < nr - 1 and wc < nc - 1:
            cells = whole_inner[wc][2 * wr:2 * wr + 2]
            metas = ((WIN, wide, False),) * 2
        elif wr < nr - 1:
            cells = [f[2 * wr + i] for i in range(2) for f in (whole_edge, whole_side)]
            metas = ((half, short, False),) * 4
        elif wc < nc - 1:
            cells = [own_inner[wc], inner_in[wc]]
            metas = ((WIN, wide, False), (WIN, wide, True))
        else:
            cells = [own_edge, own_side, edge_in, corner_in]
            metas = ((half, short, False),) * 2 + ((half, short, True),) * 2
        cells = [p[:, b].reshape(2, -1, width) for p in cells]
        done, sums = window_call(
            cells, metas, norm_gain, w_qkv, w_proj, sums, parts if step == len(order) - 1 else None
        )
        out[b, wr, wc] = [d.reshape(half, pad, width) for d, (n, pad, _) in zip(done, metas)]

    late = [(out[b, nr - 1, wc][1], lambda v: shared(v, back=True)) for b in range(samples) for wc in range(nc - 1)]
    for b in range(samples):
        own, own_lon, other, other_lon = out[b, nr - 1, nc - 1]
        late.append((other, lambda v: shared(v, back=True)))
        late.append((other_lon, lambda v: shared(v, back=True, east=1)))
        late.append((own_lon, lambda v: along_lon(v, 1)))
    total, moved = reduce_weights(sums[0], sums[1], lons, late)

    rows_out = []
    for b in range(samples):
        def stacked(own, back, between, upper):
            above = jnp.where(upper, own, back)
            below = jnp.where(upper, back, own)
            return jnp.concatenate([above] + between + [below], axis=0)

        columns = []
        for wc in range(nc - 1):
            own, other = out[b, nr - 1, wc]
            between = [out[b, wr, wc][i] for wr in range(nr - 1) for i in range(2)]
            columns.append(stacked(own, moved[b * (nc - 1) + wc], between, odd == 1)[:, :WIN])
        own = out[b, nr - 1, nc - 1][0]
        back, far, near = moved[samples * (nc - 1) + 3 * b:][:3]
        between = [out[b, wr, nc - 1][i] for wr in range(nr - 1) for i in (0, 2)]
        columns.append(stacked(own, back, between, odd == 1)[:, :half])
        between = [along_lon(out[b, wr, nc - 1][i], 1) for wr in range(nr - 1) for i in (1, 3)]
        columns.insert(0, stacked(near, far, between, odd == 0)[:, :half])
        rows_out.append(jnp.concatenate(columns, axis=1))
    returned = jnp.stack(rows_out)
    grad_in = (grad_out.astype(F32) + returned.astype(F32)).astype(BF)
    total_cells = (
        lax.axis_size("dp") * samples * lat_rows * lax.axis_size("lat") * lon_cols * lons
    )
    factor = float(total_cells) ** (-0.5)
    cut = 3 * width // parts
    return (grad_in, total[:cut].T * factor, total[cut:].T * factor)


def solution(mesh):
    in_specs = (P("dp", "lat", "lon", None), P("dp", "lat", "lon", None), P(), P(), P())
    out_specs = (P("dp", "lat", "lon", None), P("dp", ("lat", "lon")), P("dp", ("lat", "lon")))
    return jax.shard_map(
        per_device, mesh=mesh, in_specs=in_specs, out_specs=out_specs, check_vma=False
    )
```
